32 devices in a mesh: inst: 4 (over x, core), space: 8 (over z, y).
Axes of the slice: x: 2, y: 2, z: 4, core: 2. Of those that a mesh axis runs over, the one named last changes fastest.
Arguments:
- adjoint: bfloat16 [8, 5, 128, 32, 256], P('inst', None, 'space'), may hold values from -6 to 6
- flux_terms: bfloat16 [8, 5, 3, 128, 32, 256], P('inst', None, None, 'space'), may hold values from -6 to 6
- stiffness: float32 [128, 32, 256], P('space', 'inst'), may hold values from 0.1 to 1
- normals: float32 [3, 128, 32], P(None, 'space', 'inst'), may hold values from -6 to 6
- design_map: int32 [128, 32], P('space', 'inst'), may hold values from 0 to 255
Outputs:
- mesh_adjoint: float32 [3, 128, 32, 256], P(None, 'space', 'inst')
- design_grad: float32 [256], P(('inst', 'space'))
The draws below stay inside these ranges and needn't reach their ends.
All inputs are finite; a program needn't handle non-finite values.
Results may differ from the reference program's by a relative error of at most 0.00075.
Values sent between devices are 32-bit elements; how exact they have to be, the bound alone decides.
No kernel may reach another device: no remote copies, remote signals or barrier semaphores. Data moves between devices by JAX's collectives and lax.ppermute only.
A program may use at most 64 MiB of HBM per device.

```python
import math
import jax
import jax.numpy as jnp
from jax import lax

NV = 5
NZ = 256
SWEEPS = 2
INSTANCES = 8
NXG = 128
NYG = 32
NDV = 256


def plant(entries, stream_key, smallest, largest):
    shape = entries.shape
    place = [jax.random.randint(jax.random.fold_in(stream_key, axis), (), 0, shape[axis]) for axis in range(len(shape))]
    entries = entries.at[tuple(place)].set(smallest)
    longest = shape.index(max(shape))
    place[longest] = (place[longest] + 1) % shape[longest]
    return entries.at[tuple(place)].set(largest)


def block_scale(key, dims, pieces, smallest, largest):
    loudness = 1.0
    for position, blocks in pieces:
        heights = jax.random.uniform(jax.random.fold_in(jax.random.fold_in(key, 6), position), (blocks,), jnp.float32, smallest / len(pieces), largest / len(pieces))
        loudness = loudness * jnp.repeat(jnp.exp(heights), dims[position] // blocks).reshape((-1,) + (1,) * (len(dims) - 1 - position))
    return loudness


def noise(own_key, shape, scale, most, split=(), kind=jnp.bfloat16):
    values = jax.random.normal(own_key, shape, jnp.float32) * scale
    if len(split) > 0:
        values = block_scale(own_key, shape, split, -0.22, 0.18) * values
    return jnp.clip(values, min=-most, max=most).astype(kind)


def setup_inputs(seed: int = 0) -> dict:
    arg_keys = jax.random.split(jax.random.key(seed), 6)
    adjoint = noise(arg_keys[0], (INSTANCES, NV, NXG, NYG, NZ), 1.0, 6.0, ((0, 4), (2, 8)))
    flux_terms = noise(arg_keys[1], (INSTANCES, NV, 3, NXG, NYG, NZ), 1.0, 6.0, ((0, 4), (3, 8)))
    stiffness = jnp.clip(jnp.exp(math.log(1.0) - 2.3025851 * jax.random.uniform(arg_keys[2], (NXG, NYG, NZ), jnp.float32) ** block_scale(arg_keys[2], (NXG, NYG, NZ), ((0, 8), (1, 4)), -0.2, 0.2)), 0.1, 1.0)
    normals = noise(arg_keys[3], (3, NXG, NYG), 1.0, 6.0, ((1, 8), (2, 4)), jnp.float32)
    design_map = plant(jax.random.randint(arg_keys[4], (NXG, NYG), 0, NDV), jax.random.fold_in(arg_keys[4], 1), 0, NDV - 1).astype(jnp.int32)
    return {"adjoint": adjoint, "flux_terms": flux_terms, "stiffness": stiffness, "normals": normals, "design_map": design_map}


def transpose_metric(weighted):
    padded = jnp.pad(weighted, ((0, 0), (1, 1), (1, 1), (1, 1)))
    first = padded[0, :-2, 1:-1, 1:-1] - padded[0, 2:, 1:-1, 1:-1]
    second = padded[1, 1:-1, :-2, 1:-1] - padded[1, 1:-1, 2:, 1:-1]
    third = padded[2, 1:-1, 1:-1, :-2] - padded[2, 1:-1, 1:-1, 2:]
    return weighted + 0.5 * jnp.stack([first, second, third])


def neighbours(field):
    padded = jnp.pad(field, ((0, 0), (1, 1), (1, 1), (1, 1)))
    summed = padded[:, :-2, 1:-1, 1:-1] + padded[:, 2:, 1:-1, 1:-1]
    summed = summed + padded[:, 1:-1, :-2, 1:-1] + padded[:, 1:-1, 2:, 1:-1]
    summed = summed + padded[:, 1:-1, 1:-1, :-2] + padded[:, 1:-1, 1:-1, 2:]
    return summed


def reference(adjoint, flux_terms, stiffness, normals, design_map):
    def accumulate(carried, pair):
        adj_one, flux_one = pair
        term = jnp.einsum("vxyz,vdxyz->dxyz", adj_one.astype(jnp.float32), flux_one.astype(jnp.float32))
        return carried + term, None

    start_sum = jnp.zeros((3, NXG, NYG, NZ), jnp.float32)
    summed, _ = lax.scan(accumulate, start_sum, (adjoint, flux_terms))
    weighted = summed / INSTANCES
    volume_grad = transpose_metric(weighted)
    diagonal = 6.5 * stiffness
    mesh_adjoint = volume_grad / diagonal
    for sweep_index in range(SWEEPS):
        mesh_adjoint = (volume_grad + neighbours(stiffness * mesh_adjoint)) / diagonal
    surface = jnp.sum(normals * mesh_adjoint[:, :, :, 0], axis=0)
    flat_ids = design_map.reshape(-1)
    one_hot = (flat_ids[:, None] == jnp.arange(NDV, dtype=jnp.int32)[None, :]).astype(jnp.float32)
    design_grad = jnp.dot(surface.reshape(-1), one_hot, precision=lax.Precision.HIGHEST)
    return mesh_adjoint, design_grad
```

```python
import functools
import jax
import jax.numpy as jnp
from jax import lax
from jax.experimental import pallas as pl
from jax.experimental.pallas import tpu as pltpu
from jax.sharding import PartitionSpec as P

DIAG = 6.5
RELAX = 1.0 / DIAG
DV_DEV = 8
REACH = 3
PAD = REACH + 1
CHUNK = 2
REACHES = (3, 2, 2)
LOW_AT = (0, 3, 5)
OVER = 7


def row_neighbours(slab):
    rows = slab.shape[0]
    row = lax.broadcasted_iota(jnp.int32, slab.shape, 0)
    down = jnp.where(row == 0, 0.0, pltpu.roll(slab, 1, 0))
    up = jnp.where(row == rows - 1, 0.0, pltpu.roll(slab, rows - 1, 0))
    return down, up


def lane_difference(slab):
    lanes = slab.shape[1]
    lane = lax.broadcasted_iota(jnp.int32, slab.shape, 1)
    left = jnp.where(lane == 0, 0.0, pltpu.roll(slab, 1, 1))
    right = jnp.where(lane == lanes - 1, 0.0, pltpu.roll(slab, lanes - 1, 1))
    return left - right


def front_kernel(
    scale, place_ref, adj_hbm, flux_hbm,
    main_ko, main_kx, main_so, main_sx, over_ko, over_kx, over_so, over_sx,
    adj, flux, work, metric, plane, side, band, adj_sems, flux_sems,
):
    kinds, variables, rows, width, depth = adj.shape
    chunks = rows // CHUNK
    low_open = place_ref[0].astype(jnp.float32)
    high_open = place_ref[1].astype(jnp.float32)
    core_one = place_ref[2] == 1
    far_one = place_ref[3] == 1

    def adj_copy(i):
        part = pl.ds(i * CHUNK, CHUNK)
        return pltpu.make_async_copy(
            adj_hbm.at[:, :, part], adj.at[:, :, part], adj_sems.at[i]
        )

    def flux_copy(i):
        part = pl.ds(i * CHUNK, CHUNK)
        return pltpu.make_async_copy(
            flux_hbm.at[:, :, :, part], flux.at[:, :, :, part], flux_sems.at[i]
        )

    for i in range(chunks):
        adj_copy(i).start()
        flux_copy(i).start()

    near = jnp.abs(
        lax.broadcasted_iota(jnp.int32, (depth, depth), 0)
        - lax.broadcasted_iota(jnp.int32, (depth, depth), 1)
    )
    lane = lax.broadcasted_iota(jnp.int32, (depth, depth), 1)
    ends = jnp.where((lane == 0) | (lane == depth - 1), 1.0, 2.0)
    band[:, :depth] = jnp.where(near == 1, 1.0, 0.0).astype(jnp.bfloat16)
    band[:, depth:] = jnp.where(near == 0, ends, jnp.where(near == 2, 1.0, 0.0)).astype(
        jnp.bfloat16
    )
    zero = jnp.zeros((width, depth), jnp.float32)
    for d in range(3):
        for x in (-2, -1, rows, rows + 1):
            metric[d, x + PAD] = zero
            side[d, x + PAD] = zero
            plane[d, x + PAD] = zero
    work[0, PAD - 2] = zero
    work[0, PAD - 1] = zero
    work[0, PAD + rows] = zero
    work[0, PAD + rows + 1] = zero

    def weigh(x):
        for h in range(width // 16):
            part = slice(16 * h, 16 * h + 16)
            sums = [jnp.zeros((16, depth), jnp.float32) for _ in range(3)]
            for k in range(kinds):
                for v in range(variables):
                    a = adj[k, v, x, part].astype(jnp.float32)
                    for d in range(3):
                        sums[d] = sums[d] + a * flux[k, v, d, x, part].astype(jnp.float32)
            for d in range(3):
                work[d, x + PAD, part] = sums[d] * scale

    def in_plane(d, x):
        r = x + PAD
        here = work[d, r]
        if d == 0:
            m = here + 0.5 * (work[0, r - 1] - work[0, r + 1])
            m = m * jnp.where(x < 0, low_open, jnp.where(x >= rows, high_open, 1.0))
        elif d == 1:
            down, up = row_neighbours(here)
            m = here + 0.5 * (down - up)
        else:
            m = here + 0.5 * lane_difference(here)
        high = m.astype(jnp.bfloat16)
        low = (m - high.astype(jnp.float32)).astype(jnp.bfloat16)
        along = jnp.dot(high, band[...], preferred_element_type=jnp.float32) + jnp.dot(
            low, band[...], preferred_element_type=jnp.float32
        )
        down, up = row_neighbours(m)
        once = (down + up) + along[:, :depth]
        down, up = row_neighbours(once + along[:, :depth])
        twice = (down + up) + along[:, depth:]
        returns = 2.0 - jnp.where(
            x == 0, 1.0 - low_open, jnp.where(x == rows - 1, 1.0 - high_open, 0.0)
        )
        metric[d, r] = m
        side[d, r] = RELAX * m + (2 * RELAX * RELAX) * once
        plane[d, r] = m * (1.0 + RELAX * RELAX * returns) + (
            RELAX * once + (RELAX * RELAX) * twice
        )

    def gather(i, _):
        @pl.when(i > 0)
        def _():
            for j in range(CHUNK):
                in_plane(1, (i - 1) * CHUNK + j)
                in_plane(2, (i - 1) * CHUNK + j)
                in_plane(0, (i - 1) * CHUNK + j - 1)

        @pl.when(i < chunks)
        def _():
            adj_copy(i).wait()
            flux_copy(i).wait()
            for j in range(CHUNK):
                weigh(i * CHUNK + j)

        return 0

    lax.fori_loop(0, chunks + 1, gather, 0)
    in_plane(0, rows - 1)
    in_plane(0, rows)

    def put(refs, index, value):
        blocks = [value[8 * b : 8 * b + 8] for b in range(4)]
        keep_0 = jnp.where(core_one, blocks[1], blocks[0])
        keep_1 = jnp.where(core_one, blocks[3], blocks[2])
        send_0 = jnp.where(core_one, blocks[0], blocks[1])
        send_1 = jnp.where(core_one, blocks[2], blocks[3])
        refs[0][index] = jnp.where(far_one, keep_1, keep_0)
        refs[1][index] = jnp.where(far_one, keep_0, keep_1)
        refs[2][index] = jnp.where(far_one, send_1, send_0)
        refs[3][index] = jnp.where(far_one, send_0, send_1)

    main_refs = (main_ko, main_kx, main_so, main_sx)
    over_refs = (over_ko, over_kx, over_so, over_sx)

    def reached(d, x):
        r = x + PAD
        first, last = (PAD - 1, PAD + rows) if d == 0 else (PAD, PAD + rows - 1)

        def total(field, places):
            return functools.reduce(
                jnp.add, [field[d, s] for s in places if first <= s <= last]
            )

        value = (RELAX * RELAX) * total(metric, (r - 2, r + 2))
        if first <= r + 1 <= last or first <= r - 1 <= last:
            value = value + total(side, (r - 1, r + 1))
        if first <= r <= last:
            value = value + plane[d, r]
        return value

    for d in range(3):
        for x in range(-REACHES[d], 0):
            put(over_refs, LOW_AT[d] + x + REACHES[d], reached(d, x))
        for x in range(rows, rows + REACHES[d]):
            put(over_refs, OVER + LOW_AT[d] + x - rows, reached(d, x))

    def inner(x, _):
        r = x + PAD
        for d in range(3):
            value = plane[d, r] + (side[d, r - 1] + side[d, r + 1])
            value = value + (RELAX * RELAX) * (metric[d, r - 2] + metric[d, r + 2])
            put(main_refs, (d, x), value)
        return 0

    lax.fori_loop(0, rows, inner, 0)


def front(place, adjoint, flux_terms, instance_count):
    kinds, variables, rows, width, depth = adjoint.shape
    f32 = jnp.float32
    block = width // 4
    main = jax.ShapeDtypeStruct((3, rows, block, depth), f32)
    over = jax.ShapeDtypeStruct((2 * OVER, block, depth), f32)
    vmem = pl.BlockSpec(memory_space=pltpu.VMEM)
    hbm = pl.BlockSpec(memory_space=pltpu.HBM)
    padded = (3, rows + 2 * PAD, width, depth)
    return pl.pallas_call(
        functools.partial(front_kernel, 1.0 / instance_count),
        out_shape=[main] * 4 + [over] * 4,
        in_specs=[pl.BlockSpec(memory_space=pltpu.SMEM), hbm, hbm],
        out_specs=[vmem] * 8,
        scratch_shapes=[
            pltpu.VMEM(adjoint.shape, adjoint.dtype),
            pltpu.VMEM(flux_terms.shape, flux_terms.dtype),
            pltpu.VMEM(padded, f32),
            pltpu.VMEM(padded, f32),
            pltpu.VMEM(padded, f32),
            pltpu.VMEM(padded, f32),
            pltpu.VMEM((depth, 2 * depth), jnp.bfloat16),
            pltpu.SemaphoreType.DMA((rows // CHUNK,)),
            pltpu.SemaphoreType.DMA((rows // CHUNK,)),
        ],
        compiler_params=pltpu.CompilerParams(vmem_limit_bytes=40 * 2**20),
        cost_estimate=pl.CostEstimate(
            flops=60_000_000, bytes_accessed=13_000_000, transcendentals=0
        ),
    )(place, adjoint, flux_terms)


def last_kernel(keep, near, far, from_low, from_high, stiffness, normals, ids, out, share):
    rows, block = keep.shape[1], keep.shape[2]
    total = share.shape[1]
    slots = lax.broadcasted_iota(jnp.int32, (block, total), 1)
    tally = jnp.zeros((block, total), jnp.float32)
    for x in range(rows):
        inverse = RELAX / stiffness[x]
        surface = jnp.zeros((block, 1), jnp.float32)
        for d in range(3):
            value = keep[d, x] + near[d, x] + far[d, x]
            if x < REACHES[d]:
                value = value + from_low[LOW_AT[d] + x]
            if x >= rows - REACHES[d]:
                value = value + from_high[LOW_AT[d] + x - rows + REACHES[d]]
            value = value * inverse
            out[d, x] = value
            surface = surface + normals[d, :, x : x + 1] * value[:, 0:1]
        tally = tally + jnp.where(slots == ids[:, x : x + 1], surface, 0.0)
    share[...] = jnp.sum(tally, axis=0, keepdims=True)


def per_device(adjoint, flux_terms, stiffness, normals, design_map):
    insts, spaces = lax.axis_size("inst"), lax.axis_size("space")
    inst, space = lax.axis_index("inst"), lax.axis_index("space")
    rows, block, depth = stiffness.shape
    width = block * insts
    place = jnp.stack([space > 0, space < spaces - 1, inst % 2, inst // 2]).astype(jnp.int32)

    main_ko, main_kx, main_so, main_sx, over_ko, over_kx, over_so, over_sx = front(
        place, adjoint, flux_terms, adjoint.shape[0] * insts
    )

    other_core = [(i, i ^ 1) for i in range(insts)]
    other_chip = [(i, i ^ 2) for i in range(insts)]
    over_x = over_kx + lax.ppermute(over_sx, "inst", other_core)
    main_x = main_kx + lax.ppermute(main_sx, "inst", other_core)
    over_far = lax.ppermute(over_x, "inst", other_chip)
    main_far = lax.ppermute(main_x, "inst", other_chip)
    over_near = lax.ppermute(over_so, "inst", other_core)
    main_near = lax.ppermute(main_so, "inst", other_core)
    over = over_ko + over_near + over_far
    from_high = lax.ppermute(over[:OVER], "space", [(i + 1, i) for i in range(spaces - 1)])
    from_low = lax.ppermute(over[OVER:], "space", [(i, i + 1) for i in range(spaces - 1)])

    total = DV_DEV * insts * spaces
    vmem = pl.BlockSpec(memory_space=pltpu.VMEM)
    mesh_adjoint, share = pl.pallas_call(
        last_kernel,
        out_shape=[
            jax.ShapeDtypeStruct((3, rows, block, depth), jnp.float32),
            jax.ShapeDtypeStruct((1, total), jnp.float32),
        ],
        in_specs=[vmem] * 8,
        out_specs=[vmem] * 2,
        compiler_params=pltpu.CompilerParams(vmem_limit_bytes=4 * 2**20),
    )(
        main_ko, main_near, main_far, from_low, from_high, stiffness,
        normals.transpose(0, 2, 1), design_map.T,
    )
    shares = lax.all_to_all(
        share.reshape(insts * spaces, DV_DEV), ("inst", "space"), 0, 0, tiled=True
    )
    design_grad = jnp.sum(shares, axis=0)
    return (mesh_adjoint, design_grad)


def solution(mesh):
    in_specs = (
        P("inst", None, "space", None, None),
        P("inst", None, None, "space", None, None),
        P("space", "inst", None),
        P(None, "space", "inst"),
        P("space", "inst"),
    )
    out_specs = (P(None, "space", "inst", None), P(("inst", "space")))
    return jax.shard_map(
        per_device, mesh=mesh, in_specs=in_specs, out_specs=out_specs, check_vma=False
    )
```

```python
import functools
import jax
import jax.numpy as jnp
from jax import lax
from jax.experimental import pallas as pl
from jax.experimental.pallas import tpu as pltpu
from jax.sharding import PartitionSpec as P

DIAG = 6.5
DV_DEV = 8
REACH = 3
PAD = REACH + 1
CHUNK = 4
REACHES = (3, 2, 2)
LOW_AT = (0, 3, 5)
OVER = 7


def shifted_rows(tiles, top, bottom):
    down = [pltpu.roll(t, 1, 0) for t in tiles]
    up = [pltpu.roll(t, 7, 0) for t in tiles]
    zero = jnp.zeros_like(tiles[0])
    down = [jnp.where(top, p, n) for p, n in zip([zero] + down[:-1], down)]
    up = [jnp.where(bottom, n, p) for p, n in zip(up, up[1:] + [zero])]
    return down, up


def front_kernel(
    adj_hbm, flux_hbm,
    main_ko, main_kx, main_so, main_sx, over_ko, over_kx, over_so, over_sx,
    adj, flux, work, metric, plane, side, band, stack, along, adj_sems, flux_sems,
):
    kinds, variables, rows, width, depth = adj.shape
    chunks = rows // CHUNK
    tiles = width // 8
    inst, space = lax.axis_index("inst"), lax.axis_index("space")
    low_open = jnp.where(space > 0, 1.0, 0.0)
    high_open = jnp.where(space < lax.axis_size("space") - 1, 1.0, 0.0)

    def adj_copy(i):
        part = pl.ds(i * CHUNK, CHUNK)
        return pltpu.make_async_copy(
            adj_hbm.at[:, :, part], adj.at[:, :, part], adj_sems.at[i]
        )

    def flux_copy(i):
        part = pl.ds(i * CHUNK, CHUNK)
        return pltpu.make_async_copy(
            flux_hbm.at[:, :, :, part], flux.at[:, :, :, part], flux_sems.at[i]
        )

    for i in range(chunks):
        adj_copy(i).start()
        flux_copy(i).start()

    near = jnp.abs(
        lax.broadcasted_iota(jnp.int32, (depth, depth), 0)
        - lax.broadcasted_iota(jnp.int32, (depth, depth), 1)
    )
    lane = lax.broadcasted_iota(jnp.int32, (depth, depth), 1)
    ends = jnp.where((lane == 0) | (lane == depth - 1), 1.0, 2.0)
    once = jnp.where(near == 1, 1.0, 0.0).astype(jnp.bfloat16)
    twice = jnp.where(near == 0, ends, jnp.where(near == 2, 1.0, 0.0)).astype(jnp.bfloat16)
    for half in (slice(0, depth), slice(depth, 2 * depth)):
        band[half, :depth] = once
        band[half, depth:] = twice
    zero = jnp.zeros((width, depth), jnp.float32)
    for d in range(3):
        for x in (-2, -1, rows, rows + 1):
            metric[d, x + PAD] = zero
            side[d, x + PAD] = zero
            plane[d, x + PAD] = zero
    for x in (-2, -1, rows, rows + 1):
        work[0, x + PAD] = zero

    row = lax.broadcasted_iota(jnp.int32, (8, depth), 0)
    top, bottom = row == 0, row == 7
    column = lax.broadcasted_iota(jnp.int32, (8, depth), 1)
    first, last = column == 0, column == depth - 1

    def weigh(x):
        for h in range(width // 16):
            part = slice(16 * h, 16 * h + 16)
            sums = [jnp.zeros((16, depth), jnp.float32) for _ in range(3)]
            for k in range(kinds):
                for v in range(variables):
                    a = adj[k, v, x, part].astype(jnp.float32)
                    for d in range(3):
                        sums[d] = sums[d] + a * flux[k, v, d, x, part].astype(jnp.float32)
            for d in range(3):
                work[d, x + PAD, part] = sums[d]

    def tile(t):
        return slice(8 * t, 8 * t + 8)

    def planes(slabs):
        count = len(slabs) * width
        for s, (d, x) in enumerate(slabs):
            r = x + PAD
            here = [work[d, r, tile(t)] for t in range(tiles)]
            if d == 0:
                open_ = jnp.where(x < 0, low_open, jnp.where(x >= rows, high_open, 1.0))
                low = [work[0, r - 1, tile(t)] for t in range(tiles)]
                high = [work[0, r + 1, tile(t)] for t in range(tiles)]
                m = [(h + 0.5 * (p - n)) * open_ for h, p, n in zip(here, low, high)]
            elif d == 1:
                low, high = shifted_rows(here, top, bottom)
                m = [h + 0.5 * (p - n) for h, p, n in zip(here, low, high)]
            else:
                m = [
                    h + 0.5 * (
                        jnp.where(first, 0.0, pltpu.roll(h, 1, 1))
                        - jnp.where(last, 0.0, pltpu.roll(h, depth - 1, 1))
                    )
                    for h in here
                ]
            for t in range(tiles):
                metric[d, r, tile(t)] = m[t]
            for t in range(0, tiles, 2):
                both = jnp.concatenate(m[t : t + 2], axis=0)
                rounded = both.astype(jnp.bfloat16)
                part = slice(s * width + 8 * t, s * width + 8 * t + 16)
                stack[part, :depth] = rounded
                stack[part, depth:] = (both - rounded.astype(jnp.float32)).astype(jnp.bfloat16)
        along[:count] = jnp.dot(stack[:count], band[...], preferred_element_type=jnp.float32)
        for s, (d, x) in enumerate(slabs):
            r = x + PAD
            at = s * width
            m = [metric[d, r, tile(t)] for t in range(tiles)]
            along_1 = [along[at + 8 * t : at + 8 * t + 8, :depth] for t in range(tiles)]
            along_2 = [along[at + 8 * t : at + 8 * t + 8, depth:] for t in range(tiles)]
            low, high = shifted_rows(m, top, bottom)
            once = [(p + n) + q for p, n, q in zip(low, high, along_1)]
            low, high = shifted_rows([o + q for o, q in zip(once, along_1)], top, bottom)
            returns = 2.0 - jnp.where(
                x == 0, 1.0 - low_open, jnp.where(x == rows - 1, 1.0 - high_open, 0.0)
            )
            weight = DIAG * DIAG + returns
            for t in range(tiles):
                side[d, r, tile(t)] = DIAG * m[t] + (once[t] + once[t])
                twice = (low[t] + high[t]) + along_2[t]
                plane[d, r, tile(t)] = weight * m[t] + DIAG * once[t] + twice

    def settle(i, extra):
        planes(
            [(1, i * CHUNK + j) for j in range(CHUNK)]
            + [(2, i * CHUNK + j) for j in range(CHUNK)]
            + [(0, i * CHUNK + j - 1) for j in range(CHUNK + extra)]
        )

    def arrive(i):
        adj_copy(i).wait()
        flux_copy(i).wait()

    arrive(0)
    for j in range(CHUNK):
        weigh(j)

    def stage(i, _):
        arrive(i)
        settle(i - 1, 0)
        for j in range(CHUNK):
            weigh(i * CHUNK + j)
        return 0

    lax.fori_loop(1, chunks, stage, 0)
    settle(chunks - 1, 2)

    def put(refs, index, total):
        for j, ref in zip((0, 2, 1, 3), refs):
            at = pl.multiple_of(8 * (inst ^ j), 8)
            ref[index] = total(pl.ds(at, 8))

    main_refs = (main_ko, main_kx, main_so, main_sx)
    over_refs = (over_ko, over_kx, over_so, over_sx)

    def reached(d, x, part):
        r = x + PAD
        first, last = (PAD - 1, PAD + rows) if d == 0 else (PAD, PAD + rows - 1)
        terms = (
            [plane[d, r, part]] * (first <= r <= last)
            + [side[d, s, part] for s in (r - 1, r + 1) if first <= s <= last]
            + [metric[d, s, part] for s in (r - 2, r + 2) if first <= s <= last]
        )
        return functools.reduce(jnp.add, terms)

    for d in range(3):
        for x in range(-REACHES[d], 0):
            put(over_refs, LOW_AT[d] + x + REACHES[d], functools.partial(reached, d, x))
        for x in range(rows, rows + REACHES[d]):
            put(over_refs, OVER + LOW_AT[d] + x - rows, functools.partial(reached, d, x))

    def inner(x, _):
        r = x + PAD
        for d in range(3):

            def total(part):
                value = plane[d, r, part] + (side[d, r - 1, part] + side[d, r + 1, part])
                return value + (metric[d, r - 2, part] + metric[d, r + 2, part])

            put(main_refs, (d, x), total)
        return 0

    lax.fori_loop(0, rows, inner, 0, unroll=2)


def front(adjoint, flux_terms):
    kinds, variables, rows, width, depth = adjoint.shape
    f32 = jnp.float32
    block = width // 4
    main = jax.ShapeDtypeStruct((3, rows, block, depth), f32)
    over = jax.ShapeDtypeStruct((2 * OVER, block, depth), f32)
    vmem = pl.BlockSpec(memory_space=pltpu.VMEM)
    hbm = pl.BlockSpec(memory_space=pltpu.HBM)
    padded = (3, rows + 2 * PAD, width, depth)
    most = (3 * CHUNK + 2) * width
    return pl.pallas_call(
        front_kernel,
        out_shape=[main] * 4 + [over] * 4,
        in_specs=[hbm, hbm],
        out_specs=[vmem] * 8,
        scratch_shapes=[
            pltpu.VMEM(adjoint.shape, adjoint.dtype),
            pltpu.VMEM(flux_terms.shape, flux_terms.dtype),
            pltpu.VMEM(padded, f32),
            pltpu.VMEM(padded, f32),
            pltpu.VMEM(padded, f32),
            pltpu.VMEM(padded, f32),
            pltpu.VMEM((2 * depth, 2 * depth), jnp.bfloat16),
            pltpu.VMEM((most, 2 * depth), jnp.bfloat16),
            pltpu.VMEM((most, 2 * depth), f32),
            pltpu.SemaphoreType.DMA((rows // CHUNK,)),
            pltpu.SemaphoreType.DMA((rows // CHUNK,)),
        ],
        compiler_params=pltpu.CompilerParams(vmem_limit_bytes=60 * 2**20),
        cost_estimate=pl.CostEstimate(
            flops=60_000_000, bytes_accessed=13_000_000, transcendentals=0
        ),
    )(adjoint, flux_terms)


def last_kernel(scale, keep, near, far, from_low, from_high, stiffness, normals, ids, out, share):
    rows, block = keep.shape[1], keep.shape[2]
    total = share.shape[1]
    slots = lax.broadcasted_iota(jnp.int32, (block, total), 1)
    tally = jnp.zeros((block, total), jnp.float32)
    for x in range(rows):
        inverse = scale / stiffness[x]
        surface = jnp.zeros((block, 1), jnp.float32)
        for d in range(3):
            value = keep[d, x] + near[d, x] + far[d, x]
            if x < REACHES[d]:
                value = value + from_low[LOW_AT[d] + x]
            if x >= rows - REACHES[d]:
                value = value + from_high[LOW_AT[d] + x - rows + REACHES[d]]
            value = value * inverse
            out[d, x] = value
            surface = surface + normals[d, :, x : x + 1] * value[:, 0:1]
        tally = tally + jnp.where(slots == ids[:, x : x + 1], surface, 0.0)
    share[...] = jnp.sum(tally, axis=0, keepdims=True)


def per_device(adjoint, flux_terms, stiffness, normals, design_map):
    insts, spaces = lax.axis_size("inst"), lax.axis_size("space")
    inst, space = lax.axis_index("inst"), lax.axis_index("space")
    rows, block, depth = stiffness.shape

    main_ko, main_kx, main_so, main_sx, over_ko, over_kx, over_so, over_sx = front(
        adjoint, flux_terms
    )

    other_core = [(i, i ^ 1) for i in range(insts)]
    other_chip = [(i, i ^ 2) for i in range(insts)]
    over_x = over_kx + lax.ppermute(over_sx, "inst", other_core)
    main_x = main_kx + lax.ppermute(main_sx, "inst", other_core)
    over_far = lax.ppermute(over_x, "inst", other_chip)
    main_far = lax.ppermute(main_x, "inst", other_chip)
    over_near = lax.ppermute(over_so, "inst", other_core)
    main_near = lax.ppermute(main_so, "inst", other_core)
    over = over_ko + over_near + over_far
    even = space % 2 == 0
    low, high = over[:OVER], over[OVER:]
    inside = [(i, i ^ 1) for i in range(spaces)]
    across = [(i, ((i + 1) ^ 1) - 1) for i in range(1, spaces - 1)]
    from_inside = lax.ppermute(jnp.where(even, high, low), "space", inside)
    from_across = lax.ppermute(jnp.where(even, low, high), "space", across)
    from_high = jnp.where(even, from_inside, from_across)
    from_low = jnp.where(even, from_across, from_inside)

    total = DV_DEV * insts * spaces
    vmem = pl.BlockSpec(memory_space=pltpu.VMEM)
    mesh_adjoint, share = pl.pallas_call(
        functools.partial(last_kernel, 1.0 / (DIAG**3 * adjoint.shape[0] * insts)),
        out_shape=[
            jax.ShapeDtypeStruct((3, rows, block, depth), jnp.float32),
            jax.ShapeDtypeStruct((1, total), jnp.float32),
        ],
        in_specs=[vmem] * 8,
        out_specs=[vmem] * 2,
        compiler_params=pltpu.CompilerParams(vmem_limit_bytes=4 * 2**20),
    )(
        main_ko, main_near, main_far, from_low, from_high, stiffness,
        normals.transpose(0, 2, 1), design_map.T,
    )
    shares = lax.all_to_all(
        share.reshape(insts * spaces, DV_DEV), ("inst", "space"), 0, 0, tiled=True
    )
    design_grad = jnp.sum(shares, axis=0)
    return (mesh_adjoint, design_grad)


def solution(mesh):
    in_specs = (
        P("inst", None, "space", None, None),
        P("inst", None, None, "space", None, None),
        P("space", "inst", None),
        P(None, "space", "inst"),
        P("space", "inst"),
    )
    out_specs = (P(None, "space", "inst", None), P(("inst", "space")))
    return jax.shard_map(
        per_device, mesh=mesh, in_specs=in_specs, out_specs=out_specs, check_vma=False
    )
```

```python
import functools
import jax
import jax.numpy as jnp
from jax import lax
from jax.experimental import pallas as pl
from jax.experimental.pallas import tpu as pltpu
from jax.sharding import PartitionSpec as P

DIAG = 6.5
DV_DEV = 8
REACH = 3
PAD = REACH + 1
CHUNK = 4
REACHES = (3, 2, 2)
LOW_AT = (0, 3, 5)
OVER = 7
FACE = 2 * OVER
GROUP = 64
FACE_AT = (REACH, 24, 44)


def shifted_rows(tiles, top, bottom):
    down = [pltpu.roll(t, 1, 0) for t in tiles]
    up = [pltpu.roll(t, 7, 0) for t in tiles]
    zero = jnp.zeros_like(tiles[0])
    down = [jnp.where(top, p, n) for p, n in zip([zero] + down[:-1], down)]
    up = [jnp.where(bottom, n, p) for p, n in zip(up, up[1:] + [zero])]
    return down, up


def front_kernel(
    adj_hbm, flux_hbm,
    main_ko, main_kx, main_so, main_sx, over_ko, over_kx, over_s,
    adj, flux, work, metric, plane, side, band, stack, along, adj_sems, flux_sems,
):
    kinds, variables, rows, width, depth = adj.shape
    chunks = rows // CHUNK
    tiles = width // 8
    inst, space = lax.axis_index("inst"), lax.axis_index("space")
    low_open = jnp.where(space > 0, 1.0, 0.0)
    high_open = jnp.where(space < lax.axis_size("space") - 1, 1.0, 0.0)

    def adj_copy(i):
        part = pl.ds(i * CHUNK, CHUNK)
        return pltpu.make_async_copy(
            adj_hbm.at[:, :, part], adj.at[:, :, part], adj_sems.at[i]
        )

    def flux_copy(i):
        part = pl.ds(i * CHUNK, CHUNK)
        return pltpu.make_async_copy(
            flux_hbm.at[:, :, :, part], flux.at[:, :, :, part], flux_sems.at[i]
        )

    for i in range(chunks):
        adj_copy(i).start()
        flux_copy(i).start()

    near = jnp.abs(
        lax.broadcasted_iota(jnp.int32, (depth, depth), 0)
        - lax.broadcasted_iota(jnp.int32, (depth, depth), 1)
    )
    lane = lax.broadcasted_iota(jnp.int32, (depth, depth), 1)
    ends = jnp.where((lane == 0) | (lane == depth - 1), 1.0, 2.0)
    once = jnp.where(near == 1, 1.0, 0.0).astype(jnp.bfloat16)
    twice = jnp.where(near == 0, ends, jnp.where(near == 2, 1.0, 0.0)).astype(jnp.bfloat16)
    for half in (slice(0, depth), slice(depth, 2 * depth)):
        band[half, :depth] = once
        band[half, depth:] = twice
    zero = jnp.zeros((width, depth), jnp.float32)
    for d in range(3):
        for x in (-2, -1, rows, rows + 1):
            metric[d, x + PAD] = zero
            side[d, x + PAD] = zero
            plane[d, x + PAD] = zero
    for x in (-2, -1, rows, rows + 1):
        work[0, x + PAD] = zero

    row = lax.broadcasted_iota(jnp.int32, (8, depth), 0)
    top, bottom = row == 0, row == 7
    column = lax.broadcasted_iota(jnp.int32, (8, depth), 1)
    first, last = column == 0, column == depth - 1

    def weigh(x):
        for h in range(width // 16):
            part = slice(16 * h, 16 * h + 16)
            sums = [jnp.zeros((16, depth), jnp.float32) for _ in range(3)]
            for k in range(kinds):
                for v in range(variables):
                    a = adj[k, v, x, part].astype(jnp.float32)
                    for d in range(3):
                        sums[d] = sums[d] + a * flux[k, v, d, x, part].astype(jnp.float32)
            for d in range(3):
                work[d, x + PAD, part] = sums[d]

    def tile(t):
        return slice(8 * t, 8 * t + 8)

    def planes(slabs):
        count = len(slabs) * width
        for s, (d, x) in enumerate(slabs):
            r = x + PAD
            here = [work[d, r, tile(t)] for t in range(tiles)]
            if d == 0:
                open_ = jnp.where(x < 0, low_open, jnp.where(x >= rows, high_open, 1.0))
                low = [work[0, r - 1, tile(t)] for t in range(tiles)]
                high = [work[0, r + 1, tile(t)] for t in range(tiles)]
                m = [(h + 0.5 * (p - n)) * open_ for h, p, n in zip(here, low, high)]
            elif d == 1:
                low, high = shifted_rows(here, top, bottom)
                m = [h + 0.5 * (p - n) for h, p, n in zip(here, low, high)]
            else:
                m = [
                    h + 0.5 * (
                        jnp.where(first, 0.0, pltpu.roll(h, 1, 1))
                        - jnp.where(last, 0.0, pltpu.roll(h, depth - 1, 1))
                    )
                    for h in here
                ]
            for t in range(tiles):
                metric[d, r, tile(t)] = m[t]
            for t in range(0, tiles, 2):
                both = jnp.concatenate(m[t : t + 2], axis=0)
                rounded = both.astype(jnp.bfloat16)
                part = slice(s * width + 8 * t, s * width + 8 * t + 16)
                stack[part, :depth] = rounded
                stack[part, depth:] = (both - rounded.astype(jnp.float32)).astype(jnp.bfloat16)
        along[:count] = jnp.dot(stack[:count], band[...], preferred_element_type=jnp.float32)
        for s, (d, x) in enumerate(slabs):
            r = x + PAD
            at = s * width
            m = [metric[d, r, tile(t)] for t in range(tiles)]
            along_1 = [along[at + 8 * t : at + 8 * t + 8, :depth] for t in range(tiles)]
            along_2 = [along[at + 8 * t : at + 8 * t + 8, depth:] for t in range(tiles)]
            low, high = shifted_rows(m, top, bottom)
            once = [(p + n) + q for p, n, q in zip(low, high, along_1)]
            low, high = shifted_rows([o + q for o, q in zip(once, along_1)], top, bottom)
            returns = 2.0 - jnp.where(
                x == 0, 1.0 - low_open, jnp.where(x == rows - 1, 1.0 - high_open, 0.0)
            )
            weight = DIAG * DIAG + returns
            for t in range(tiles):
                side[d, r, tile(t)] = DIAG * m[t] + (once[t] + once[t])
                twice = (low[t] + high[t]) + along_2[t]
                plane[d, r, tile(t)] = weight * m[t] + DIAG * once[t] + twice

    def settle(i, extra):
        planes(
            [(1, i * CHUNK + j) for j in range(CHUNK)]
            + [(2, i * CHUNK + j) for j in range(CHUNK)]
            + [(0, i * CHUNK + j - 1) for j in range(CHUNK + extra)]
        )

    def arrive(i):
        adj_copy(i).wait()
        flux_copy(i).wait()

    arrive(0)
    for j in range(CHUNK):
        weigh(j)

    def stage(i, _):
        arrive(i)
        settle(i - 1, 0)
        for j in range(CHUNK):
            weigh(i * CHUNK + j)
        return 0

    lax.fori_loop(1, chunks, stage, 0)
    settle(chunks - 1, 2)

    def put(refs, index, place, total, face):
        for j, ref, shift in zip((0, 2, 1, 3), refs, (0, 0, FACE + 1, 0)):
            b = inst ^ j
            at = pl.multiple_of(8 * b, 8)
            value = total(pl.ds(at, 8))
            if ref is over_s:
                ref[index + shift] = value
            else:
                ref[index] = value
            face = jnp.where(column == GROUP * b + place, value[:, 0:1], face)
        return face

    main_refs = (main_ko, main_kx, main_so, main_sx)
    over_refs = (over_ko, over_kx, over_s, over_s)

    def reached(d, x, part):
        r = x + PAD
        first, last = (PAD - 1, PAD + rows) if d == 0 else (PAD, PAD + rows - 1)
        terms = (
            [plane[d, r, part]] * (first <= r <= last)
            + [side[d, s, part] for s in (r - 1, r + 1) if first <= s <= last]
            + [metric[d, s, part] for s in (r - 2, r + 2) if first <= s <= last]
        )
        return functools.reduce(jnp.add, terms)

    face = jnp.zeros((8, depth), jnp.float32)
    for d in range(3):
        for x in range(-REACHES[d], 0):
            face = put(
                over_refs, LOW_AT[d] + x + REACHES[d], FACE_AT[d] + x,
                functools.partial(reached, d, x), face,
            )
        for x in range(rows, rows + REACHES[d]):
            face = put(
                over_refs, OVER + LOW_AT[d] + x - rows, FACE_AT[d] + x,
                functools.partial(reached, d, x), face,
            )

    def inner(x, face):
        r = x + PAD
        for d in range(3):

            def total(part):
                value = plane[d, r, part] + (side[d, r - 1, part] + side[d, r + 1, part])
                return value + (metric[d, r - 2, part] + metric[d, r + 2, part])

            face = put(main_refs, (d, x), FACE_AT[d] + x, total, face)
        return face

    face = lax.fori_loop(0, rows, inner, face, unroll=2)
    over_kx[FACE] = face
    over_s[FACE] = face


def front(adjoint, flux_terms):
    kinds, variables, rows, width, depth = adjoint.shape
    f32 = jnp.float32
    block = width // 4
    main = jax.ShapeDtypeStruct((3, rows, block, depth), f32)
    vmem = pl.BlockSpec(memory_space=pltpu.VMEM)
    hbm = pl.BlockSpec(memory_space=pltpu.HBM)
    padded = (3, rows + 2 * PAD, width, depth)
    most = (3 * CHUNK + 2) * width
    over_rows = (2 * OVER, FACE + 1, FACE + 1 + 2 * OVER)
    return pl.pallas_call(
        front_kernel,
        out_shape=[main] * 4
        + [jax.ShapeDtypeStruct((count, block, depth), f32) for count in over_rows],
        in_specs=[hbm] * 2,
        out_specs=[vmem] * 7,
        scratch_shapes=[
            pltpu.VMEM(adjoint.shape, adjoint.dtype),
            pltpu.VMEM(flux_terms.shape, flux_terms.dtype),
            pltpu.VMEM(padded, f32),
            pltpu.VMEM(padded, f32),
            pltpu.VMEM(padded, f32),
            pltpu.VMEM(padded, f32),
            pltpu.VMEM((2 * depth, 2 * depth), jnp.bfloat16),
            pltpu.VMEM((most, 2 * depth), jnp.bfloat16),
            pltpu.VMEM((most, 2 * depth), f32),
            pltpu.SemaphoreType.DMA((rows // CHUNK,)),
            pltpu.SemaphoreType.DMA((rows // CHUNK,)),
        ],
        compiler_params=pltpu.CompilerParams(vmem_limit_bytes=51 * 2**20),
        cost_estimate=pl.CostEstimate(
            flops=60_000_000, bytes_accessed=13_000_000, transcendentals=0
        ),
    )(adjoint, flux_terms)


def coefs_kernel(after, stiffness, normals, ids, out):
    del after
    rows, block, depth = stiffness.shape
    column = lax.broadcasted_iota(jnp.int32, (block, depth), 1)
    own = GROUP * lax.axis_index("inst")
    coefs = jnp.zeros((block, depth), jnp.float32)
    for x in range(rows):
        inverse = 1.0 / stiffness[x, :, 0:1]
        for d in range(3):
            here = normals[d, :, x : x + 1] * inverse
            coefs = jnp.where(column == own + d * rows + x, here, coefs)
        here = ids[:, x : x + 1].astype(jnp.float32)
        coefs = jnp.where(column == own + 3 * rows + x, here, coefs)
    out[0] = coefs


def add_kernel(keep, near, after, out):
    del after
    for d in range(out.shape[0]):
        for x in range(out.shape[1]):
            out[d, x] = keep[d, x] + near[d, x]


def over_kernel(keep, near, first, far, main, inside, across, wall):
    del main
    even = lax.axis_index("space") % 2 == 0
    for i in range(OVER):
        low = keep[i] + near[FACE + 1 + i] + far[i]
        high = keep[OVER + i] + near[FACE + 1 + OVER + i] + far[OVER + i]
        inside[i] = jnp.where(even, high, low)
        across[i] = jnp.where(even, low, high)
    face = first[FACE] + far[FACE]
    inside[OVER] = face
    across[OVER] = face
    wall[0] = face
    wall[1] = first[FACE + 1] + far[FACE + 1]


def design_kernel(scale, rows, wall, from_inside, from_across, share):
    block, depth = wall.shape[1:]
    total = share.shape[1]
    even = lax.axis_index("space") % 2 == 0
    column = lax.broadcasted_iota(jnp.int32, (block, depth), 1) % GROUP
    face, coefs = wall[0], wall[1]
    inside, across = from_inside[OVER], from_across[OVER]
    from_high = pltpu.roll(jnp.where(even, inside, across), rows, 1)
    from_low = pltpu.roll(jnp.where(even, across, inside), depth - rows, 1)
    surface = jnp.zeros((block, depth), jnp.float32)
    for d in range(3):
        at, reach = FACE_AT[d], REACHES[d]
        whole = (
            face
            + jnp.where((column >= at) & (column < at + reach), from_low, 0.0)
            + jnp.where((column >= at + rows - reach) & (column < at + rows), from_high, 0.0)
        )
        turned = pltpu.roll(coefs, depth - d * rows, 1) if d else coefs
        surface = surface + pltpu.roll(whole, depth - at, 1) * turned
    ids = pltpu.roll(coefs, depth - 3 * rows, 1).astype(jnp.int32)
    slots = lax.broadcasted_iota(jnp.int32, (block, total), 1)
    tally = jnp.zeros((block, total), jnp.float32)
    for group in range(0, depth, GROUP):
        for x in range(group, group + rows):
            tally = tally + jnp.where(slots == ids[:, x : x + 1], surface[:, x : x + 1], 0.0)
    share[...] = jnp.sum(tally, axis=0, keepdims=True) * scale


def last_kernel(scale, keep, near, far, from_inside, from_across, stiffness, out):
    rows = keep.shape[1]
    even = lax.axis_index("space") % 2 == 0
    for x in range(rows):
        inverse = scale / stiffness[x]
        for d in range(3):
            value = keep[d, x] + near[d, x] + far[d, x]
            if x < REACHES[d]:
                at = LOW_AT[d] + x
                value = value + jnp.where(even, from_across[at], from_inside[at])
            if x >= rows - REACHES[d]:
                at = LOW_AT[d] + x - rows + REACHES[d]
                value = value + jnp.where(even, from_inside[at], from_across[at])
            out[d, x] = value * inverse


def per_device(adjoint, flux_terms, stiffness, normals, design_map):
    insts, spaces = lax.axis_size("inst"), lax.axis_size("space")
    inst, space = lax.axis_index("inst"), lax.axis_index("space")
    rows, block, depth = stiffness.shape
    scale = 1.0 / (DIAG**3 * adjoint.shape[0] * insts)

    vmem = pl.BlockSpec(memory_space=pltpu.VMEM)

    def on_chip(kernel, shapes, *operands):
        out = [jax.ShapeDtypeStruct(shape, jnp.float32) for shape in shapes]
        return pl.pallas_call(
            kernel,
            out_shape=out,
            in_specs=[vmem] * len(operands),
            out_specs=[vmem] * len(out),
            compiler_params=pltpu.CompilerParams(vmem_limit_bytes=4 * 2**20),
            cost_estimate=pl.CostEstimate(
                flops=500_000, bytes_accessed=1_500_000, transcendentals=0
            ),
        )(*operands)

    main_ko, main_kx, main_so, main_sx, over_ko, over_kx, over_s = front(adjoint, flux_terms)

    other_core = [(i, i ^ 1) for i in range(insts)]
    other_chip = [(i, i ^ 2) for i in range(insts)]
    over_r = lax.ppermute(over_s, "inst", other_core)
    main_r = lax.ppermute(main_sx, "inst", other_core)
    [coefs] = on_chip(
        coefs_kernel, [(1, block, depth)],
        over_kx, stiffness, normals.transpose(0, 2, 1), design_map.T,
    )
    coefs_r = lax.ppermute(coefs, "inst", other_core)
    main_near = lax.ppermute(main_so, "inst", other_core)
    over_x = jnp.concatenate([over_kx + over_r[: FACE + 1], coefs + coefs_r])
    over_far = lax.ppermute(over_x, "inst", other_chip)
    [main_x] = on_chip(add_kernel, [main_kx.shape], main_kx, main_r, over_x)
    main_far = lax.ppermute(main_x, "inst", other_chip)

    halo = (OVER + 1, block, depth)
    to_inside, to_across, wall = on_chip(
        over_kernel, [halo, halo, (2, block, depth)], over_ko, over_r, over_x, over_far, main_x
    )
    inside = [(i, i ^ 1) for i in range(spaces)]
    across = [(i, ((i + 1) ^ 1) - 1) for i in range(1, spaces - 1)]
    from_inside = lax.ppermute(to_inside, "space", inside)
    from_across = lax.ppermute(to_across, "space", across)

    total = DV_DEV * insts * spaces
    [share] = on_chip(
        functools.partial(design_kernel, scale, rows), [(1, total)],
        wall, from_inside, from_across,
    )
    step = 1
    while step < spaces:
        share = share + lax.ppermute(share, "space", [(i, i ^ step) for i in range(spaces)])
        step *= 2
    mine = (inst * spaces + space) * DV_DEV
    design_grad = lax.dynamic_slice(share, (0, mine), (1, DV_DEV)).reshape(DV_DEV)

    [mesh_adjoint] = on_chip(
        functools.partial(last_kernel, scale), [(3, rows, block, depth)],
        main_ko, main_near, main_far, from_inside, from_across, stiffness,
    )
    return (mesh_adjoint, design_grad)


def solution(mesh):
    in_specs = (
        P("inst", None, "space", None, None),
        P("inst", None, None, "space", None, None),
        P("space", "inst", None),
        P(None, "space", "inst"),
        P("space", "inst"),
    )
    out_specs = (P(None, "space", "inst", None), P(("inst", "space")))
    return jax.shard_map(
        per_device, mesh=mesh, in_specs=in_specs, out_specs=out_specs, check_vma=False
    )
```

```python
import functools
import itertools
import jax
import jax.numpy as jnp
from jax import lax
from jax.experimental import pallas as pl
from jax.experimental.pallas import tpu as pltpu
from jax.sharding import PartitionSpec as P

DIAG = 6.5
DV_DEV = 8
REACH = 3
PAD = REACH + 1
CHUNK = 4
REACHES = (3, 2, 2)
LOW_AT = (0, 3, 5)
OVER = 7
FACE = 2 * OVER
GROUP = 64
FACE_AT = (REACH, 24, 44)


def shifted_rows(tiles, top, bottom):
    down = [pltpu.roll(t, 1, 0) for t in tiles]
    up = [pltpu.roll(t, 7, 0) for t in tiles]
    zero = jnp.zeros_like(tiles[0])
    down = [jnp.where(top, p, n) for p, n in zip([zero] + down[:-1], down)]
    up = [jnp.where(bottom, n, p) for p, n in zip(up, up[1:] + [zero])]
    return down, up


def front_kernel(
    adj_hbm, flux_hbm,
    main_ko, main_kx, main_so, main_sx, over_ko, over_kx, over_s,
    adj, flux, work, metric, plane, side, band, stack, along, adj_sems, flux_sems,
):
    kinds, variables, rows, width, depth = adj.shape
    chunks = rows // CHUNK
    tiles = width // 8
    inst, space = lax.axis_index("inst"), lax.axis_index("space")
    low_open = jnp.where(space > 0, 1.0, 0.0)
    high_open = jnp.where(space < lax.axis_size("space") - 1, 1.0, 0.0)

    def adj_copy(i):
        part = pl.ds(i * CHUNK, CHUNK)
        return pltpu.make_async_copy(
            adj_hbm.at[:, :, part], adj.at[:, :, part], adj_sems.at[i]
        )

    def flux_copy(i):
        part = pl.ds(i * CHUNK, CHUNK)
        return pltpu.make_async_copy(
            flux_hbm.at[:, :, :, part], flux.at[:, :, :, part], flux_sems.at[i]
        )

    for i in range(chunks):
        adj_copy(i).start()
        flux_copy(i).start()

    near = jnp.abs(
        lax.broadcasted_iota(jnp.int32, (depth, depth), 0)
        - lax.broadcasted_iota(jnp.int32, (depth, depth), 1)
    )
    lane = lax.broadcasted_iota(jnp.int32, (depth, depth), 1)
    ends = jnp.where((lane == 0) | (lane == depth - 1), 1.0, 2.0)
    once = jnp.where(near == 1, 1.0, 0.0).astype(jnp.bfloat16)
    twice = jnp.where(near == 0, ends, jnp.where(near == 2, 1.0, 0.0)).astype(jnp.bfloat16)
    for half in (slice(0, depth), slice(depth, 2 * depth)):
        band[half, :depth] = once
        band[half, depth:] = twice
    zero = jnp.zeros((width, depth), jnp.float32)
    for d in range(3):
        for x in (-2, -1, rows, rows + 1):
            metric[d, x + PAD] = zero
            side[d, x + PAD] = zero
            plane[d, x + PAD] = zero
    for x in (-2, -1, rows, rows + 1):
        work[0, x + PAD] = zero

    row = lax.broadcasted_iota(jnp.int32, (8, depth), 0)
    top, bottom = row == 0, row == 7
    column = lax.broadcasted_iota(jnp.int32, (8, depth), 1)
    first, last = column == 0, column == depth - 1

    def weigh(x):
        for h in range(width // 16):
            part = slice(16 * h, 16 * h + 16)
            sums = [jnp.zeros((16, depth), jnp.float32) for _ in range(3)]
            for k in range(kinds):
                for v in range(variables):
                    a = adj[k, v, x, part].astype(jnp.float32)
                    for d in range(3):
                        sums[d] = sums[d] + a * flux[k, v, d, x, part].astype(jnp.float32)
            for d in range(3):
                work[d, x + PAD, part] = sums[d]

    def tile(t):
        return slice(8 * t, 8 * t + 8)

    def planes(slabs):
        count = len(slabs) * width
        for s, (d, x) in enumerate(slabs):
            r = x + PAD
            here = [work[d, r, tile(t)] for t in range(tiles)]
            if d == 0:
                open_ = jnp.where(x < 0, low_open, jnp.where(x >= rows, high_open, 1.0))
                low = [work[0, r - 1, tile(t)] for t in range(tiles)]
                high = [work[0, r + 1, tile(t)] for t in range(tiles)]
                m = [(h + 0.5 * (p - n)) * open_ for h, p, n in zip(here, low, high)]
            elif d == 1:
                low, high = shifted_rows(here, top, bottom)
                m = [h + 0.5 * (p - n) for h, p, n in zip(here, low, high)]
            else:
                m = [
                    h + 0.5 * (
                        jnp.where(first, 0.0, pltpu.roll(h, 1, 1))
                        - jnp.where(last, 0.0, pltpu.roll(h, depth - 1, 1))
                    )
                    for h in here
                ]
            for t in range(tiles):
                metric[d, r, tile(t)] = m[t]
            for t in range(0, tiles, 2):
                both = jnp.concatenate(m[t : t + 2], axis=0)
                rounded = both.astype(jnp.bfloat16)
                part = slice(s * width + 8 * t, s * width + 8 * t + 16)
                stack[part, :depth] = rounded
                stack[part, depth:] = (both - rounded.astype(jnp.float32)).astype(jnp.bfloat16)
        along[:count] = jnp.dot(stack[:count], band[...], preferred_element_type=jnp.float32)
        for s, (d, x) in enumerate(slabs):
            r = x + PAD
            at = s * width
            m = [metric[d, r, tile(t)] for t in range(tiles)]
            along_1 = [along[at + 8 * t : at + 8 * t + 8, :depth] for t in range(tiles)]
            along_2 = [along[at + 8 * t : at + 8 * t + 8, depth:] for t in range(tiles)]
            low, high = shifted_rows(m, top, bottom)
            once = [(p + n) + q for p, n, q in zip(low, high, along_1)]
            low, high = shifted_rows([o + q for o, q in zip(once, along_1)], top, bottom)
            returns = 2.0 - jnp.where(
                x == 0, 1.0 - low_open, jnp.where(x == rows - 1, 1.0 - high_open, 0.0)
            )
            weight = DIAG * DIAG + returns
            for t in range(tiles):
                side[d, r, tile(t)] = DIAG * m[t] + (once[t] + once[t])
                twice = (low[t] + high[t]) + along_2[t]
                plane[d, r, tile(t)] = weight * m[t] + DIAG * once[t] + twice

    def settle(i, extra):
        planes(
            [(1, i * CHUNK + j) for j in range(CHUNK)]
            + [(2, i * CHUNK + j) for j in range(CHUNK)]
            + [(0, i * CHUNK + j - 1) for j in range(CHUNK + extra)]
        )

    def arrive(i):
        adj_copy(i).wait()
        flux_copy(i).wait()

    arrive(0)
    for j in range(CHUNK):
        weigh(j)

    def stage(i, _):
        arrive(i)
        settle(i - 1, 0)
        for j in range(CHUNK):
            weigh(i * CHUNK + j)
        return 0

    lax.fori_loop(1, chunks, stage, 0)
    settle(chunks - 1, 2)

    def put(refs, index, place, total, face):
        for j, ref, shift in zip((0, 2, 1, 3), refs, (0, 0, FACE + 1, 0)):
            b = inst ^ j
            at = pl.multiple_of(8 * b, 8)
            value = total(pl.ds(at, 8))
            if ref is over_s:
                ref[index + shift] = value
            else:
                ref[index] = value
            face = jnp.where(column == GROUP * b + place, value[:, 0:1], face)
        return face

    main_refs = (main_ko, main_kx, main_so, main_sx)
    over_refs = (over_ko, over_kx, over_s, over_s)

    def reached(d, x, part):
        r = x + PAD
        first, last = (PAD - 1, PAD + rows) if d == 0 else (PAD, PAD + rows - 1)
        terms = (
            [plane[d, r, part]] * (first <= r <= last)
            + [side[d, s, part] for s in (r - 1, r + 1) if first <= s <= last]
            + [metric[d, s, part] for s in (r - 2, r + 2) if first <= s <= last]
        )
        return functools.reduce(jnp.add, terms)

    face = jnp.zeros((8, depth), jnp.float32)
    for d in range(3):
        for x in range(-REACHES[d], 0):
            face = put(
                over_refs, LOW_AT[d] + x + REACHES[d], FACE_AT[d] + x,
                functools.partial(reached, d, x), face,
            )
        for x in range(rows, rows + REACHES[d]):
            face = put(
                over_refs, OVER + LOW_AT[d] + x - rows, FACE_AT[d] + x,
                functools.partial(reached, d, x), face,
            )

    def inner(x, face):
        r = x + PAD
        for d in range(3):

            def total(part):
                value = plane[d, r, part] + (side[d, r - 1, part] + side[d, r + 1, part])
                return value + (metric[d, r - 2, part] + metric[d, r + 2, part])

            face = put(main_refs, (d, x), FACE_AT[d] + x, total, face)
        return face

    face = lax.fori_loop(0, rows, inner, face, unroll=2)
    over_kx[FACE] = face
    over_s[FACE] = face


def front(adjoint, flux_terms):
    kinds, variables, rows, width, depth = adjoint.shape
    f32 = jnp.float32
    block = width // 4
    main = jax.ShapeDtypeStruct((3, rows, block, depth), f32)
    vmem = pl.BlockSpec(memory_space=pltpu.VMEM)
    hbm = pl.BlockSpec(memory_space=pltpu.HBM)
    padded = (3, rows + 2 * PAD, width, depth)
    most = (3 * CHUNK + 2) * width
    over_rows = (2 * OVER, FACE + 1, FACE + 1 + 2 * OVER)
    return pl.pallas_call(
        front_kernel,
        out_shape=[main] * 4
        + [jax.ShapeDtypeStruct((count, block, depth), f32) for count in over_rows],
        in_specs=[hbm] * 2,
        out_specs=[vmem] * 7,
        scratch_shapes=[
            pltpu.VMEM(adjoint.shape, adjoint.dtype),
            pltpu.VMEM(flux_terms.shape, flux_terms.dtype),
            pltpu.VMEM(padded, f32),
            pltpu.VMEM(padded, f32),
            pltpu.VMEM(padded, f32),
            pltpu.VMEM(padded, f32),
            pltpu.VMEM((2 * depth, 2 * depth), jnp.bfloat16),
            pltpu.VMEM((most, 2 * depth), jnp.bfloat16),
            pltpu.VMEM((most, 2 * depth), f32),
            pltpu.SemaphoreType.DMA((rows // CHUNK,)),
            pltpu.SemaphoreType.DMA((rows // CHUNK,)),
        ],
        compiler_params=pltpu.CompilerParams(vmem_limit_bytes=51 * 2**20),
        cost_estimate=pl.CostEstimate(
            flops=60_000_000, bytes_accessed=13_000_000, transcendentals=0
        ),
    )(adjoint, flux_terms)


def coefs_kernel(after, stiffness, normals, ids, out):
    del after
    rows, block, depth = stiffness.shape
    column = lax.broadcasted_iota(jnp.int32, (block, depth), 1)
    own = GROUP * lax.axis_index("inst")
    coefs = jnp.zeros((block, depth), jnp.float32)
    for x in range(rows):
        inverse = 1.0 / stiffness[x, :, 0:1]
        for d in range(3):
            here = normals[d, :, x : x + 1] * inverse
            coefs = jnp.where(column == own + d * rows + x, here, coefs)
        here = ids[:, x : x + 1].astype(jnp.float32)
        coefs = jnp.where(column == own + 3 * rows + x, here, coefs)
    out[0] = coefs


def add_kernel(keep, near, after, out):
    del after
    for d in range(out.shape[0]):
        for x in range(out.shape[1]):
            out[d, x] = keep[d, x] + near[d, x]


def over_kernel(keep, near, first, far, main, inside, across, wall):
    del main
    even = lax.axis_index("space") % 2 == 0
    for i in range(OVER):
        low = keep[i] + near[FACE + 1 + i] + far[i]
        high = keep[OVER + i] + near[FACE + 1 + OVER + i] + far[OVER + i]
        inside[i] = jnp.where(even, high, low)
        across[i] = jnp.where(even, low, high)
    face = first[FACE] + far[FACE]
    inside[OVER] = face
    across[OVER] = face
    wall[0] = face
    wall[1] = first[FACE + 1] + far[FACE + 1]


def design_kernel(scale, rows, wall, from_inside, from_across, share):
    block, depth = wall.shape[1:]
    total = share.shape[1]
    even = lax.axis_index("space") % 2 == 0
    column = lax.broadcasted_iota(jnp.int32, (block, depth), 1) % GROUP
    face, coefs = wall[0], wall[1]
    inside, across = from_inside[OVER], from_across[OVER]
    from_high = pltpu.roll(jnp.where(even, inside, across), rows, 1)
    from_low = pltpu.roll(jnp.where(even, across, inside), depth - rows, 1)
    surface = jnp.zeros((block, depth), jnp.float32)
    for d in range(3):
        at, reach = FACE_AT[d], REACHES[d]
        whole = (
            face
            + jnp.where((column >= at) & (column < at + reach), from_low, 0.0)
            + jnp.where((column >= at + rows - reach) & (column < at + rows), from_high, 0.0)
        )
        turned = pltpu.roll(coefs, depth - d * rows, 1) if d else coefs
        surface = surface + pltpu.roll(whole, depth - at, 1) * turned
    ids = pltpu.roll(coefs, depth - 3 * rows, 1).astype(jnp.int32)
    slots = lax.broadcasted_iota(jnp.int32, (block, total), 1)
    tally = jnp.zeros((block, total), jnp.float32)
    for group in range(0, depth, GROUP):
        for x in range(group, group + rows):
            tally = tally + jnp.where(slots == ids[:, x : x + 1], surface[:, x : x + 1], 0.0)
    share[...] = jnp.sum(tally, axis=0, keepdims=True) * scale


def last_kernel(scale, keep, near, far, from_inside, from_across, stiffness, out):
    rows = keep.shape[1]
    even = lax.axis_index("space") % 2 == 0
    for x in range(rows):
        inverse = scale / stiffness[x]
        for d in range(3):
            value = keep[d, x] + near[d, x] + far[d, x]
            if x < REACHES[d]:
                at = LOW_AT[d] + x
                value = value + jnp.where(even, from_across[at], from_inside[at])
            if x >= rows - REACHES[d]:
                at = LOW_AT[d] + x - rows + REACHES[d]
                value = value + jnp.where(even, from_inside[at], from_across[at])
            out[d, x] = value * inverse


def per_device(adjoint, flux_terms, stiffness, normals, design_map):
    insts, spaces = lax.axis_size("inst"), lax.axis_size("space")
    inst, space = lax.axis_index("inst"), lax.axis_index("space")
    rows, block, depth = stiffness.shape
    scale = 1.0 / (DIAG**3 * adjoint.shape[0] * insts)

    vmem = pl.BlockSpec(memory_space=pltpu.VMEM)

    def on_chip(kernel, shapes, *operands, weight=1):
        out = [jax.ShapeDtypeStruct(shape, jnp.float32) for shape in shapes]
        return pl.pallas_call(
            kernel,
            out_shape=out,
            in_specs=[vmem] * len(operands),
            out_specs=[vmem] * len(out),
            compiler_params=pltpu.CompilerParams(vmem_limit_bytes=4 * 2**20),
            cost_estimate=pl.CostEstimate(
                flops=500_000 * weight, bytes_accessed=1_500_000 * weight, transcendentals=0
            ),
        )(*operands)

    main_ko, main_kx, main_so, main_sx, over_ko, over_kx, over_s = front(adjoint, flux_terms)

    other_core = [(i, i ^ 1) for i in range(insts)]
    other_chip = [(i, i ^ 2) for i in range(insts)]
    over_r = lax.ppermute(over_s, "inst", other_core)
    main_r = lax.ppermute(main_sx, "inst", other_core)
    [coefs] = on_chip(
        coefs_kernel, [(1, block, depth)],
        over_kx, stiffness, normals.transpose(0, 2, 1), design_map.T,
    )
    coefs_r = lax.ppermute(coefs, "inst", other_core)
    main_near = lax.ppermute(main_so, "inst", other_core)
    over_x = jnp.concatenate([over_kx + over_r[: FACE + 1], coefs + coefs_r])
    over_far = lax.ppermute(over_x, "inst", other_chip)
    [main_x] = on_chip(add_kernel, [main_kx.shape], main_kx, main_r, over_far)
    main_far = lax.ppermute(main_x, "inst", other_chip)

    halo = (OVER + 1, block, depth)
    to_inside, to_across, wall = on_chip(
        over_kernel, [halo, halo, (2, block, depth)], over_ko, over_r, over_x, over_far, main_x
    )
    inside = [(i, i ^ 1) for i in range(spaces)]
    across = [(i, ((i + 1) ^ 1) - 1) for i in range(1, spaces - 1)]
    from_inside = lax.ppermute(to_inside, "space", inside)
    from_across = lax.ppermute(to_across, "space", across)

    total = DV_DEV * insts * spaces
    [share] = on_chip(
        functools.partial(design_kernel, scale, rows), [(1, total)],
        wall, from_inside, from_across,
    )
    bits = spaces.bit_length() - 1
    groups = [(0,)] * (bits % 2) + [(b, b + 1) for b in range(bits % 2, bits, 2)]
    for group in groups:
        steps = [
            sum(1 << b for b, one in zip(group, ones) if one)
            for ones in itertools.product((0, 1), repeat=len(group))
        ][1:]
        others = [
            lax.ppermute(share, "space", [(i, i ^ step) for i in range(spaces)])
            for step in steps
        ]
        share = functools.reduce(jnp.add, others, share)
    mine = (inst * spaces + space) * DV_DEV
    design_grad = lax.dynamic_slice(share, (0, mine), (1, DV_DEV)).reshape(DV_DEV)

    [mesh_adjoint] = on_chip(
        functools.partial(last_kernel, scale), [(3, rows, block, depth)],
        main_ko, main_near, main_far, from_inside, from_across, stiffness,
    )
    return (mesh_adjoint, design_grad)


def solution(mesh):
    in_specs = (
        P("inst", None, "space", None, None),
        P("inst", None, None, "space", None, None),
        P("space", "inst", None),
        P(None, "space", "inst"),
        P("space", "inst"),
    )
    out_specs = (P(None, "space", "inst", None), P(("inst", "space")))
    return jax.shard_map(
        per_device, mesh=mesh, in_specs=in_specs, out_specs=out_specs, check_vma=False
    )
```

```python
import functools
import jax
import jax.numpy as jnp
from jax import lax
from jax.experimental import pallas as pl
from jax.experimental.pallas import tpu as pltpu
from jax.sharding import PartitionSpec as P

DIAG = 6.5
DV_DEV = 8
REACH = 3
PAD = REACH + 1
CHUNK = 4
REACHES = (3, 2, 2)
LOW_AT = (0, 3, 5)
OVER = 7
FACE = 2 * OVER
GROUP = 64
FACE_AT = (REACH, 24, 44)


def shifted_rows(tiles, top, bottom):
    down = [pltpu.roll(t, 1, 0) for t in tiles]
    up = [pltpu.roll(t, 7, 0) for t in tiles]
    zero = jnp.zeros_like(tiles[0])
    down = [jnp.where(top, p, n) for p, n in zip([zero] + down[:-1], down)]
    up = [jnp.where(bottom, n, p) for p, n in zip(up, up[1:] + [zero])]
    return down, up


def front_kernel(
    adj_hbm, flux_hbm,
    main_ko, main_kx, main_so, main_sx, over_ko, over_kx, over_s,
    adj, flux, work, metric, plane, side, band, stack, along, adj_sems, flux_sems,
):
    kinds, variables, rows, width, depth = adj.shape
    chunks = rows // CHUNK
    tiles = width // 8
    inst, space = lax.axis_index("inst"), lax.axis_index("space")
    low_open = jnp.where(space > 0, 1.0, 0.0)
    high_open = jnp.where(space < lax.axis_size("space") - 1, 1.0, 0.0)

    def adj_copy(i):
        part = pl.ds(i * CHUNK, CHUNK)
        return pltpu.make_async_copy(
            adj_hbm.at[:, :, part], adj.at[:, :, part], adj_sems.at[i]
        )

    def flux_copy(i):
        part = pl.ds(i * CHUNK, CHUNK)
        return pltpu.make_async_copy(
            flux_hbm.at[:, :, :, part], flux.at[:, :, :, part], flux_sems.at[i]
        )

    for i in range(chunks):
        adj_copy(i).start()
        flux_copy(i).start()

    near = jnp.abs(
        lax.broadcasted_iota(jnp.int32, (depth, depth), 0)
        - lax.broadcasted_iota(jnp.int32, (depth, depth), 1)
    )
    lane = lax.broadcasted_iota(jnp.int32, (depth, depth), 1)
    ends = jnp.where((lane == 0) | (lane == depth - 1), 1.0, 2.0)
    once = jnp.where(near == 1, 1.0, 0.0).astype(jnp.bfloat16)
    twice = jnp.where(near == 0, ends, jnp.where(near == 2, 1.0, 0.0)).astype(jnp.bfloat16)
    for half in (slice(0, depth), slice(depth, 2 * depth)):
        band[half, :depth] = once
        band[half, depth:] = twice
    zero = jnp.zeros((width, depth), jnp.float32)
    for d in range(3):
        for x in (-2, -1, rows, rows + 1):
            metric[d, x + PAD] = zero
            side[d, x + PAD] = zero
            plane[d, x + PAD] = zero
    for x in (-2, -1, rows, rows + 1):
        work[0, x + PAD] = zero

    row = lax.broadcasted_iota(jnp.int32, (8, depth), 0)
    top, bottom = row == 0, row == 7
    column = lax.broadcasted_iota(jnp.int32, (8, depth), 1)
    first, last = column == 0, column == depth - 1

    def weigh(x):
        for h in range(width // 16):
            part = slice(16 * h, 16 * h + 16)
            sums = [jnp.zeros((16, depth), jnp.float32) for _ in range(3)]
            for k in range(kinds):
                for v in range(variables):
                    a = adj[k, v, x, part].astype(jnp.float32)
                    for d in range(3):
                        sums[d] = sums[d] + a * flux[k, v, d, x, part].astype(jnp.float32)
            for d in range(3):
                work[d, x + PAD, part] = sums[d]

    def tile(t):
        return slice(8 * t, 8 * t + 8)

    def planes(slabs):
        count = len(slabs) * width
        for s, (d, x) in enumerate(slabs):
            r = x + PAD
            here = [work[d, r, tile(t)] for t in range(tiles)]
            if d == 0:
                open_ = jnp.where(x < 0, low_open, jnp.where(x >= rows, high_open, 1.0))
                low = [work[0, r - 1, tile(t)] for t in range(tiles)]
                high = [work[0, r + 1, tile(t)] for t in range(tiles)]
                m = [(h + 0.5 * (p - n)) * open_ for h, p, n in zip(here, low, high)]
            elif d == 1:
                low, high = shifted_rows(here, top, bottom)
                m = [h + 0.5 * (p - n) for h, p, n in zip(here, low, high)]
            else:
                m = [
                    h + 0.5 * (
                        jnp.where(first, 0.0, pltpu.roll(h, 1, 1))
                        - jnp.where(last, 0.0, pltpu.roll(h, depth - 1, 1))
                    )
                    for h in here
                ]
            for t in range(tiles):
                metric[d, r, tile(t)] = m[t]
            for t in range(0, tiles, 2):
                both = jnp.concatenate(m[t : t + 2], axis=0)
                rounded = both.astype(jnp.bfloat16)
                part = slice(s * width + 8 * t, s * width + 8 * t + 16)
                stack[part, :depth] = rounded
                stack[part, depth:] = (both - rounded.astype(jnp.float32)).astype(jnp.bfloat16)
        along[:count] = jnp.dot(stack[:count], band[...], preferred_element_type=jnp.float32)
        for s, (d, x) in enumerate(slabs):
            r = x + PAD
            at = s * width
            m = [metric[d, r, tile(t)] for t in range(tiles)]
            along_1 = [along[at + 8 * t : at + 8 * t + 8, :depth] for t in range(tiles)]
            along_2 = [along[at + 8 * t : at + 8 * t + 8, depth:] for t in range(tiles)]
            low, high = shifted_rows(m, top, bottom)
            once = [(p + n) + q for p, n, q in zip(low, high, along_1)]
            low, high = shifted_rows([o + q for o, q in zip(once, along_1)], top, bottom)
            returns = 2.0 - jnp.where(
                x == 0, 1.0 - low_open, jnp.where(x == rows - 1, 1.0 - high_open, 0.0)
            )
            weight = DIAG * DIAG + returns
            for t in range(tiles):
                side[d, r, tile(t)] = DIAG * m[t] + (once[t] + once[t])
                twice = (low[t] + high[t]) + along_2[t]
                plane[d, r, tile(t)] = weight * m[t] + DIAG * once[t] + twice

    def settle(i, extra):
        planes(
            [(1, i * CHUNK + j) for j in range(CHUNK)]
            + [(2, i * CHUNK + j) for j in range(CHUNK)]
            + [(0, i * CHUNK + j - 1) for j in range(CHUNK + extra)]
        )

    def arrive(i):
        adj_copy(i).wait()
        flux_copy(i).wait()

    arrive(0)
    for j in range(CHUNK):
        weigh(j)

    def stage(i, _):
        arrive(i)
        settle(i - 1, 0)
        for j in range(CHUNK):
            weigh(i * CHUNK + j)
        return 0

    lax.fori_loop(1, chunks, stage, 0)
    settle(chunks - 1, 2)

    def put(refs, index, place, total, face):
        for j, ref, shift in zip((0, 2, 1, 3), refs, (0, 0, FACE + 1, 0)):
            b = inst ^ j
            at = pl.multiple_of(8 * b, 8)
            value = total(pl.ds(at, 8))
            if ref is over_s:
                ref[index + shift] = value
            else:
                ref[index] = value
            face = jnp.where(column == GROUP * b + place, value[:, 0:1], face)
        return face

    main_refs = (main_ko, main_kx, main_so, main_sx)
    over_refs = (over_ko, over_kx, over_s, over_s)

    def reached(d, x, part):
        r = x + PAD
        first, last = (PAD - 1, PAD + rows) if d == 0 else (PAD, PAD + rows - 1)
        terms = (
            [plane[d, r, part]] * (first <= r <= last)
            + [side[d, s, part] for s in (r - 1, r + 1) if first <= s <= last]
            + [metric[d, s, part] for s in (r - 2, r + 2) if first <= s <= last]
        )
        return functools.reduce(jnp.add, terms)

    face = jnp.zeros((8, depth), jnp.float32)
    for d in range(3):
        for x in range(-REACHES[d], 0):
            face = put(
                over_refs, LOW_AT[d] + x + REACHES[d], FACE_AT[d] + x,
                functools.partial(reached, d, x), face,
            )
        for x in range(rows, rows + REACHES[d]):
            face = put(
                over_refs, OVER + LOW_AT[d] + x - rows, FACE_AT[d] + x,
                functools.partial(reached, d, x), face,
            )

    def inner(x, face):
        r = x + PAD
        for d in range(3):

            def total(part):
                value = plane[d, r, part] + (side[d, r - 1, part] + side[d, r + 1, part])
                return value + (metric[d, r - 2, part] + metric[d, r + 2, part])

            face = put(main_refs, (d, x), FACE_AT[d] + x, total, face)
        return face

    face = lax.fori_loop(0, rows, inner, face, unroll=2)
    over_kx[FACE] = face
    over_s[FACE] = face


def front(adjoint, flux_terms):
    kinds, variables, rows, width, depth = adjoint.shape
    f32 = jnp.float32
    block = width // 4
    main = jax.ShapeDtypeStruct((3, rows, block, depth), f32)
    vmem = pl.BlockSpec(memory_space=pltpu.VMEM)
    hbm = pl.BlockSpec(memory_space=pltpu.HBM)
    padded = (3, rows + 2 * PAD, width, depth)
    most = (3 * CHUNK + 2) * width
    over_rows = (2 * OVER, FACE + 1, FACE + 1 + 2 * OVER)
    return pl.pallas_call(
        front_kernel,
        out_shape=[main] * 4
        + [jax.ShapeDtypeStruct((count, block, depth), f32) for count in over_rows],
        in_specs=[hbm] * 2,
        out_specs=[vmem] * 7,
        scratch_shapes=[
            pltpu.VMEM(adjoint.shape, adjoint.dtype),
            pltpu.VMEM(flux_terms.shape, flux_terms.dtype),
            pltpu.VMEM(padded, f32),
            pltpu.VMEM(padded, f32),
            pltpu.VMEM(padded, f32),
            pltpu.VMEM(padded, f32),
            pltpu.VMEM((2 * depth, 2 * depth), jnp.bfloat16),
            pltpu.VMEM((most, 2 * depth), jnp.bfloat16),
            pltpu.VMEM((most, 2 * depth), f32),
            pltpu.SemaphoreType.DMA((rows // CHUNK,)),
            pltpu.SemaphoreType.DMA((rows // CHUNK,)),
        ],
        compiler_params=pltpu.CompilerParams(vmem_limit_bytes=51 * 2**20),
        cost_estimate=pl.CostEstimate(
            flops=60_000_000, bytes_accessed=13_000_000, transcendentals=0
        ),
    )(adjoint, flux_terms)


def coefs_kernel(after, stiffness, normals, ids, out):
    del after
    rows, block, depth = stiffness.shape
    column = lax.broadcasted_iota(jnp.int32, (block, depth), 1)
    own = GROUP * lax.axis_index("inst")
    coefs = jnp.zeros((block, depth), jnp.float32)
    for x in range(rows):
        inverse = 1.0 / stiffness[x, :, 0:1]
        for d in range(3):
            here = normals[d, :, x : x + 1] * inverse
            coefs = jnp.where(column == own + d * rows + x, here, coefs)
        here = ids[:, x : x + 1].astype(jnp.float32)
        coefs = jnp.where(column == own + 3 * rows + x, here, coefs)
    out[0] = coefs


def add_kernel(keep, near, after, out):
    del after
    for d in range(out.shape[0]):
        for x in range(out.shape[1]):
            out[d, x] = keep[d, x] + near[d, x]


def over_kernel(keep, near, first, far, main, inside, across, wall):
    del main
    even = lax.axis_index("space") % 2 == 0
    for i in range(OVER):
        low = keep[i] + near[FACE + 1 + i] + far[i]
        high = keep[OVER + i] + near[FACE + 1 + OVER + i] + far[OVER + i]
        inside[i] = jnp.where(even, high, low)
        across[i] = jnp.where(even, low, high)
    face = first[FACE] + far[FACE]
    inside[OVER] = face
    across[OVER] = face
    wall[0] = face
    wall[1] = first[FACE + 1] + far[FACE + 1]


def design_kernel(scale, rows, wall, from_inside, from_across, share):
    block, depth = wall.shape[1:]
    even = lax.axis_index("space") % 2 == 0
    column = lax.broadcasted_iota(jnp.int32, (block, depth), 1) % GROUP
    face, coefs = wall[0], wall[1]
    inside, across = from_inside[OVER], from_across[OVER]
    from_high = pltpu.roll(jnp.where(even, inside, across), rows, 1)
    from_low = pltpu.roll(jnp.where(even, across, inside), depth - rows, 1)
    surface = jnp.zeros((block, depth), jnp.float32)
    for d in range(3):
        at, reach = FACE_AT[d], REACHES[d]
        whole = (
            face
            + jnp.where((column >= at) & (column < at + reach), from_low, 0.0)
            + jnp.where((column >= at + rows - reach) & (column < at + rows), from_high, 0.0)
        )
        turned = pltpu.roll(coefs, depth - d * rows, 1) if d else coefs
        surface = surface + pltpu.roll(whole, depth - at, 1) * turned
    ids = pltpu.roll(coefs, depth - 3 * rows, 1).astype(jnp.int32)
    spaces, part = share.shape
    insts = part // DV_DEV
    row = ids // DV_DEV
    ids = (row % spaces) * part + (row // spaces) * DV_DEV + ids % DV_DEV
    slots = lax.broadcasted_iota(jnp.int32, (block, spaces * part), 1)
    tally = jnp.zeros((block, spaces * part), jnp.float32)
    for group in range(0, insts * GROUP, GROUP):
        for x in range(group, group + rows):
            tally = tally + jnp.where(slots == ids[:, x : x + 1], surface[:, x : x + 1], 0.0)
    sums = jnp.sum(tally, axis=0, keepdims=True) * scale
    for s in range(spaces):
        share[s : s + 1, :] = sums[:, s * part : (s + 1) * part]


def last_kernel(scale, keep, near, far, from_inside, from_across, stiffness, out):
    rows = keep.shape[1]
    even = lax.axis_index("space") % 2 == 0
    for x in range(rows):
        inverse = scale / stiffness[x]
        for d in range(3):
            value = keep[d, x] + near[d, x] + far[d, x]
            if x < REACHES[d]:
                at = LOW_AT[d] + x
                value = value + jnp.where(even, from_across[at], from_inside[at])
            if x >= rows - REACHES[d]:
                at = LOW_AT[d] + x - rows + REACHES[d]
                value = value + jnp.where(even, from_inside[at], from_across[at])
            out[d, x] = value * inverse


def per_device(adjoint, flux_terms, stiffness, normals, design_map):
    insts, spaces = lax.axis_size("inst"), lax.axis_size("space")
    inst, space = lax.axis_index("inst"), lax.axis_index("space")
    rows, block, depth = stiffness.shape
    scale = 1.0 / (DIAG**3 * adjoint.shape[0] * insts)

    vmem = pl.BlockSpec(memory_space=pltpu.VMEM)

    def on_chip(kernel, shapes, *operands, weight=1):
        out = [jax.ShapeDtypeStruct(shape, jnp.float32) for shape in shapes]
        return pl.pallas_call(
            kernel,
            out_shape=out,
            in_specs=[vmem] * len(operands),
            out_specs=[vmem] * len(out),
            compiler_params=pltpu.CompilerParams(vmem_limit_bytes=4 * 2**20),
            cost_estimate=pl.CostEstimate(
                flops=500_000 * weight, bytes_accessed=1_500_000 * weight, transcendentals=0
            ),
        )(*operands)

    main_ko, main_kx, main_so, main_sx, over_ko, over_kx, over_s = front(adjoint, flux_terms)

    other_core = [(i, i ^ 1) for i in range(insts)]
    other_chip = [(i, i ^ 2) for i in range(insts)]
    over_r = lax.ppermute(over_s, "inst", other_core)
    main_r = lax.ppermute(main_sx, "inst", other_core)
    [coefs] = on_chip(
        coefs_kernel, [(1, block, depth)],
        over_kx, stiffness, normals.transpose(0, 2, 1), design_map.T,
    )
    coefs_r = lax.ppermute(coefs, "inst", other_core)
    main_near = lax.ppermute(main_so, "inst", other_core)
    over_x = jnp.concatenate([over_kx + over_r[: FACE + 1], coefs + coefs_r])
    over_far = lax.ppermute(over_x, "inst", other_chip)
    [main_x] = on_chip(add_kernel, [main_kx.shape], main_kx, main_r, over_far)
    main_far = lax.ppermute(main_x, "inst", other_chip)

    halo = (OVER + 1, block, depth)
    to_inside, to_across, wall = on_chip(
        over_kernel, [halo, halo, (2, block, depth)], over_ko, over_r, over_x, over_far, main_x
    )
    inside = [(i, i ^ 1) for i in range(spaces)]
    across = [(i, ((i + 1) ^ 1) - 1) for i in range(1, spaces - 1)]
    from_inside = lax.ppermute(to_inside, "space", inside)
    from_across = lax.ppermute(to_across, "space", across)

    [share] = on_chip(
        functools.partial(design_kernel, scale, rows), [(spaces, DV_DEV * insts)],
        wall, from_inside, from_across,
    )
    shares = lax.all_to_all(share, "space", 0, 0, tiled=True)
    mine = jnp.sum(shares, axis=0)
    design_grad = lax.dynamic_slice(mine, (inst * DV_DEV,), (DV_DEV,))
    [mesh_adjoint] = on_chip(
        functools.partial(last_kernel, scale), [(3, rows, block, depth)],
        main_ko, main_near, main_far, from_inside, from_across, stiffness,
    )
    return (mesh_adjoint, design_grad)


def solution(mesh):
    in_specs = (
        P("inst", None, "space", None, None),
        P("inst", None, None, "space", None, None),
        P("space", "inst", None),
        P(None, "space", "inst"),
        P("space", "inst"),
    )
    out_specs = (P(None, "space", "inst", None), P(("inst", "space")))
    return jax.shard_map(
        per_device, mesh=mesh, in_specs=in_specs, out_specs=out_specs, check_vma=False
    )
```

```python
import functools
import jax
import jax.numpy as jnp
from jax import lax
from jax.experimental import pallas as pl
from jax.experimental.pallas import tpu as pltpu
from jax.sharding import PartitionSpec as P

DIAG = 6.5
DV_DEV = 8
REACH = 3
PAD = REACH + 1
CHUNK = 4
REACHES = (3, 2, 2)
LOW_AT = (0, 3, 5)
OVER = 7
FACE = 2 * OVER
GROUP = 64
FACE_AT = (REACH, 24, 44)


def shifted_rows(tiles, top, bottom):
    down = [pltpu.roll(t, 1, 0) for t in tiles]
    up = [pltpu.roll(t, 7, 0) for t in tiles]
    zero = jnp.zeros_like(tiles[0])
    down = [jnp.where(top, p, n) for p, n in zip([zero] + down[:-1], down)]
    up = [jnp.where(bottom, n, p) for p, n in zip(up, up[1:] + [zero])]
    return down, up


def front_kernel(
    adj_hbm, flux_hbm,
    main_ko, main_kx, main_so, main_sx, over_ko, over_kx, over_s, wall,
    adj, flux, work, metric, plane, side, band, stack, along, adj_sems, flux_sems,
):
    kinds, variables, rows, width, depth = adj.shape
    chunks = rows // CHUNK
    tiles = width // 8
    inst, space = lax.axis_index("inst"), lax.axis_index("space")
    low_open = jnp.where(space > 0, 1.0, 0.0)
    high_open = jnp.where(space < lax.axis_size("space") - 1, 1.0, 0.0)

    def adj_copy(i):
        part = pl.ds(i * CHUNK, CHUNK)
        return pltpu.make_async_copy(
            adj_hbm.at[:, :, part], adj.at[:, :, part], adj_sems.at[i]
        )

    def flux_copy(i):
        part = pl.ds(i * CHUNK, CHUNK)
        return pltpu.make_async_copy(
            flux_hbm.at[:, :, :, part], flux.at[:, :, :, part], flux_sems.at[i]
        )

    for i in range(chunks):
        adj_copy(i).start()
        flux_copy(i).start()

    near = jnp.abs(
        lax.broadcasted_iota(jnp.int32, (depth, depth), 0)
        - lax.broadcasted_iota(jnp.int32, (depth, depth), 1)
    )
    lane = lax.broadcasted_iota(jnp.int32, (depth, depth), 1)
    ends = jnp.where((lane == 0) | (lane == depth - 1), 1.0, 2.0)
    once = jnp.where(near == 1, 1.0, 0.0).astype(jnp.bfloat16)
    twice = jnp.where(near == 0, ends, jnp.where(near == 2, 1.0, 0.0)).astype(jnp.bfloat16)
    for half in (slice(0, depth), slice(depth, 2 * depth)):
        band[half, :depth] = once
        band[half, depth:] = twice
    zero = jnp.zeros((width, depth), jnp.float32)
    for d in range(3):
        for x in (-2, -1, rows, rows + 1):
            metric[d, x + PAD] = zero
            side[d, x + PAD] = zero
            plane[d, x + PAD] = zero
    for x in (-2, -1, rows, rows + 1):
        work[0, x + PAD] = zero

    row = lax.broadcasted_iota(jnp.int32, (8, depth), 0)
    top, bottom = row == 0, row == 7
    column = lax.broadcasted_iota(jnp.int32, (8, depth), 1)
    first, last = column == 0, column == depth - 1

    def weigh(x):
        for h in range(width // 16):
            part = slice(16 * h, 16 * h + 16)
            sums = [jnp.zeros((16, depth), jnp.float32) for _ in range(3)]
            for k in range(kinds):
                for v in range(variables):
                    a = adj[k, v, x, part].astype(jnp.float32)
                    for d in range(3):
                        sums[d] = sums[d] + a * flux[k, v, d, x, part].astype(jnp.float32)
            for d in range(3):
                work[d, x + PAD, part] = sums[d]

    def tile(t):
        return slice(8 * t, 8 * t + 8)

    def planes(slabs):
        count = len(slabs) * width
        for s, (d, x) in enumerate(slabs):
            r = x + PAD
            here = [work[d, r, tile(t)] for t in range(tiles)]
            if d == 0:
                open_ = jnp.where(x < 0, low_open, jnp.where(x >= rows, high_open, 1.0))
                low = [work[0, r - 1, tile(t)] for t in range(tiles)]
                high = [work[0, r + 1, tile(t)] for t in range(tiles)]
                m = [(h + 0.5 * (p - n)) * open_ for h, p, n in zip(here, low, high)]
            elif d == 1:
                low, high = shifted_rows(here, top, bottom)
                m = [h + 0.5 * (p - n) for h, p, n in zip(here, low, high)]
            else:
                m = [
                    h + 0.5 * (
                        jnp.where(first, 0.0, pltpu.roll(h, 1, 1))
                        - jnp.where(last, 0.0, pltpu.roll(h, depth - 1, 1))
                    )
                    for h in here
                ]
            for t in range(tiles):
                metric[d, r, tile(t)] = m[t]
            for t in range(0, tiles, 2):
                both = jnp.concatenate(m[t : t + 2], axis=0)
                rounded = both.astype(jnp.bfloat16)
                part = slice(s * width + 8 * t, s * width + 8 * t + 16)
                stack[part, :depth] = rounded
                stack[part, depth:] = (both - rounded.astype(jnp.float32)).astype(jnp.bfloat16)
        along[:count] = jnp.dot(stack[:count], band[...], preferred_element_type=jnp.float32)
        for s, (d, x) in enumerate(slabs):
            r = x + PAD
            at = s * width
            m = [metric[d, r, tile(t)] for t in range(tiles)]
            along_1 = [along[at + 8 * t : at + 8 * t + 8, :depth] for t in range(tiles)]
            along_2 = [along[at + 8 * t : at + 8 * t + 8, depth:] for t in range(tiles)]
            low, high = shifted_rows(m, top, bottom)
            once = [(p + n) + q for p, n, q in zip(low, high, along_1)]
            low, high = shifted_rows([o + q for o, q in zip(once, along_1)], top, bottom)
            returns = 2.0 - jnp.where(
                x == 0, 1.0 - low_open, jnp.where(x == rows - 1, 1.0 - high_open, 0.0)
            )
            weight = DIAG * DIAG + returns
            for t in range(tiles):
                side[d, r, tile(t)] = DIAG * m[t] + (once[t] + once[t])
                twice = (low[t] + high[t]) + along_2[t]
                plane[d, r, tile(t)] = weight * m[t] + DIAG * once[t] + twice

    def settle(i, extra):
        planes(
            [(1, i * CHUNK + j) for j in range(CHUNK)]
            + [(2, i * CHUNK + j) for j in range(CHUNK)]
            + [(0, i * CHUNK + j - 1) for j in range(CHUNK + extra)]
        )

    def arrive(i):
        adj_copy(i).wait()
        flux_copy(i).wait()

    arrive(0)
    for j in range(CHUNK):
        weigh(j)

    def stage(i, _):
        arrive(i)
        settle(i - 1, 0)
        for j in range(CHUNK):
            weigh(i * CHUNK + j)
        return 0

    lax.fori_loop(1, chunks, stage, 0)
    settle(chunks - 1, 2)

    def put(refs, index, place, total, face):
        for j, ref, shift in zip((0, 2, 1, 3), refs, (0, 0, 2 * OVER, 0)):
            b = inst ^ j
            at = pl.multiple_of(8 * b, 8)
            value = total(pl.ds(at, 8))
            if ref is over_s:
                ref[index + shift] = value
            else:
                ref[index] = value
            face = jnp.where(column == GROUP * b + place, value[:, 0:1], face)
        return face

    main_refs = (main_ko, main_kx, main_so, main_sx)
    over_refs = (over_ko, over_kx, over_s, over_s)

    def reached(d, x, part):
        r = x + PAD
        first, last = (PAD - 1, PAD + rows) if d == 0 else (PAD, PAD + rows - 1)
        terms = (
            [plane[d, r, part]] * (first <= r <= last)
            + [side[d, s, part] for s in (r - 1, r + 1) if first <= s <= last]
            + [metric[d, s, part] for s in (r - 2, r + 2) if first <= s <= last]
        )
        return functools.reduce(jnp.add, terms)

    face = jnp.zeros((8, depth), jnp.float32)
    for d in range(3):
        for x in range(-REACHES[d], 0):
            face = put(
                over_refs, LOW_AT[d] + x + REACHES[d], FACE_AT[d] + x,
                functools.partial(reached, d, x), face,
            )
        for x in range(rows, rows + REACHES[d]):
            face = put(
                over_refs, OVER + LOW_AT[d] + x - rows, FACE_AT[d] + x,
                functools.partial(reached, d, x), face,
            )

    def inner(x, face):
        r = x + PAD
        for d in range(3):

            def total(part):
                value = plane[d, r, part] + (side[d, r - 1, part] + side[d, r + 1, part])
                return value + (metric[d, r - 2, part] + metric[d, r + 2, part])

            face = put(main_refs, (d, x), FACE_AT[d] + x, total, face)
        return face

    face = lax.fori_loop(0, rows, inner, face, unroll=2)
    wall[0] = face


def front(adjoint, flux_terms):
    kinds, variables, rows, width, depth = adjoint.shape
    f32 = jnp.float32
    block = width // 4
    main = jax.ShapeDtypeStruct((3, rows, block, depth), f32)
    vmem = pl.BlockSpec(memory_space=pltpu.VMEM)
    hbm = pl.BlockSpec(memory_space=pltpu.HBM)
    padded = (3, rows + 2 * PAD, width, depth)
    most = (3 * CHUNK + 2) * width
    over_rows = (2 * OVER, 2 * OVER, 4 * OVER, 1)
    return pl.pallas_call(
        front_kernel,
        out_shape=[main] * 4
        + [jax.ShapeDtypeStruct((count, block, depth), f32) for count in over_rows],
        in_specs=[hbm] * 2,
        out_specs=[vmem] * 8,
        scratch_shapes=[
            pltpu.VMEM(adjoint.shape, adjoint.dtype),
            pltpu.VMEM(flux_terms.shape, flux_terms.dtype),
            pltpu.VMEM(padded, f32),
            pltpu.VMEM(padded, f32),
            pltpu.VMEM(padded, f32),
            pltpu.VMEM(padded, f32),
            pltpu.VMEM((2 * depth, 2 * depth), jnp.bfloat16),
            pltpu.VMEM((most, 2 * depth), jnp.bfloat16),
            pltpu.VMEM((most, 2 * depth), f32),
            pltpu.SemaphoreType.DMA((rows // CHUNK,)),
            pltpu.SemaphoreType.DMA((rows // CHUNK,)),
        ],
        compiler_params=pltpu.CompilerParams(vmem_limit_bytes=51 * 2**20),
        cost_estimate=pl.CostEstimate(
            flops=60_000_000, bytes_accessed=13_000_000, transcendentals=0
        ),
    )(adjoint, flux_terms)


def coefs_kernel(after, stiffness, normals, ids, out):
    del after
    rows, block, depth = stiffness.shape
    column = lax.broadcasted_iota(jnp.int32, (block, depth), 1)
    own = GROUP * lax.axis_index("inst")
    coefs = jnp.zeros((block, depth), jnp.float32)
    for x in range(rows):
        inverse = 1.0 / stiffness[x, :, 0:1]
        for d in range(3):
            here = normals[d, :, x : x + 1] * inverse
            coefs = jnp.where(column == own + d * rows + x, here, coefs)
        here = ids[:, x : x + 1].astype(jnp.float32)
        coefs = jnp.where(column == own + 3 * rows + x, here, coefs)
    out[0] = coefs


def add_kernel(keep, near, after, out):
    del after
    for d in range(out.shape[0]):
        for x in range(out.shape[1]):
            out[d, x] = keep[d, x] + near[d, x]


def near_kernel(over, over_near, face, face_near, coefs, coefs_near, out):
    for i in range(2 * OVER):
        out[i] = over[i] + over_near[i]
    out[FACE] = face[0] + face_near[0]
    out[FACE + 1] = coefs[0] + coefs_near[0]


def over_low(keep, over_near, far, i):
    return keep[i] + over_near[2 * OVER + i] + far[i]


def over_high(keep, over_near, far, i):
    return keep[OVER + i] + over_near[3 * OVER + i] + far[OVER + i]


def across_kernel(keep, over_near, near, far, out):
    even = lax.axis_index("space") % 2 == 0
    for i in range(OVER):
        low, high = (f(keep, over_near, far, i) for f in (over_low, over_high))
        out[i] = jnp.where(even, low, high)
    out[OVER] = near[FACE] + far[FACE]


def from_neighbour(face, other, rows, low):
    depth = face.shape[1]
    column = lax.broadcasted_iota(jnp.int32, face.shape, 1) % GROUP
    at_low = functools.reduce(
        jnp.logical_or,
        [(column >= at) & (column < at + n) for at, n in zip(FACE_AT, REACHES)],
    )
    at_high = functools.reduce(
        jnp.logical_or,
        [
            (column >= at + rows - n) & (column < at + rows)
            for at, n in zip(FACE_AT, REACHES)
        ],
    )
    given = jnp.where(
        low,
        jnp.where(at_low, pltpu.roll(other, depth - rows, 1), 0.0),
        jnp.where(at_high, pltpu.roll(other, rows, 1), 0.0),
    )
    return face + given


def inside_kernel(rows, spaces, keep, over_near, near, far, across, out):
    space = lax.axis_index("space")
    even = space % 2 == 0
    for i in range(OVER):
        low, high = (f(keep, over_near, far, i) for f in (over_low, over_high))
        out[i] = jnp.where(even, high, low)
    inner = (space > 0) & (space < spaces - 1)
    other = jnp.where(inner, across[OVER], 0.0)
    out[OVER] = from_neighbour(near[FACE] + far[FACE], other, rows, even)
    out[OVER + 1] = near[FACE + 1] + far[FACE + 1]


def design_kernel(scale, rows, spaces, own, other, share):
    block, depth = own.shape[1:]
    total = share.shape[1]
    even = lax.axis_index("space") % 2 == 0
    slots = lax.broadcasted_iota(jnp.int32, (block, total), 1)
    tally = jnp.zeros((block, total), jnp.float32)
    for one, two, low in ((own, other, ~even), (other, own, even)):
        whole = from_neighbour(one[OVER], two[OVER], rows, low)
        coefs = one[OVER + 1]
        surface = jnp.zeros((block, depth), jnp.float32)
        for d in range(3):
            turned = pltpu.roll(coefs, depth - d * rows, 1) if d else coefs
            surface = surface + pltpu.roll(whole, depth - FACE_AT[d], 1) * turned
        ids = pltpu.roll(coefs, depth - 3 * rows, 1).astype(jnp.int32)
        for group in range(0, depth, GROUP):
            for x in range(group, group + rows):
                tally = tally + jnp.where(
                    slots == ids[:, x : x + 1], surface[:, x : x + 1], 0.0
                )
    share[...] = jnp.sum(tally, axis=0, keepdims=True) * scale


def last_kernel(scale, spaces, keep, near, far, from_inside, from_across, stiffness, out):
    rows = keep.shape[1]
    space = lax.axis_index("space")
    even = space % 2 == 0
    inner = (space > 0) & (space < spaces - 1)
    for x in range(rows):
        inverse = scale / stiffness[x]
        for d in range(3):
            value = keep[d, x] + near[d, x] + far[d, x]
            for at, side in (
                (LOW_AT[d] + x, even if x < REACHES[d] else None),
                (LOW_AT[d] + x - rows + REACHES[d], ~even if x >= rows - REACHES[d] else None),
            ):
                if side is not None:
                    across = jnp.where(inner, from_across[at], 0.0)
                    value = value + jnp.where(side, across, from_inside[at])
            out[d, x] = value * inverse


def per_device(adjoint, flux_terms, stiffness, normals, design_map):
    insts, spaces = lax.axis_size("inst"), lax.axis_size("space")
    inst, space = lax.axis_index("inst"), lax.axis_index("space")
    rows, block, depth = stiffness.shape
    scale = 1.0 / (DIAG**3 * adjoint.shape[0] * insts)

    vmem = pl.BlockSpec(memory_space=pltpu.VMEM)

    def on_chip(kernel, shapes, *operands, weight=1):
        out = [jax.ShapeDtypeStruct(shape, jnp.float32) for shape in shapes]
        return pl.pallas_call(
            kernel,
            out_shape=out,
            in_specs=[vmem] * len(operands),
            out_specs=[vmem] * len(out),
            compiler_params=pltpu.CompilerParams(vmem_limit_bytes=4 * 2**20),
            cost_estimate=pl.CostEstimate(
                flops=500_000 * weight, bytes_accessed=1_500_000 * weight, transcendentals=0
            ),
        )(*operands)

    main_ko, main_kx, main_so, main_sx, over_ko, over_kx, over_s, face = front(
        adjoint, flux_terms
    )

    other_core = [(i, i ^ 1) for i in range(insts)]
    other_chip = [(i, i ^ 2) for i in range(insts)]
    inside = [(i, i ^ 1) for i in range(spaces)]
    across = [(i, min(max(((i + 1) ^ 1) - 1, 0), spaces - 1)) for i in range(spaces)]

    plane = (1, block, depth)
    face_r = lax.ppermute(face, "inst", other_core)
    [coefs] = on_chip(
        coefs_kernel, [plane], face, stiffness, normals.transpose(0, 2, 1), design_map.T
    )
    coefs_r = lax.ppermute(coefs, "inst", other_core)
    over_r = lax.ppermute(over_s, "inst", other_core)
    main_r = lax.ppermute(main_sx, "inst", other_core)
    main_near = lax.ppermute(main_so, "inst", other_core)
    [near] = on_chip(
        near_kernel, [(FACE + 2, block, depth)], over_kx, over_r, face, face_r, coefs, coefs_r
    )
    far = lax.ppermute(near, "inst", other_chip)
    [main_x] = on_chip(add_kernel, [main_kx.shape], main_kx, main_r, far)
    main_far = lax.ppermute(main_x, "inst", other_chip)

    [to_across] = on_chip(
        across_kernel, [(OVER + 1, block, depth)], over_ko, over_r, near, far
    )
    from_across = lax.ppermute(to_across, "space", across)
    [to_inside] = on_chip(
        functools.partial(inside_kernel, rows, spaces), [(OVER + 2, block, depth)],
        over_ko, over_r, near, far, from_across,
    )
    from_inside = lax.ppermute(to_inside, "space", inside)
    [share] = on_chip(
        functools.partial(design_kernel, scale, rows, spaces),
        [(1, DV_DEV * insts * spaces)],
        to_inside, from_inside,
    )
    step = 2
    while step < spaces:
        share = share + lax.ppermute(share, "space", [(i, i ^ step) for i in range(spaces)])
        step *= 2
    mine = (inst * spaces + space) * DV_DEV
    design_grad = lax.dynamic_slice(share, (0, mine), (1, DV_DEV)).reshape(DV_DEV)

    [mesh_adjoint] = on_chip(
        functools.partial(last_kernel, scale, spaces), [(3, rows, block, depth)],
        main_ko, main_near, main_far, from_inside, from_across, stiffness,
    )
    return (mesh_adjoint, design_grad)


def solution(mesh):
    in_specs = (
        P("inst", None, "space", None, None),
        P("inst", None, None, "space", None, None),
        P("space", "inst", None),
        P(None, "space", "inst"),
        P("space", "inst"),
    )
    out_specs = (P(None, "space", "inst", None), P(("inst", "space")))
    return jax.shard_map(
        per_device, mesh=mesh, in_specs=in_specs, out_specs=out_specs, check_vma=False
    )
```

```python
import functools
import jax
import jax.numpy as jnp
from jax import lax
from jax.experimental import pallas as pl
from jax.experimental.pallas import tpu as pltpu
from jax.sharding import PartitionSpec as P

DIAG = 6.5
DV_DEV = 8
REACH = 3
PAD = REACH + 1
CHUNK = 4
REACHES = (3, 2, 2)
LOW_AT = (0, 3, 5)
OVER = 7
FACE = 2 * OVER
GROUP = 64
FACE_AT = (REACH, 24, 44)


def shifted_rows(tiles, top, bottom):
    down = [pltpu.roll(t, 1, 0) for t in tiles]
    up = [pltpu.roll(t, 7, 0) for t in tiles]
    zero = jnp.zeros_like(tiles[0])
    down = [jnp.where(top, p, n) for p, n in zip([zero] + down[:-1], down)]
    up = [jnp.where(bottom, n, p) for p, n in zip(up, up[1:] + [zero])]
    return down, up


def front_kernel(
    adj_hbm, flux_hbm,
    main_ko, main_kx, main_so, main_sx, over_ko, over_kx, over_s, wall,
    adj, flux, work, metric, plane, side, band, stack, along, adj_sems, flux_sems,
):
    kinds, variables, rows, width, depth = adj.shape
    chunks = rows // CHUNK
    tiles = width // 8
    inst, space = lax.axis_index("inst"), lax.axis_index("space")
    low_open = jnp.where(space > 0, 1.0, 0.0)
    high_open = jnp.where(space < lax.axis_size("space") - 1, 1.0, 0.0)

    def adj_copy(i):
        part = pl.ds(i * CHUNK, CHUNK)
        return pltpu.make_async_copy(
            adj_hbm.at[:, :, part], adj.at[:, :, part], adj_sems.at[i]
        )

    def flux_copy(i):
        part = pl.ds(i * CHUNK, CHUNK)
        return pltpu.make_async_copy(
            flux_hbm.at[:, :, :, part], flux.at[:, :, :, part], flux_sems.at[i]
        )

    for i in range(chunks):
        adj_copy(i).start()
        flux_copy(i).start()

    near = jnp.abs(
        lax.broadcasted_iota(jnp.int32, (depth, depth), 0)
        - lax.broadcasted_iota(jnp.int32, (depth, depth), 1)
    )
    lane = lax.broadcasted_iota(jnp.int32, (depth, depth), 1)
    ends = jnp.where((lane == 0) | (lane == depth - 1), 1.0, 2.0)
    once = jnp.where(near == 1, 1.0, 0.0).astype(jnp.bfloat16)
    twice = jnp.where(near == 0, ends, jnp.where(near == 2, 1.0, 0.0)).astype(jnp.bfloat16)
    for half in (slice(0, depth), slice(depth, 2 * depth)):
        band[half, :depth] = once
        band[half, depth:] = twice
    zero = jnp.zeros((width, depth), jnp.float32)
    for d in range(3):
        for x in (-2, -1, rows, rows + 1):
            metric[d, x + PAD] = zero
            side[d, x + PAD] = zero
            plane[d, x + PAD] = zero
    for x in (-2, -1, rows, rows + 1):
        work[0, x + PAD] = zero

    row = lax.broadcasted_iota(jnp.int32, (8, depth), 0)
    top, bottom = row == 0, row == 7
    column = lax.broadcasted_iota(jnp.int32, (8, depth), 1)
    first, last = column == 0, column == depth - 1

    def weigh(x):
        for h in range(width // 16):
            part = slice(16 * h, 16 * h + 16)
            sums = [jnp.zeros((16, depth), jnp.float32) for _ in range(3)]
            for k in range(kinds):
                for v in range(variables):
                    a = adj[k, v, x, part].astype(jnp.float32)
                    for d in range(3):
                        sums[d] = sums[d] + a * flux[k, v, d, x, part].astype(jnp.float32)
            for d in range(3):
                work[d, x + PAD, part] = sums[d]

    def tile(t):
        return slice(8 * t, 8 * t + 8)

    def planes(slabs):
        count = len(slabs) * width
        for s, (d, x) in enumerate(slabs):
            r = x + PAD
            here = [work[d, r, tile(t)] for t in range(tiles)]
            if d == 0:
                open_ = jnp.where(x < 0, low_open, jnp.where(x >= rows, high_open, 1.0))
                low = [work[0, r - 1, tile(t)] for t in range(tiles)]
                high = [work[0, r + 1, tile(t)] for t in range(tiles)]
                m = [(h + 0.5 * (p - n)) * open_ for h, p, n in zip(here, low, high)]
            elif d == 1:
                low, high = shifted_rows(here, top, bottom)
                m = [h + 0.5 * (p - n) for h, p, n in zip(here, low, high)]
            else:
                m = [
                    h + 0.5 * (
                        jnp.where(first, 0.0, pltpu.roll(h, 1, 1))
                        - jnp.where(last, 0.0, pltpu.roll(h, depth - 1, 1))
                    )
                    for h in here
                ]
            for t in range(tiles):
                metric[d, r, tile(t)] = m[t]
            for t in range(0, tiles, 2):
                both = jnp.concatenate(m[t : t + 2], axis=0)
                rounded = both.astype(jnp.bfloat16)
                part = slice(s * width + 8 * t, s * width + 8 * t + 16)
                stack[part, :depth] = rounded
                stack[part, depth:] = (both - rounded.astype(jnp.float32)).astype(jnp.bfloat16)
        along[:count] = jnp.dot(stack[:count], band[...], preferred_element_type=jnp.float32)
        for s, (d, x) in enumerate(slabs):
            r = x + PAD
            at = s * width
            m = [metric[d, r, tile(t)] for t in range(tiles)]
            along_1 = [along[at + 8 * t : at + 8 * t + 8, :depth] for t in range(tiles)]
            along_2 = [along[at + 8 * t : at + 8 * t + 8, depth:] for t in range(tiles)]
            low, high = shifted_rows(m, top, bottom)
            once = [(p + n) + q for p, n, q in zip(low, high, along_1)]
            low, high = shifted_rows([o + q for o, q in zip(once, along_1)], top, bottom)
            returns = 2.0 - jnp.where(
                x == 0, 1.0 - low_open, jnp.where(x == rows - 1, 1.0 - high_open, 0.0)
            )
            weight = DIAG * DIAG + returns
            for t in range(tiles):
                side[d, r, tile(t)] = DIAG * m[t] + (once[t] + once[t])
                twice = (low[t] + high[t]) + along_2[t]
                plane[d, r, tile(t)] = weight * m[t] + DIAG * once[t] + twice

    def settle(i, extra):
        planes(
            [(1, i * CHUNK + j) for j in range(CHUNK)]
            + [(2, i * CHUNK + j) for j in range(CHUNK)]
            + [(0, i * CHUNK + j - 1) for j in range(CHUNK + extra)]
        )

    def arrive(i):
        adj_copy(i).wait()
        flux_copy(i).wait()

    arrive(0)
    for j in range(CHUNK):
        weigh(j)

    def stage(i, _):
        arrive(i)
        settle(i - 1, 0)
        for j in range(CHUNK):
            weigh(i * CHUNK + j)
        return 0

    lax.fori_loop(1, chunks, stage, 0)
    settle(chunks - 1, 2)

    def put(refs, index, place, total, face):
        for j, ref, shift in zip((0, 2, 1, 3), refs, (0, 0, 2 * OVER, 0)):
            b = inst ^ j
            at = pl.multiple_of(8 * b, 8)
            value = total(pl.ds(at, 8))
            if ref is over_s:
                ref[index + shift] = value
            else:
                ref[index] = value
            face = jnp.where(column == GROUP * b + place, value[:, 0:1], face)
        return face

    main_refs = (main_ko, main_kx, main_so, main_sx)
    over_refs = (over_ko, over_kx, over_s, over_s)

    def reached(d, x, part):
        r = x + PAD
        first, last = (PAD - 1, PAD + rows) if d == 0 else (PAD, PAD + rows - 1)
        terms = (
            [plane[d, r, part]] * (first <= r <= last)
            + [side[d, s, part] for s in (r - 1, r + 1) if first <= s <= last]
            + [metric[d, s, part] for s in (r - 2, r + 2) if first <= s <= last]
        )
        return functools.reduce(jnp.add, terms)

    face = jnp.zeros((8, depth), jnp.float32)
    for d in range(3):
        for x in range(-REACHES[d], 0):
            face = put(
                over_refs, LOW_AT[d] + x + REACHES[d], FACE_AT[d] + x,
                functools.partial(reached, d, x), face,
            )
        for x in range(rows, rows + REACHES[d]):
            face = put(
                over_refs, OVER + LOW_AT[d] + x - rows, FACE_AT[d] + x,
                functools.partial(reached, d, x), face,
            )

    def inner(x, face):
        r = x + PAD
        for d in range(3):

            def total(part):
                value = plane[d, r, part] + (side[d, r - 1, part] + side[d, r + 1, part])
                return value + (metric[d, r - 2, part] + metric[d, r + 2, part])

            face = put(main_refs, (d, x), FACE_AT[d] + x, total, face)
        return face

    face = lax.fori_loop(0, rows, inner, face, unroll=2)
    wall[0] = face


def front(adjoint, flux_terms):
    kinds, variables, rows, width, depth = adjoint.shape
    f32 = jnp.float32
    block = width // 4
    main = jax.ShapeDtypeStruct((3, rows, block, depth), f32)
    vmem = pl.BlockSpec(memory_space=pltpu.VMEM)
    hbm = pl.BlockSpec(memory_space=pltpu.HBM)
    padded = (3, rows + 2 * PAD, width, depth)
    most = (3 * CHUNK + 2) * width
    over_rows = (2 * OVER, 2 * OVER, 4 * OVER, 1)
    return pl.pallas_call(
        front_kernel,
        out_shape=[main] * 4
        + [jax.ShapeDtypeStruct((count, block, depth), f32) for count in over_rows],
        in_specs=[hbm] * 2,
        out_specs=[vmem] * 8,
        scratch_shapes=[
            pltpu.VMEM(adjoint.shape, adjoint.dtype),
            pltpu.VMEM(flux_terms.shape, flux_terms.dtype),
            pltpu.VMEM(padded, f32),
            pltpu.VMEM(padded, f32),
            pltpu.VMEM(padded, f32),
            pltpu.VMEM(padded, f32),
            pltpu.VMEM((2 * depth, 2 * depth), jnp.bfloat16),
            pltpu.VMEM((most, 2 * depth), jnp.bfloat16),
            pltpu.VMEM((most, 2 * depth), f32),
            pltpu.SemaphoreType.DMA((rows // CHUNK,)),
            pltpu.SemaphoreType.DMA((rows // CHUNK,)),
        ],
        compiler_params=pltpu.CompilerParams(vmem_limit_bytes=51 * 2**20),
        cost_estimate=pl.CostEstimate(
            flops=60_000_000, bytes_accessed=13_000_000, transcendentals=0
        ),
    )(adjoint, flux_terms)


def coefs_kernel(after, stiffness, normals, ids, out):
    del after
    rows, block, depth = stiffness.shape
    column = lax.broadcasted_iota(jnp.int32, (block, depth), 1)
    own = GROUP * lax.axis_index("inst")
    coefs = jnp.zeros((block, depth), jnp.float32)
    for x in range(rows):
        inverse = 1.0 / stiffness[x, :, 0:1]
        for d in range(3):
            here = normals[d, :, x : x + 1] * inverse
            coefs = jnp.where(column == own + d * rows + x, here, coefs)
        here = ids[:, x : x + 1].astype(jnp.float32)
        coefs = jnp.where(column == own + 3 * rows + x, here, coefs)
    out[0] = coefs


def add_kernel(keep, near, after, out):
    del after
    for d in range(out.shape[0]):
        for x in range(out.shape[1]):
            out[d, x] = keep[d, x] + near[d, x]


def near_kernel(over, over_near, face, face_near, coefs, coefs_near, out):
    for i in range(2 * OVER):
        out[i] = over[i] + over_near[i]
    out[FACE] = face[0] + face_near[0]
    out[FACE + 1] = coefs[0] + coefs_near[0]


def over_low(keep, over_near, far, i):
    return keep[i] + over_near[2 * OVER + i] + far[i]


def over_high(keep, over_near, far, i):
    return keep[OVER + i] + over_near[3 * OVER + i] + far[OVER + i]


def first_kernel(keep, over_near, near, far, out):
    even = lax.axis_index("space") % 2 == 0
    for i in range(OVER):
        low, high = (f(keep, over_near, far, i) for f in (over_low, over_high))
        out[i] = jnp.where(even, high, low)
        out[OVER + i] = jnp.where(even, low, high)
    out[2 * OVER] = near[FACE] + far[FACE]
    out[2 * OVER + 1] = near[FACE + 1] + far[FACE + 1]


def in_order(bit, own, other):
    upper = (lax.axis_index("space") >> bit) % 2 == 1
    count = 2 << bit
    at = own.shape[0] - count
    lows = [jnp.where(upper, other[at + i], own[at + i]) for i in range(count)]
    highs = [jnp.where(upper, own[at + i], other[at + i]) for i in range(count)]
    return lows + highs


def next_kernel(bit, own, other, out):
    at = OVER if bit == 0 else 0
    for i in range(OVER):
        out[i] = other[at + i]
    for i, value in enumerate(in_order(bit, own, other)):
        out[OVER + i] = value


def design_kernel(scale, rows, bit, own, other, out):
    planes = in_order(bit, own, other)
    faces, coefs = planes[::2], planes[1::2]
    spaces = len(faces)
    block, depth = faces[0].shape
    column = lax.broadcasted_iota(jnp.int32, (block, depth), 1) % GROUP
    at_low = functools.reduce(
        jnp.logical_or,
        [(column >= at) & (column < at + n) for at, n in zip(FACE_AT, REACHES)],
    )
    at_high = functools.reduce(
        jnp.logical_or,
        [
            (column >= at + rows - n) & (column < at + rows)
            for at, n in zip(FACE_AT, REACHES)
        ],
    )
    mine = (lax.axis_index("inst") * spaces + lax.axis_index("space")) * DV_DEV
    sums = [jnp.zeros((block, depth), jnp.float32) for _ in range(DV_DEV)]
    for s in range(spaces):
        whole = faces[s]
        if s > 0:
            whole = whole + jnp.where(at_low, pltpu.roll(faces[s - 1], depth - rows, 1), 0.0)
        if s < spaces - 1:
            whole = whole + jnp.where(at_high, pltpu.roll(faces[s + 1], rows, 1), 0.0)
        surface = jnp.zeros((block, depth), jnp.float32)
        for d in range(3):
            turned = pltpu.roll(coefs[s], depth - d * rows, 1) if d else coefs[s]
            surface = surface + pltpu.roll(whole, depth - FACE_AT[d], 1) * turned
        ids = pltpu.roll(coefs[s], depth - 3 * rows, 1).astype(jnp.int32) - mine
        ids = jnp.where(column < rows, ids, -1)
        for j in range(DV_DEV):
            sums[j] = sums[j] + jnp.where(ids == j, surface, 0.0)
    for j in range(DV_DEV):
        out[j] = jnp.sum(sums[j]) * scale


def last_kernel(scale, bits, keep, near, far, stiffness, inside, *rest):
    rows = keep.shape[1]
    outside, out = (inside, *rest[:-1]), rest[-1]
    space = lax.axis_index("space")
    even = space % 2 == 0
    flips = jnp.where(even, space, -1 - space)
    last = [(flips & ((2 << b) - 1)) == (1 << b) for b in range(bits)]

    def outer(i):
        value = 0.0
        for b in range(1, bits):
            value = jnp.where(last[b], outside[b][i], value)
        return value

    for x in range(rows):
        inverse = scale / stiffness[x]
        for d in range(3):
            value = keep[d, x] + near[d, x] + far[d, x]
            for at, side in (
                (LOW_AT[d] + x, even if x < REACHES[d] else None),
                (LOW_AT[d] + x - rows + REACHES[d], ~even if x >= rows - REACHES[d] else None),
            ):
                if side is not None:
                    value = value + jnp.where(side, outer(at), inside[at])
            out[d, x] = value * inverse


def per_device(adjoint, flux_terms, stiffness, normals, design_map):
    insts, spaces = lax.axis_size("inst"), lax.axis_size("space")
    rows, block, depth = stiffness.shape
    scale = 1.0 / (DIAG**3 * adjoint.shape[0] * insts)

    vmem = pl.BlockSpec(memory_space=pltpu.VMEM)

    def on_chip(kernel, shapes, *operands, weight=1):
        out = [jax.ShapeDtypeStruct(shape, jnp.float32) for shape in shapes]
        return pl.pallas_call(
            kernel,
            out_shape=out,
            in_specs=[vmem] * len(operands),
            out_specs=[vmem] * len(out),
            compiler_params=pltpu.CompilerParams(vmem_limit_bytes=4 * 2**20),
            cost_estimate=pl.CostEstimate(
                flops=500_000 * weight, bytes_accessed=1_500_000 * weight, transcendentals=0
            ),
        )(*operands)

    main_ko, main_kx, main_so, main_sx, over_ko, over_kx, over_s, face = front(
        adjoint, flux_terms
    )

    other_core = [(i, i ^ 1) for i in range(insts)]
    other_chip = [(i, i ^ 2) for i in range(insts)]

    plane = (1, block, depth)
    face_r = lax.ppermute(face, "inst", other_core)
    [coefs] = on_chip(
        coefs_kernel, [plane], face, stiffness, normals.transpose(0, 2, 1), design_map.T
    )
    coefs_r = lax.ppermute(coefs, "inst", other_core)
    over_r = lax.ppermute(over_s, "inst", other_core)
    main_r = lax.ppermute(main_sx, "inst", other_core)
    main_near = lax.ppermute(main_so, "inst", other_core)
    [near] = on_chip(
        near_kernel, [(FACE + 2, block, depth)], over_kx, over_r, face, face_r, coefs, coefs_r
    )
    far = lax.ppermute(near, "inst", other_chip)
    [main_x] = on_chip(add_kernel, [main_kx.shape], main_kx, main_r, far)
    main_far = lax.ppermute(main_x, "inst", other_chip)

    bits = spaces.bit_length() - 1
    [going] = on_chip(
        first_kernel, [(2 * OVER + 2, block, depth)], over_ko, over_r, near, far
    )
    arrived = []
    for bit in range(bits):
        if bit > 0:
            [going] = on_chip(
                functools.partial(next_kernel, bit - 1),
                [(OVER + (2 << bit), block, depth)],
                going, arrived[-1],
            )
        swap = [(i, i ^ (1 << bit)) for i in range(spaces)]
        arrived.append(lax.ppermute(going, "space", swap))
    design_grad = pl.pallas_call(
        functools.partial(design_kernel, scale, rows, bits - 1),
        out_shape=jax.ShapeDtypeStruct((DV_DEV,), jnp.float32),
        in_specs=[vmem] * 2,
        out_specs=pl.BlockSpec(memory_space=pltpu.SMEM),
        compiler_params=pltpu.CompilerParams(vmem_limit_bytes=4 * 2**20),
    )(going, arrived[-1])
    [mesh_adjoint] = on_chip(
        functools.partial(last_kernel, scale, bits), [(3, rows, block, depth)],
        main_ko, main_near, main_far, stiffness, *arrived,
    )
    return (mesh_adjoint, design_grad)


def solution(mesh):
    in_specs = (
        P("inst", None, "space", None, None),
        P("inst", None, None, "space", None, None),
        P("space", "inst", None),
        P(None, "space", "inst"),
        P("space", "inst"),
    )
    out_specs = (P(None, "space", "inst", None), P(("inst", "space")))
    return jax.shard_map(
        per_device, mesh=mesh, in_specs=in_specs, out_specs=out_specs, check_vma=False
    )
```

```python
import functools
import jax
import jax.numpy as jnp
from jax import lax
from jax.experimental import pallas as pl
from jax.experimental.pallas import tpu as pltpu
from jax.sharding import PartitionSpec as P

DIAG = 6.5
DV_DEV = 8
REACH = 3
PAD = REACH + 1
CHUNK = 4
REACHES = (3, 2, 2)
LOW_AT = (0, 3, 5)
OVER = 7
GROUP = 64
FACE_AT = (REACH, 24, 44)


def shifted_rows(tiles, top, bottom):
    down = [pltpu.roll(t, 1, 0) for t in tiles]
    up = [pltpu.roll(t, 7, 0) for t in tiles]
    zero = jnp.zeros_like(tiles[0])
    down = [jnp.where(top, p, n) for p, n in zip([zero] + down[:-1], down)]
    up = [jnp.where(bottom, n, p) for p, n in zip(up, up[1:] + [zero])]
    return down, up


def front_kernel(
    adj_hbm, flux_hbm,
    main_ko, main_kx, main_so, main_sx, over_ko, over_kx, over_s, wall,
    adj, flux, work, metric, plane, side, band, stack, along, adj_sems, flux_sems,
):
    kinds, variables, rows, width, depth = adj.shape
    chunks = rows // CHUNK
    tiles = width // 8
    inst, space = lax.axis_index("inst"), lax.axis_index("space")
    low_open = jnp.where(space > 0, 1.0, 0.0)
    high_open = jnp.where(space < lax.axis_size("space") - 1, 1.0, 0.0)

    def adj_copy(i):
        part = pl.ds(i * CHUNK, CHUNK)
        return pltpu.make_async_copy(
            adj_hbm.at[:, :, part], adj.at[:, :, part], adj_sems.at[i]
        )

    def flux_copy(i):
        part = pl.ds(i * CHUNK, CHUNK)
        return pltpu.make_async_copy(
            flux_hbm.at[:, :, :, part], flux.at[:, :, :, part], flux_sems.at[i]
        )

    for i in range(chunks):
        adj_copy(i).start()
        flux_copy(i).start()

    near = jnp.abs(
        lax.broadcasted_iota(jnp.int32, (depth, depth), 0)
        - lax.broadcasted_iota(jnp.int32, (depth, depth), 1)
    )
    lane = lax.broadcasted_iota(jnp.int32, (depth, depth), 1)
    ends = jnp.where((lane == 0) | (lane == depth - 1), 1.0, 2.0)
    once = jnp.where(near == 1, 1.0, 0.0).astype(jnp.bfloat16)
    twice = jnp.where(near == 0, ends, jnp.where(near == 2, 1.0, 0.0)).astype(jnp.bfloat16)
    for half in (slice(0, depth), slice(depth, 2 * depth)):
        band[half, :depth] = once
        band[half, depth:] = twice
    zero = jnp.zeros((width, depth), jnp.float32)
    for d in range(3):
        for x in (-2, -1, rows, rows + 1):
            metric[d, x + PAD] = zero
            side[d, x + PAD] = zero
            plane[d, x + PAD] = zero
    for x in (-2, -1, rows, rows + 1):
        work[0, x + PAD] = zero

    row = lax.broadcasted_iota(jnp.int32, (8, depth), 0)
    top, bottom = row == 0, row == 7
    column = lax.broadcasted_iota(jnp.int32, (8, depth), 1)
    first, last = column == 0, column == depth - 1

    def weigh(x):
        for h in range(width // 16):
            part = slice(16 * h, 16 * h + 16)
            sums = [jnp.zeros((16, depth), jnp.float32) for _ in range(3)]
            for k in range(kinds):
                for v in range(variables):
                    a = adj[k, v, x, part].astype(jnp.float32)
                    for d in range(3):
                        sums[d] = sums[d] + a * flux[k, v, d, x, part].astype(jnp.float32)
            for d in range(3):
                work[d, x + PAD, part] = sums[d]

    def tile(t):
        return slice(8 * t, 8 * t + 8)

    def planes(slabs):
        count = len(slabs) * width
        for s, (d, x) in enumerate(slabs):
            r = x + PAD
            here = [work[d, r, tile(t)] for t in range(tiles)]
            if d == 0:
                open_ = jnp.where(x < 0, low_open, jnp.where(x >= rows, high_open, 1.0))
                low = [work[0, r - 1, tile(t)] for t in range(tiles)]
                high = [work[0, r + 1, tile(t)] for t in range(tiles)]
                m = [(h + 0.5 * (p - n)) * open_ for h, p, n in zip(here, low, high)]
            elif d == 1:
                low, high = shifted_rows(here, top, bottom)
                m = [h + 0.5 * (p - n) for h, p, n in zip(here, low, high)]
            else:
                m = [
                    h + 0.5 * (
                        jnp.where(first, 0.0, pltpu.roll(h, 1, 1))
                        - jnp.where(last, 0.0, pltpu.roll(h, depth - 1, 1))
                    )
                    for h in here
                ]
            for t in range(tiles):
                metric[d, r, tile(t)] = m[t]
            for t in range(0, tiles, 2):
                both = jnp.concatenate(m[t : t + 2], axis=0)
                rounded = both.astype(jnp.bfloat16)
                part = slice(s * width + 8 * t, s * width + 8 * t + 16)
                stack[part, :depth] = rounded
                stack[part, depth:] = (both - rounded.astype(jnp.float32)).astype(jnp.bfloat16)
        along[:count] = jnp.dot(stack[:count], band[...], preferred_element_type=jnp.float32)
        for s, (d, x) in enumerate(slabs):
            r = x + PAD
            at = s * width
            m = [metric[d, r, tile(t)] for t in range(tiles)]
            along_1 = [along[at + 8 * t : at + 8 * t + 8, :depth] for t in range(tiles)]
            along_2 = [along[at + 8 * t : at + 8 * t + 8, depth:] for t in range(tiles)]
            low, high = shifted_rows(m, top, bottom)
            once = [(p + n) + q for p, n, q in zip(low, high, along_1)]
            low, high = shifted_rows([o + q for o, q in zip(once, along_1)], top, bottom)
            returns = 2.0 - jnp.where(
                x == 0, 1.0 - low_open, jnp.where(x == rows - 1, 1.0 - high_open, 0.0)
            )
            weight = DIAG * DIAG + returns
            for t in range(tiles):
                side[d, r, tile(t)] = DIAG * m[t] + (once[t] + once[t])
                twice = (low[t] + high[t]) + along_2[t]
                plane[d, r, tile(t)] = weight * m[t] + DIAG * once[t] + twice

    def settle(i, extra):
        planes(
            [(1, i * CHUNK + j) for j in range(CHUNK)]
            + [(2, i * CHUNK + j) for j in range(CHUNK)]
            + [(0, i * CHUNK + j - 1) for j in range(CHUNK + extra)]
        )

    def arrive(i):
        adj_copy(i).wait()
        flux_copy(i).wait()

    arrive(0)
    for j in range(CHUNK):
        weigh(j)

    def stage(i, _):
        arrive(i)
        settle(i - 1, 0)
        for j in range(CHUNK):
            weigh(i * CHUNK + j)
        return 0

    lax.fori_loop(1, chunks, stage, 0)
    settle(chunks - 1, 2)

    def put(refs, index, place, total, face):
        for j, ref, shift in zip((0, 2, 1, 3), refs, (0, 0, 2 * OVER, 0)):
            b = inst ^ j
            at = pl.multiple_of(8 * b, 8)
            value = total(pl.ds(at, 8))
            if ref is over_s:
                ref[index + shift] = value
            else:
                ref[index] = value
            face = jnp.where(column == GROUP * b + place, value[:, 0:1], face)
        return face

    main_refs = (main_ko, main_kx, main_so, main_sx)
    over_refs = (over_ko, over_kx, over_s, over_s)

    def reached(d, x, part):
        r = x + PAD
        first, last = (PAD - 1, PAD + rows) if d == 0 else (PAD, PAD + rows - 1)
        terms = (
            [plane[d, r, part]] * (first <= r <= last)
            + [side[d, s, part] for s in (r - 1, r + 1) if first <= s <= last]
            + [metric[d, s, part] for s in (r - 2, r + 2) if first <= s <= last]
        )
        return functools.reduce(jnp.add, terms)

    face = jnp.zeros((8, depth), jnp.float32)
    for d in range(3):
        for x in range(-REACHES[d], 0):
            face = put(
                over_refs, LOW_AT[d] + x + REACHES[d], FACE_AT[d] + x,
                functools.partial(reached, d, x), face,
            )
        for x in range(rows, rows + REACHES[d]):
            face = put(
                over_refs, OVER + LOW_AT[d] + x - rows, FACE_AT[d] + x,
                functools.partial(reached, d, x), face,
            )

    def inner(x, face):
        r = x + PAD
        for d in range(3):

            def total(part):
                value = plane[d, r, part] + (side[d, r - 1, part] + side[d, r + 1, part])
                return value + (metric[d, r - 2, part] + metric[d, r + 2, part])

            face = put(main_refs, (d, x), FACE_AT[d] + x, total, face)
        return face

    face = lax.fori_loop(0, rows, inner, face, unroll=2)
    wall[0] = face


def front(adjoint, flux_terms):
    kinds, variables, rows, width, depth = adjoint.shape
    f32 = jnp.float32
    block = width // 4
    main = jax.ShapeDtypeStruct((3, rows, block, depth), f32)
    vmem = pl.BlockSpec(memory_space=pltpu.VMEM)
    hbm = pl.BlockSpec(memory_space=pltpu.HBM)
    padded = (3, rows + 2 * PAD, width, depth)
    most = (3 * CHUNK + 2) * width
    over_rows = (2 * OVER, 2 * OVER, 4 * OVER, 1)
    return pl.pallas_call(
        front_kernel,
        out_shape=[main] * 4
        + [jax.ShapeDtypeStruct((count, block, depth), f32) for count in over_rows],
        in_specs=[hbm] * 2,
        out_specs=[vmem] * 8,
        scratch_shapes=[
            pltpu.VMEM(adjoint.shape, adjoint.dtype),
            pltpu.VMEM(flux_terms.shape, flux_terms.dtype),
            pltpu.VMEM(padded, f32),
            pltpu.VMEM(padded, f32),
            pltpu.VMEM(padded, f32),
            pltpu.VMEM(padded, f32),
            pltpu.VMEM((2 * depth, 2 * depth), jnp.bfloat16),
            pltpu.VMEM((most, 2 * depth), jnp.bfloat16),
            pltpu.VMEM((most, 2 * depth), f32),
            pltpu.SemaphoreType.DMA((rows // CHUNK,)),
            pltpu.SemaphoreType.DMA((rows // CHUNK,)),
        ],
        compiler_params=pltpu.CompilerParams(vmem_limit_bytes=51 * 2**20),
        cost_estimate=pl.CostEstimate(
            flops=60_000_000, bytes_accessed=13_000_000, transcendentals=0
        ),
    )(adjoint, flux_terms)


def coefs_kernel(after, stiffness, normals, ids, out):
    del after
    rows, block, depth = stiffness.shape
    column = lax.broadcasted_iota(jnp.int32, (block, depth), 1)
    own = GROUP * lax.axis_index("inst")
    coefs = jnp.zeros((block, depth), jnp.float32)
    for x in range(rows):
        inverse = 1.0 / stiffness[x, :, 0:1]
        for d in range(3):
            here = normals[d, :, x : x + 1] * inverse
            coefs = jnp.where(column == own + d * rows + x, here, coefs)
        here = ids[:, x : x + 1].astype(jnp.float32)
        coefs = jnp.where(column == own + 3 * rows + x, here, coefs)
    out[0] = coefs


def add_kernel(keep, near, *rest):
    out = rest[-1]
    for d in range(out.shape[0]):
        for x in range(out.shape[1]):
            out[d, x] = keep[d, x] + near[d, x]


def pass_kernel(value, after, out):
    del after
    for i in range(out.shape[0]):
        out[i] = value[i]


def wall_near_kernel(face, face_near, coefs, coefs_near, out):
    out[0] = face[0] + face_near[0]
    out[1] = coefs[0] + coefs_near[0]


def wall_kernel(near, far, after, out):
    del after
    out[0] = near[0] + far[0]
    out[1] = near[1] + far[1]


def over_low(keep, over_near, far, i):
    return keep[i] + over_near[2 * OVER + i] + far[i]


def over_high(keep, over_near, far, i):
    return keep[OVER + i] + over_near[3 * OVER + i] + far[OVER + i]


def over_kernel(keep, over_near, far, after, inside, outside):
    del after
    even = lax.axis_index("space") % 2 == 0
    for i in range(OVER):
        low, high = (f(keep, over_near, far, i) for f in (over_low, over_high))
        inside[i] = jnp.where(even, high, low)
        outside[i] = jnp.where(even, low, high)


def in_order(bit, own, other):
    upper = (lax.axis_index("space") >> bit) % 2 == 1
    count = 2 << bit
    lows = [jnp.where(upper, other[i], own[i]) for i in range(count)]
    highs = [jnp.where(upper, own[i], other[i]) for i in range(count)]
    return lows + highs


def gather_kernel(bit, own, other, out):
    for i, value in enumerate(in_order(bit, own, other)):
        out[i] = value


def design_kernel(scale, rows, bit, own, other, out):
    planes = in_order(bit, own, other)
    faces, coefs = planes[::2], planes[1::2]
    spaces = len(faces)
    block, depth = faces[0].shape
    column = lax.broadcasted_iota(jnp.int32, (block, depth), 1) % GROUP
    at_low = functools.reduce(
        jnp.logical_or,
        [(column >= at) & (column < at + n) for at, n in zip(FACE_AT, REACHES)],
    )
    at_high = functools.reduce(
        jnp.logical_or,
        [
            (column >= at + rows - n) & (column < at + rows)
            for at, n in zip(FACE_AT, REACHES)
        ],
    )
    mine = (lax.axis_index("inst") * spaces + lax.axis_index("space")) * DV_DEV
    sums = [jnp.zeros((block, depth), jnp.float32) for _ in range(DV_DEV)]
    for s in range(spaces):
        whole = faces[s]
        if s > 0:
            whole = whole + jnp.where(at_low, pltpu.roll(faces[s - 1], depth - rows, 1), 0.0)
        if s < spaces - 1:
            whole = whole + jnp.where(at_high, pltpu.roll(faces[s + 1], rows, 1), 0.0)
        surface = jnp.zeros((block, depth), jnp.float32)
        for d in range(3):
            turned = pltpu.roll(coefs[s], depth - d * rows, 1) if d else coefs[s]
            surface = surface + pltpu.roll(whole, depth - FACE_AT[d], 1) * turned
        ids = pltpu.roll(coefs[s], depth - 3 * rows, 1).astype(jnp.int32) - mine
        ids = jnp.where(column < rows, ids, -1)
        for j in range(DV_DEV):
            sums[j] = sums[j] + jnp.where(ids == j, surface, 0.0)
    for j in range(DV_DEV):
        out[j] = jnp.sum(sums[j]) * scale


def last_kernel(scale, bits, keep, near, far, stiffness, inside, *rest):
    rows = keep.shape[1]
    outside, out = rest[:-1], rest[-1]
    space = lax.axis_index("space")
    even = space % 2 == 0
    flips = jnp.where(even, space, -1 - space)
    last = [(flips & ((2 << b) - 1)) == (1 << b) for b in range(bits)]

    def outer(i):
        value = 0.0
        for b in range(1, bits):
            value = jnp.where(last[b], outside[b][i], value)
        return value

    for x in range(rows):
        inverse = scale / stiffness[x]
        for d in range(3):
            value = keep[d, x] + near[d, x] + far[d, x]
            for at, side in (
                (LOW_AT[d] + x, even if x < REACHES[d] else None),
                (LOW_AT[d] + x - rows + REACHES[d], ~even if x >= rows - REACHES[d] else None),
            ):
                if side is not None:
                    value = value + jnp.where(side, outer(at), inside[at])
            out[d, x] = value * inverse


def per_device(adjoint, flux_terms, stiffness, normals, design_map):
    insts, spaces = lax.axis_size("inst"), lax.axis_size("space")
    rows, block, depth = stiffness.shape
    scale = 1.0 / (DIAG**3 * adjoint.shape[0] * insts)

    vmem = pl.BlockSpec(memory_space=pltpu.VMEM)

    def on_chip(kernel, shapes, *operands, weight=1):
        out = [jax.ShapeDtypeStruct(shape, jnp.float32) for shape in shapes]
        return pl.pallas_call(
            kernel,
            out_shape=out,
            in_specs=[vmem] * len(operands),
            out_specs=[vmem] * len(out),
            compiler_params=pltpu.CompilerParams(vmem_limit_bytes=4 * 2**20),
            cost_estimate=pl.CostEstimate(
                flops=500_000 * weight, bytes_accessed=1_500_000 * weight, transcendentals=0
            ),
        )(*operands)

    main_ko, main_kx, main_so, main_sx, over_ko, over_kx, over_s, face = front(
        adjoint, flux_terms
    )

    other_core = [(i, i ^ 1) for i in range(insts)]
    other_chip = [(i, i ^ 2) for i in range(insts)]

    plane = (1, block, depth)
    face_r = lax.ppermute(face, "inst", other_core)
    [coefs] = on_chip(
        coefs_kernel, [plane], face, stiffness, normals.transpose(0, 2, 1), design_map.T
    )
    coefs_r = lax.ppermute(coefs, "inst", other_core)
    [wall_near] = on_chip(
        wall_near_kernel, [(2, block, depth)], face, face_r, coefs, coefs_r
    )
    wall_far = lax.ppermute(wall_near, "inst", other_chip)
    over_r = lax.ppermute(over_s, "inst", other_core)
    main_r = lax.ppermute(main_sx, "inst", other_core)
    main_near = lax.ppermute(main_so, "inst", other_core)
    over_x = over_kx + over_r[: 2 * OVER]
    over_far = lax.ppermute(over_x, "inst", other_chip)
    [wall] = on_chip(wall_kernel, [(2, block, depth)], wall_near, wall_far, over_x)

    bits = spaces.bit_length() - 1
    swaps = [[(i, i ^ (1 << bit)) for i in range(spaces)] for bit in range(bits)]
    halo = (OVER, block, depth)
    arrived = []
    for bit in range(bits):
        if bit > 0:
            [wall] = on_chip(
                functools.partial(gather_kernel, bit - 1),
                [(2 << bit, block, depth)],
                wall, walls,
            )
        if bit == 1:
            inside, outside = on_chip(
                over_kernel, [halo, halo], over_ko, over_r, over_far, wall
            )
            [main_x] = on_chip(add_kernel, [main_kx.shape], main_kx, main_r, over_far, wall)
        walls = lax.ppermute(wall, "space", swaps[bit])
        if bit > 1:
            [outside] = on_chip(pass_kernel, [halo], outside, wall)
        if bit > 0:
            outside = lax.ppermute(outside, "space", swaps[bit - 1])
            arrived.append(outside)
    main_far = lax.ppermute(main_x, "inst", other_chip)
    inside = lax.ppermute(inside, "space", swaps[0])
    arrived.append(lax.ppermute(outside, "space", swaps[-1]))
    design_grad = pl.pallas_call(
        functools.partial(design_kernel, scale, rows, bits - 1),
        out_shape=jax.ShapeDtypeStruct((DV_DEV,), jnp.float32),
        in_specs=[vmem] * 2,
        out_specs=pl.BlockSpec(memory_space=pltpu.SMEM),
        compiler_params=pltpu.CompilerParams(vmem_limit_bytes=4 * 2**20),
    )(wall, walls)
    [mesh_adjoint] = on_chip(
        functools.partial(last_kernel, scale, bits), [(3, rows, block, depth)],
        main_ko, main_near, main_far, stiffness, inside, *arrived,
    )
    return (mesh_adjoint, design_grad)


def solution(mesh):
    in_specs = (
        P("inst", None, "space", None, None),
        P("inst", None, None, "space", None, None),
        P("space", "inst", None),
        P(None, "space", "inst"),
        P("space", "inst"),
    )
    out_specs = (P(None, "space", "inst", None), P(("inst", "space")))
    return jax.shard_map(
        per_device, mesh=mesh, in_specs=in_specs, out_specs=out_specs, check_vma=False
    )
```

```python
import functools
import jax
import jax.numpy as jnp
from jax import lax
from jax.experimental import pallas as pl
from jax.experimental.pallas import tpu as pltpu
from jax.sharding import PartitionSpec as P

DIAG = 6.5
DV_DEV = 8
REACH = 3
PAD = REACH + 1
CHUNK = 4
REACHES = (3, 2, 2)
LOW_AT = (0, 3, 5)
OVER = 7
FACE = 2 * OVER
GROUP = 64
FACE_AT = (REACH, 24, 44)


def shifted_rows(tiles, top, bottom):
    down = [pltpu.roll(t, 1, 0) for t in tiles]
    up = [pltpu.roll(t, 7, 0) for t in tiles]
    zero = jnp.zeros_like(tiles[0])
    down = [jnp.where(top, p, n) for p, n in zip([zero] + down[:-1], down)]
    up = [jnp.where(bottom, n, p) for p, n in zip(up, up[1:] + [zero])]
    return down, up


def front_kernel(
    adj_hbm, flux_hbm,
    main_ko, main_kx, main_so, main_sx, over_ko, over_kx, over_s, wall,
    adj, flux, work, metric, plane, side, band, stack, along, adj_sems, flux_sems,
):
    kinds, variables, rows, width, depth = adj.shape
    chunks = rows // CHUNK
    tiles = width // 8
    inst, space = lax.axis_index("inst"), lax.axis_index("space")
    low_open = jnp.where(space > 0, 1.0, 0.0)
    high_open = jnp.where(space < lax.axis_size("space") - 1, 1.0, 0.0)

    def adj_copy(i):
        part = pl.ds(i * CHUNK, CHUNK)
        return pltpu.make_async_copy(
            adj_hbm.at[:, :, part], adj.at[:, :, part], adj_sems.at[i]
        )

    def flux_copy(i):
        part = pl.ds(i * CHUNK, CHUNK)
        return pltpu.make_async_copy(
            flux_hbm.at[:, :, :, part], flux.at[:, :, :, part], flux_sems.at[i]
        )

    for i in range(chunks):
        adj_copy(i).start()
        flux_copy(i).start()

    near = jnp.abs(
        lax.broadcasted_iota(jnp.int32, (depth, depth), 0)
        - lax.broadcasted_iota(jnp.int32, (depth, depth), 1)
    )
    lane = lax.broadcasted_iota(jnp.int32, (depth, depth), 1)
    ends = jnp.where((lane == 0) | (lane == depth - 1), 1.0, 2.0)
    once = jnp.where(near == 1, 1.0, 0.0).astype(jnp.bfloat16)
    twice = jnp.where(near == 0, ends, jnp.where(near == 2, 1.0, 0.0)).astype(jnp.bfloat16)
    for half in (slice(0, depth), slice(depth, 2 * depth)):
        band[half, :depth] = once
        band[half, depth:] = twice
    zero = jnp.zeros((width, depth), jnp.float32)
    for d in range(3):
        for x in (-2, -1, rows, rows + 1):
            metric[d, x + PAD] = zero
            side[d, x + PAD] = zero
            plane[d, x + PAD] = zero
    for x in (-2, -1, rows, rows + 1):
        work[0, x + PAD] = zero

    row = lax.broadcasted_iota(jnp.int32, (8, depth), 0)
    top, bottom = row == 0, row == 7
    column = lax.broadcasted_iota(jnp.int32, (8, depth), 1)
    first, last = column == 0, column == depth - 1

    def weigh(x):
        for h in range(width // 16):
            part = slice(16 * h, 16 * h + 16)
            sums = [jnp.zeros((16, depth), jnp.float32) for _ in range(3)]
            for k in range(kinds):
                for v in range(variables):
                    a = adj[k, v, x, part].astype(jnp.float32)
                    for d in range(3):
                        sums[d] = sums[d] + a * flux[k, v, d, x, part].astype(jnp.float32)
            for d in range(3):
                work[d, x + PAD, part] = sums[d]

    def tile(t):
        return slice(8 * t, 8 * t + 8)

    def planes(slabs):
        count = len(slabs) * width
        for s, (d, x) in enumerate(slabs):
            r = x + PAD
            here = [work[d, r, tile(t)] for t in range(tiles)]
            if d == 0:
                open_ = jnp.where(x < 0, low_open, jnp.where(x >= rows, high_open, 1.0))
                low = [work[0, r - 1, tile(t)] for t in range(tiles)]
                high = [work[0, r + 1, tile(t)] for t in range(tiles)]
                m = [(h + 0.5 * (p - n)) * open_ for h, p, n in zip(here, low, high)]
            elif d == 1:
                low, high = shifted_rows(here, top, bottom)
                m = [h + 0.5 * (p - n) for h, p, n in zip(here, low, high)]
            else:
                m = [
                    h + 0.5 * (
                        jnp.where(first, 0.0, pltpu.roll(h, 1, 1))
                        - jnp.where(last, 0.0, pltpu.roll(h, depth - 1, 1))
                    )
                    for h in here
                ]
            for t in range(tiles):
                metric[d, r, tile(t)] = m[t]
            for t in range(0, tiles, 2):
                both = jnp.concatenate(m[t : t + 2], axis=0)
                rounded = both.astype(jnp.bfloat16)
                part = slice(s * width + 8 * t, s * width + 8 * t + 16)
                stack[part, :depth] = rounded
                stack[part, depth:] = (both - rounded.astype(jnp.float32)).astype(jnp.bfloat16)
        along[:count] = jnp.dot(stack[:count], band[...], preferred_element_type=jnp.float32)
        for s, (d, x) in enumerate(slabs):
            r = x + PAD
            at = s * width
            m = [metric[d, r, tile(t)] for t in range(tiles)]
            along_1 = [along[at + 8 * t : at + 8 * t + 8, :depth] for t in range(tiles)]
            along_2 = [along[at + 8 * t : at + 8 * t + 8, depth:] for t in range(tiles)]
            low, high = shifted_rows(m, top, bottom)
            once = [(p + n) + q for p, n, q in zip(low, high, along_1)]
            low, high = shifted_rows([o + q for o, q in zip(once, along_1)], top, bottom)
            returns = 2.0 - jnp.where(
                x == 0, 1.0 - low_open, jnp.where(x == rows - 1, 1.0 - high_open, 0.0)
            )
            weight = DIAG * DIAG + returns
            for t in range(tiles):
                side[d, r, tile(t)] = DIAG * m[t] + (once[t] + once[t])
                twice = (low[t] + high[t]) + along_2[t]
                plane[d, r, tile(t)] = weight * m[t] + DIAG * once[t] + twice

    def settle(i, extra):
        planes(
            [(1, i * CHUNK + j) for j in range(CHUNK)]
            + [(2, i * CHUNK + j) for j in range(CHUNK)]
            + [(0, i * CHUNK + j - 1) for j in range(CHUNK + extra)]
        )

    def arrive(i):
        adj_copy(i).wait()
        flux_copy(i).wait()

    arrive(0)
    for j in range(CHUNK):
        weigh(j)

    def stage(i, _):
        arrive(i)
        settle(i - 1, 0)
        for j in range(CHUNK):
            weigh(i * CHUNK + j)
        return 0

    lax.fori_loop(1, chunks, stage, 0)
    settle(chunks - 1, 2)

    def put(refs, index, place, total, face):
        for j, ref, shift in zip((0, 2, 1, 3), refs, (0, 0, 2 * OVER, 0)):
            b = inst ^ j
            at = pl.multiple_of(8 * b, 8)
            value = total(pl.ds(at, 8))
            if ref is over_s:
                ref[index + shift] = value
            else:
                ref[index] = value
            face = jnp.where(column == GROUP * b + place, value[:, 0:1], face)
        return face

    main_refs = (main_ko, main_kx, main_so, main_sx)
    over_refs = (over_ko, over_kx, over_s, over_s)

    def reached(d, x, part):
        r = x + PAD
        first, last = (PAD - 1, PAD + rows) if d == 0 else (PAD, PAD + rows - 1)
        terms = (
            [plane[d, r, part]] * (first <= r <= last)
            + [side[d, s, part] for s in (r - 1, r + 1) if first <= s <= last]
            + [metric[d, s, part] for s in (r - 2, r + 2) if first <= s <= last]
        )
        return functools.reduce(jnp.add, terms)

    face = jnp.zeros((8, depth), jnp.float32)
    for d in range(3):
        for x in range(-REACHES[d], 0):
            face = put(
                over_refs, LOW_AT[d] + x + REACHES[d], FACE_AT[d] + x,
                functools.partial(reached, d, x), face,
            )
        for x in range(rows, rows + REACHES[d]):
            face = put(
                over_refs, OVER + LOW_AT[d] + x - rows, FACE_AT[d] + x,
                functools.partial(reached, d, x), face,
            )

    def inner(x, face):
        r = x + PAD
        for d in range(3):

            def total(part):
                value = plane[d, r, part] + (side[d, r - 1, part] + side[d, r + 1, part])
                return value + (metric[d, r - 2, part] + metric[d, r + 2, part])

            face = put(main_refs, (d, x), FACE_AT[d] + x, total, face)
        return face

    face = lax.fori_loop(0, rows, inner, face, unroll=2)
    wall[0] = face


def front(adjoint, flux_terms):
    kinds, variables, rows, width, depth = adjoint.shape
    f32 = jnp.float32
    block = width // 4
    main = jax.ShapeDtypeStruct((3, rows, block, depth), f32)
    vmem = pl.BlockSpec(memory_space=pltpu.VMEM)
    hbm = pl.BlockSpec(memory_space=pltpu.HBM)
    padded = (3, rows + 2 * PAD, width, depth)
    most = (3 * CHUNK + 2) * width
    over_rows = (2 * OVER, 2 * OVER, 4 * OVER, 1)
    return pl.pallas_call(
        front_kernel,
        out_shape=[main] * 4
        + [jax.ShapeDtypeStruct((count, block, depth), f32) for count in over_rows],
        in_specs=[hbm] * 2,
        out_specs=[vmem] * 8,
        scratch_shapes=[
            pltpu.VMEM(adjoint.shape, adjoint.dtype),
            pltpu.VMEM(flux_terms.shape, flux_terms.dtype),
            pltpu.VMEM(padded, f32),
            pltpu.VMEM(padded, f32),
            pltpu.VMEM(padded, f32),
            pltpu.VMEM(padded, f32),
            pltpu.VMEM((2 * depth, 2 * depth), jnp.bfloat16),
            pltpu.VMEM((most, 2 * depth), jnp.bfloat16),
            pltpu.VMEM((most, 2 * depth), f32),
            pltpu.SemaphoreType.DMA((rows // CHUNK,)),
            pltpu.SemaphoreType.DMA((rows // CHUNK,)),
        ],
        compiler_params=pltpu.CompilerParams(vmem_limit_bytes=51 * 2**20),
        cost_estimate=pl.CostEstimate(
            flops=60_000_000, bytes_accessed=13_000_000, transcendentals=0
        ),
    )(adjoint, flux_terms)


def coefs_kernel(after, stiffness, normals, ids, out):
    del after
    rows, block, depth = stiffness.shape
    column = lax.broadcasted_iota(jnp.int32, (block, depth), 1)
    own = GROUP * lax.axis_index("inst")
    coefs = jnp.zeros((block, depth), jnp.float32)
    for x in range(rows):
        inverse = 1.0 / stiffness[x, :, 0:1]
        for d in range(3):
            here = normals[d, :, x : x + 1] * inverse
            coefs = jnp.where(column == own + d * rows + x, here, coefs)
        here = ids[:, x : x + 1].astype(jnp.float32)
        coefs = jnp.where(column == own + 3 * rows + x, here, coefs)
    out[0] = coefs


def add_kernel(keep, near, after, out):
    del after
    for d in range(out.shape[0]):
        for x in range(out.shape[1]):
            out[d, x] = keep[d, x] + near[d, x]


def near_kernel(over, over_near, face, face_near, coefs, coefs_near, out):
    for i in range(2 * OVER):
        out[i] = over[i] + over_near[i]
    out[FACE] = face[0] + face_near[0]
    out[FACE + 1] = coefs[0] + coefs_near[0]


def over_low(keep, over_near, far, i):
    return keep[i] + over_near[2 * OVER + i] + far[i]


def over_high(keep, over_near, far, i):
    return keep[OVER + i] + over_near[3 * OVER + i] + far[OVER + i]


def wall_kernel(near, far, wall):
    wall[0] = near[FACE] + far[FACE]
    wall[1] = near[FACE + 1] + far[FACE + 1]


def over_kernel(keep, over_near, far, after, inside, outside):
    del after
    even = lax.axis_index("space") % 2 == 0
    for i in range(OVER):
        low, high = (f(keep, over_near, far, i) for f in (over_low, over_high))
        inside[i] = jnp.where(even, high, low)
        outside[i] = jnp.where(even, low, high)


def in_order(bit, own, other):
    upper = (lax.axis_index("space") >> bit) % 2 == 1
    groups = own.shape[0] // 2
    lows = [[jnp.where(upper, other[i], own[i]) for i in (2 * g, 2 * g + 1)] for g in range(groups)]
    highs = [[jnp.where(upper, own[i], other[i]) for i in (2 * g, 2 * g + 1)] for g in range(groups)]
    return lows, highs


def gather_kernel(bit, own, other, out):
    lows, highs = in_order(bit, own, other)
    for g, (low, high) in enumerate(zip(lows, highs)):
        for i, value in enumerate(low + high):
            out[4 * g + i] = value


def held_kernel(spaces, even_pairs, odd_pairs, out):
    space = lax.axis_index("space")
    above = space % 2 == 0
    pair = space // 2
    by_even = jnp.where(above, pair % 2 == 0, pair % 2 == 1)
    none = jnp.where(above, pair == spaces // 2 - 1, pair == 0)
    for i in range(OVER):
        value = jnp.where(by_even, even_pairs[i], odd_pairs[i])
        out[i] = jnp.where(none, 0.0, value)


def design_kernel(scale, rows, bit, own, other, out):
    lows, highs = in_order(bit, own, other)
    planes = [pair for both in zip(lows, highs) for pair in both]
    faces, coefs = zip(*planes)
    spaces = len(faces)
    block, depth = faces[0].shape
    column = lax.broadcasted_iota(jnp.int32, (block, depth), 1) % GROUP
    at_low = functools.reduce(
        jnp.logical_or,
        [(column >= at) & (column < at + n) for at, n in zip(FACE_AT, REACHES)],
    )
    at_high = functools.reduce(
        jnp.logical_or,
        [
            (column >= at + rows - n) & (column < at + rows)
            for at, n in zip(FACE_AT, REACHES)
        ],
    )
    mine = (lax.axis_index("inst") * spaces + lax.axis_index("space")) * DV_DEV
    sums = [jnp.zeros((block, depth), jnp.float32) for _ in range(DV_DEV)]
    for s in range(spaces):
        whole = faces[s]
        if s > 0:
            whole = whole + jnp.where(at_low, pltpu.roll(faces[s - 1], depth - rows, 1), 0.0)
        if s < spaces - 1:
            whole = whole + jnp.where(at_high, pltpu.roll(faces[s + 1], rows, 1), 0.0)
        surface = jnp.zeros((block, depth), jnp.float32)
        for d in range(3):
            turned = pltpu.roll(coefs[s], depth - d * rows, 1) if d else coefs[s]
            surface = surface + pltpu.roll(whole, depth - FACE_AT[d], 1) * turned
        ids = pltpu.roll(coefs[s], depth - 3 * rows, 1).astype(jnp.int32) - mine
        ids = jnp.where(column < rows, ids, -1)
        for j in range(DV_DEV):
            sums[j] = sums[j] + jnp.where(ids == j, surface, 0.0)
    for j in range(DV_DEV):
        out[j] = jnp.sum(sums[j]) * scale


def last_kernel(scale, keep, near, far, stiffness, inside, outside, out):
    rows = keep.shape[1]
    even = lax.axis_index("space") % 2 == 0
    for x in range(rows):
        inverse = scale / stiffness[x]
        for d in range(3):
            value = keep[d, x] + near[d, x] + far[d, x]
            for at, side in (
                (LOW_AT[d] + x, even if x < REACHES[d] else None),
                (LOW_AT[d] + x - rows + REACHES[d], ~even if x >= rows - REACHES[d] else None),
            ):
                if side is not None:
                    value = value + jnp.where(side, outside[at], inside[at])
            out[d, x] = value * inverse


def per_device(adjoint, flux_terms, stiffness, normals, design_map):
    insts, spaces = lax.axis_size("inst"), lax.axis_size("space")
    rows, block, depth = stiffness.shape
    scale = 1.0 / (DIAG**3 * adjoint.shape[0] * insts)

    vmem = pl.BlockSpec(memory_space=pltpu.VMEM)

    def on_chip(kernel, shapes, *operands, weight=1):
        out = [jax.ShapeDtypeStruct(shape, jnp.float32) for shape in shapes]
        return pl.pallas_call(
            kernel,
            out_shape=out,
            in_specs=[vmem] * len(operands),
            out_specs=[vmem] * len(out),
            compiler_params=pltpu.CompilerParams(vmem_limit_bytes=4 * 2**20),
            cost_estimate=pl.CostEstimate(
                flops=500_000 * weight, bytes_accessed=1_500_000 * weight, transcendentals=0
            ),
        )(*operands)

    main_ko, main_kx, main_so, main_sx, over_ko, over_kx, over_s, face = front(
        adjoint, flux_terms
    )

    other_core = [(i, i ^ 1) for i in range(insts)]
    other_chip = [(i, i ^ 2) for i in range(insts)]

    plane = (1, block, depth)
    face_r = lax.ppermute(face, "inst", other_core)
    [coefs] = on_chip(
        coefs_kernel, [plane], face, stiffness, normals.transpose(0, 2, 1), design_map.T
    )
    coefs_r = lax.ppermute(coefs, "inst", other_core)
    over_r = lax.ppermute(over_s, "inst", other_core)
    main_r = lax.ppermute(main_sx, "inst", other_core)
    main_near = lax.ppermute(main_so, "inst", other_core)
    [near] = on_chip(
        near_kernel, [(FACE + 2, block, depth)], over_kx, over_r, face, face_r, coefs, coefs_r
    )
    far = lax.ppermute(near, "inst", other_chip)
    halo, walls = (OVER, block, depth), (2, block, depth)
    [wall] = on_chip(wall_kernel, [walls], near, far)
    [main_x] = on_chip(add_kernel, [main_kx.shape], main_kx, main_r, wall)
    main_far = lax.ppermute(main_x, "inst", other_chip)

    pairs = spaces // 2
    odd_pairs = [
        (i, i if i // 2 in (0, pairs - 1) else ((i + 2) ^ 2) - 2) for i in range(spaces)
    ]
    for bit in reversed(range(spaces.bit_length() - 1)):
        swap = [(i, i ^ (1 << bit)) for i in range(spaces)]
        if bit == 1:
            inside, outside = on_chip(over_kernel, [halo, halo], over_ko, over_r, far, wall)
            by_even = lax.ppermute(outside, "space", swap)
            by_odd = lax.ppermute(outside, "space", odd_pairs)
        if bit == 0:
            [held] = on_chip(functools.partial(held_kernel, spaces), [halo], by_even, by_odd)
            inside = lax.ppermute(inside, "space", swap)
            outside = lax.ppermute(held, "space", swap)
        other = lax.ppermute(wall, "space", swap)
        if bit > 0:
            walls = (2 * walls[0], block, depth)
            [wall] = on_chip(functools.partial(gather_kernel, bit), [walls], wall, other)
    design_grad = pl.pallas_call(
        functools.partial(design_kernel, scale, rows, 0),
        out_shape=jax.ShapeDtypeStruct((DV_DEV,), jnp.float32),
        in_specs=[vmem] * 2,
        out_specs=pl.BlockSpec(memory_space=pltpu.SMEM),
        compiler_params=pltpu.CompilerParams(vmem_limit_bytes=4 * 2**20),
    )(wall, other)
    [mesh_adjoint] = on_chip(
        functools.partial(last_kernel, scale), [(3, rows, block, depth)],
        main_ko, main_near, main_far, stiffness, inside, outside,
    )
    return (mesh_adjoint, design_grad)


def solution(mesh):
    in_specs = (
        P("inst", None, "space", None, None),
        P("inst", None, None, "space", None, None),
        P("space", "inst", None),
        P(None, "space", "inst"),
        P("space", "inst"),
    )
    out_specs = (P(None, "space", "inst", None), P(("inst", "space")))
    return jax.shard_map(
        per_device, mesh=mesh, in_specs=in_specs, out_specs=out_specs, check_vma=False
    )
```

```python
import functools
import jax
import jax.numpy as jnp
from jax import lax
from jax.experimental import pallas as pl
from jax.experimental.pallas import tpu as pltpu
from jax.sharding import PartitionSpec as P

DIAG = 6.5
DV_DEV = 8
REACH = 3
PAD = REACH + 1
CHUNK = 4
REACHES = (3, 2, 2)
LOW_AT = (0, 3, 5)
OVER = 7
GROUP = 64
FACE_AT = (REACH, 24, 44)


def shifted_rows(tiles, top, bottom):
    down = [pltpu.roll(t, 1, 0) for t in tiles]
    up = [pltpu.roll(t, 7, 0) for t in tiles]
    zero = jnp.zeros_like(tiles[0])
    down = [jnp.where(top, p, n) for p, n in zip([zero] + down[:-1], down)]
    up = [jnp.where(bottom, n, p) for p, n in zip(up, up[1:] + [zero])]
    return down, up


def front_kernel(
    adj_hbm, flux_hbm,
    main_ko, main_kx, main_so, main_sx, over_ko, over_kx, over_s, wall,
    adj, flux, work, metric, plane, side, band, stack, along, adj_sems, flux_sems,
):
    kinds, variables, rows, width, depth = adj.shape
    chunks = rows // CHUNK
    tiles = width // 8
    inst, space = lax.axis_index("inst"), lax.axis_index("space")
    low_open = jnp.where(space > 0, 1.0, 0.0)
    high_open = jnp.where(space < lax.axis_size("space") - 1, 1.0, 0.0)

    def adj_copy(i):
        part = pl.ds(i * CHUNK, CHUNK)
        return pltpu.make_async_copy(
            adj_hbm.at[:, :, part], adj.at[:, :, part], adj_sems.at[i]
        )

    def flux_copy(i):
        part = pl.ds(i * CHUNK, CHUNK)
        return pltpu.make_async_copy(
            flux_hbm.at[:, :, :, part], flux.at[:, :, :, part], flux_sems.at[i]
        )

    for i in range(chunks):
        adj_copy(i).start()
        flux_copy(i).start()

    near = jnp.abs(
        lax.broadcasted_iota(jnp.int32, (depth, depth), 0)
        - lax.broadcasted_iota(jnp.int32, (depth, depth), 1)
    )
    lane = lax.broadcasted_iota(jnp.int32, (depth, depth), 1)
    ends = jnp.where((lane == 0) | (lane == depth - 1), 1.0, 2.0)
    once = jnp.where(near == 1, 1.0, 0.0).astype(jnp.bfloat16)
    twice = jnp.where(near == 0, ends, jnp.where(near == 2, 1.0, 0.0)).astype(jnp.bfloat16)
    for half in (slice(0, depth), slice(depth, 2 * depth)):
        band[half, :depth] = once
        band[half, depth:] = twice
    zero = jnp.zeros((width, depth), jnp.float32)
    for d in range(3):
        for x in (-2, -1, rows, rows + 1):
            metric[d, x + PAD] = zero
            side[d, x + PAD] = zero
            plane[d, x + PAD] = zero
    for x in (-2, -1, rows, rows + 1):
        work[0, x + PAD] = zero

    row = lax.broadcasted_iota(jnp.int32, (8, depth), 0)
    top, bottom = row == 0, row == 7
    column = lax.broadcasted_iota(jnp.int32, (8, depth), 1)
    first, last = column == 0, column == depth - 1

    def weigh(x):
        for h in range(width // 16):
            part = slice(16 * h, 16 * h + 16)
            sums = [jnp.zeros((16, depth), jnp.float32) for _ in range(3)]
            for k in range(kinds):
                for v in range(variables):
                    a = adj[k, v, x, part].astype(jnp.float32)
                    for d in range(3):
                        sums[d] = sums[d] + a * flux[k, v, d, x, part].astype(jnp.float32)
            for d in range(3):
                work[d, x + PAD, part] = sums[d]

    def tile(t):
        return slice(8 * t, 8 * t + 8)

    def planes(slabs):
        count = len(slabs) * width
        for s, (d, x) in enumerate(slabs):
            r = x + PAD
            here = [work[d, r, tile(t)] for t in range(tiles)]
            if d == 0:
                open_ = jnp.where(x < 0, low_open, jnp.where(x >= rows, high_open, 1.0))
                low = [work[0, r - 1, tile(t)] for t in range(tiles)]
                high = [work[0, r + 1, tile(t)] for t in range(tiles)]
                m = [(h + 0.5 * (p - n)) * open_ for h, p, n in zip(here, low, high)]
            elif d == 1:
                low, high = shifted_rows(here, top, bottom)
                m = [h + 0.5 * (p - n) for h, p, n in zip(here, low, high)]
            else:
                m = [
                    h + 0.5 * (
                        jnp.where(first, 0.0, pltpu.roll(h, 1, 1))
                        - jnp.where(last, 0.0, pltpu.roll(h, depth - 1, 1))
                    )
                    for h in here
                ]
            for t in range(tiles):
                metric[d, r, tile(t)] = m[t]
            for t in range(0, tiles, 2):
                both = jnp.concatenate(m[t : t + 2], axis=0)
                rounded = both.astype(jnp.bfloat16)
                part = slice(s * width + 8 * t, s * width + 8 * t + 16)
                stack[part, :depth] = rounded
                stack[part, depth:] = (both - rounded.astype(jnp.float32)).astype(jnp.bfloat16)
        along[:count] = jnp.dot(stack[:count], band[...], preferred_element_type=jnp.float32)
        for s, (d, x) in enumerate(slabs):
            r = x + PAD
            at = s * width
            m = [metric[d, r, tile(t)] for t in range(tiles)]
            along_1 = [along[at + 8 * t : at + 8 * t + 8, :depth] for t in range(tiles)]
            along_2 = [along[at + 8 * t : at + 8 * t + 8, depth:] for t in range(tiles)]
            low, high = shifted_rows(m, top, bottom)
            once = [(p + n) + q for p, n, q in zip(low, high, along_1)]
            low, high = shifted_rows([o + q for o, q in zip(once, along_1)], top, bottom)
            returns = 2.0 - jnp.where(
                x == 0, 1.0 - low_open, jnp.where(x == rows - 1, 1.0 - high_open, 0.0)
            )
            weight = DIAG * DIAG + returns
            for t in range(tiles):
                side[d, r, tile(t)] = DIAG * m[t] + (once[t] + once[t])
                twice = (low[t] + high[t]) + along_2[t]
                plane[d, r, tile(t)] = weight * m[t] + DIAG * once[t] + twice

    def settle(i, extra):
        planes(
            [(1, i * CHUNK + j) for j in range(CHUNK)]
            + [(2, i * CHUNK + j) for j in range(CHUNK)]
            + [(0, i * CHUNK + j - 1) for j in range(CHUNK + extra)]
        )

    def arrive(i):
        adj_copy(i).wait()
        flux_copy(i).wait()

    arrive(0)
    for j in range(CHUNK):
        weigh(j)

    def stage(i, _):
        arrive(i)
        settle(i - 1, 0)
        for j in range(CHUNK):
            weigh(i * CHUNK + j)
        return 0

    lax.fori_loop(1, chunks, stage, 0)
    settle(chunks - 1, 2)

    def put(refs, index, place, total, face):
        for j, ref, shift in zip((0, 2, 1, 3), refs, (0, 0, 2 * OVER, 0)):
            b = inst ^ j
            at = pl.multiple_of(8 * b, 8)
            value = total(pl.ds(at, 8))
            if ref is over_s:
                ref[index + shift] = value
            else:
                ref[index] = value
            face = jnp.where(column == GROUP * b + place, value[:, 0:1], face)
        return face

    main_refs = (main_ko, main_kx, main_so, main_sx)
    over_refs = (over_ko, over_kx, over_s, over_s)

    def reached(d, x, part):
        r = x + PAD
        first, last = (PAD - 1, PAD + rows) if d == 0 else (PAD, PAD + rows - 1)
        terms = (
            [plane[d, r, part]] * (first <= r <= last)
            + [side[d, s, part] for s in (r - 1, r + 1) if first <= s <= last]
            + [metric[d, s, part] for s in (r - 2, r + 2) if first <= s <= last]
        )
        return functools.reduce(jnp.add, terms)

    face = jnp.zeros((8, depth), jnp.float32)
    for d in range(3):
        for x in range(-REACHES[d], 0):
            face = put(
                over_refs, LOW_AT[d] + x + REACHES[d], FACE_AT[d] + x,
                functools.partial(reached, d, x), face,
            )
        for x in range(rows, rows + REACHES[d]):
            face = put(
                over_refs, OVER + LOW_AT[d] + x - rows, FACE_AT[d] + x,
                functools.partial(reached, d, x), face,
            )

    def inner(x, face):
        r = x + PAD
        for d in range(3):

            def total(part):
                value = plane[d, r, part] + (side[d, r - 1, part] + side[d, r + 1, part])
                return value + (metric[d, r - 2, part] + metric[d, r + 2, part])

            face = put(main_refs, (d, x), FACE_AT[d] + x, total, face)
        return face

    face = lax.fori_loop(0, rows, inner, face, unroll=2)
    wall[0] = face


def front(adjoint, flux_terms):
    kinds, variables, rows, width, depth = adjoint.shape
    f32 = jnp.float32
    block = width // 4
    main = jax.ShapeDtypeStruct((3, rows, block, depth), f32)
    vmem = pl.BlockSpec(memory_space=pltpu.VMEM)
    hbm = pl.BlockSpec(memory_space=pltpu.HBM)
    padded = (3, rows + 2 * PAD, width, depth)
    most = (3 * CHUNK + 2) * width
    over_rows = (2 * OVER, 2 * OVER, 4 * OVER, 1)
    return pl.pallas_call(
        front_kernel,
        out_shape=[main] * 4
        + [jax.ShapeDtypeStruct((count, block, depth), f32) for count in over_rows],
        in_specs=[hbm] * 2,
        out_specs=[vmem] * 8,
        scratch_shapes=[
            pltpu.VMEM(adjoint.shape, adjoint.dtype),
            pltpu.VMEM(flux_terms.shape, flux_terms.dtype),
            pltpu.VMEM(padded, f32),
            pltpu.VMEM(padded, f32),
            pltpu.VMEM(padded, f32),
            pltpu.VMEM(padded, f32),
            pltpu.VMEM((2 * depth, 2 * depth), jnp.bfloat16),
            pltpu.VMEM((most, 2 * depth), jnp.bfloat16),
            pltpu.VMEM((most, 2 * depth), f32),
            pltpu.SemaphoreType.DMA((rows // CHUNK,)),
            pltpu.SemaphoreType.DMA((rows // CHUNK,)),
        ],
        compiler_params=pltpu.CompilerParams(vmem_limit_bytes=51 * 2**20),
        cost_estimate=pl.CostEstimate(
            flops=60_000_000, bytes_accessed=13_000_000, transcendentals=0
        ),
    )(adjoint, flux_terms)


def coefs_kernel(after, stiffness, normals, ids, out):
    del after
    rows, block, depth = stiffness.shape
    column = lax.broadcasted_iota(jnp.int32, (block, depth), 1)
    own = GROUP * lax.axis_index("inst")
    coefs = jnp.zeros((block, depth), jnp.float32)
    for x in range(rows):
        inverse = 1.0 / stiffness[x, :, 0:1]
        for d in range(3):
            here = normals[d, :, x : x + 1] * inverse
            coefs = jnp.where(column == own + d * rows + x, here, coefs)
        here = ids[:, x : x + 1].astype(jnp.float32)
        coefs = jnp.where(column == own + 3 * rows + x, here, coefs)
    out[0] = coefs


def add_kernel(keep, near, *rest):
    out = rest[-1]
    for d in range(out.shape[0]):
        for x in range(out.shape[1]):
            out[d, x] = keep[d, x] + near[d, x]


def near_kernel(over, over_near, face, face_near, coefs, coefs_near, wall, out):
    wall[0] = face[0] + face_near[0]
    wall[1] = coefs[0] + coefs_near[0]
    for i in range(2 * OVER):
        out[i] = over[i] + over_near[i]


def over_low(keep, over_near, far, i):
    return keep[i] + over_near[2 * OVER + i] + far[i]


def over_high(keep, over_near, far, i):
    return keep[OVER + i] + over_near[3 * OVER + i] + far[OVER + i]


def wall_kernel(near, far, out):
    for i in range(2):
        value = near[i] + far[i]
        for s in range(out.shape[0]):
            out[s, i] = value


def over_kernel(keep, over_near, far, after, inside, outside):
    del after
    even = lax.axis_index("space") % 2 == 0
    for i in range(OVER):
        low, high = (f(keep, over_near, far, i) for f in (over_low, over_high))
        inside[i] = jnp.where(even, high, low)
        outside[i] = jnp.where(even, low, high)


def design_kernel(scale, rows, walls, out):
    faces = [walls[s, 0] for s in range(walls.shape[0])]
    coefs = [walls[s, 1] for s in range(walls.shape[0])]
    spaces = len(faces)
    block, depth = faces[0].shape
    column = lax.broadcasted_iota(jnp.int32, (block, depth), 1) % GROUP
    at_low = functools.reduce(
        jnp.logical_or,
        [(column >= at) & (column < at + n) for at, n in zip(FACE_AT, REACHES)],
    )
    at_high = functools.reduce(
        jnp.logical_or,
        [
            (column >= at + rows - n) & (column < at + rows)
            for at, n in zip(FACE_AT, REACHES)
        ],
    )
    mine = (lax.axis_index("inst") * spaces + lax.axis_index("space")) * DV_DEV
    sums = [jnp.zeros((block, depth), jnp.float32) for _ in range(DV_DEV)]
    for s in range(spaces):
        whole = faces[s]
        if s > 0:
            whole = whole + jnp.where(at_low, pltpu.roll(faces[s - 1], depth - rows, 1), 0.0)
        if s < spaces - 1:
            whole = whole + jnp.where(at_high, pltpu.roll(faces[s + 1], rows, 1), 0.0)
        surface = jnp.zeros((block, depth), jnp.float32)
        for d in range(3):
            turned = pltpu.roll(coefs[s], depth - d * rows, 1) if d else coefs[s]
            surface = surface + pltpu.roll(whole, depth - FACE_AT[d], 1) * turned
        ids = pltpu.roll(coefs[s], depth - 3 * rows, 1).astype(jnp.int32) - mine
        ids = jnp.where(column < rows, ids, -1)
        for j in range(DV_DEV):
            sums[j] = sums[j] + jnp.where(ids == j, surface, 0.0)
    for j in range(DV_DEV):
        out[j] = jnp.sum(sums[j]) * scale


def last_kernel(scale, spaces, keep, near, far, stiffness, inside, across, out):
    rows = keep.shape[1]
    space = lax.axis_index("space")
    even = space % 2 == 0
    inner = (space > 0) & (space < spaces - 1)
    for x in range(rows):
        inverse = scale / stiffness[x]
        for d in range(3):
            value = keep[d, x] + near[d, x] + far[d, x]
            for at, side in (
                (LOW_AT[d] + x, even if x < REACHES[d] else None),
                (LOW_AT[d] + x - rows + REACHES[d], ~even if x >= rows - REACHES[d] else None),
            ):
                if side is not None:
                    outer = jnp.where(inner, across[at], 0.0)
                    value = value + jnp.where(side, outer, inside[at])
            out[d, x] = value * inverse


def per_device(adjoint, flux_terms, stiffness, normals, design_map):
    insts, spaces = lax.axis_size("inst"), lax.axis_size("space")
    rows, block, depth = stiffness.shape
    scale = 1.0 / (DIAG**3 * adjoint.shape[0] * insts)

    vmem = pl.BlockSpec(memory_space=pltpu.VMEM)

    def on_chip(kernel, shapes, *operands, weight=1):
        out = [jax.ShapeDtypeStruct(shape, jnp.float32) for shape in shapes]
        return pl.pallas_call(
            kernel,
            out_shape=out,
            in_specs=[vmem] * len(operands),
            out_specs=[vmem] * len(out),
            compiler_params=pltpu.CompilerParams(vmem_limit_bytes=4 * 2**20),
            cost_estimate=pl.CostEstimate(
                flops=500_000 * weight, bytes_accessed=1_500_000 * weight, transcendentals=0
            ),
        )(*operands)

    main_ko, main_kx, main_so, main_sx, over_ko, over_kx, over_s, face = front(
        adjoint, flux_terms
    )

    other_core = [(i, i ^ 1) for i in range(insts)]
    other_chip = [(i, i ^ 2) for i in range(insts)]

    plane = (1, block, depth)
    face_r = lax.ppermute(face, "inst", other_core)
    [coefs] = on_chip(
        coefs_kernel, [plane], face, stiffness, normals.transpose(0, 2, 1), design_map.T
    )
    coefs_r = lax.ppermute(coefs, "inst", other_core)
    over_r = lax.ppermute(over_s, "inst", other_core)
    main_r = lax.ppermute(main_sx, "inst", other_core)
    main_near = lax.ppermute(main_so, "inst", other_core)
    halo, plane = (OVER, block, depth), (2, block, depth)
    wall_near, over_x = on_chip(
        near_kernel, [plane, over_kx.shape], over_kx, over_r, face, face_r, coefs, coefs_r
    )
    wall_far = lax.ppermute(wall_near, "inst", other_chip)
    over_far = lax.ppermute(over_x, "inst", other_chip)
    [wall] = on_chip(wall_kernel, [(spaces,) + plane], wall_near, wall_far)
    walls = lax.all_to_all(wall, "space", 0, 0, tiled=True)
    [main_x] = on_chip(add_kernel, [main_kx.shape], main_kx, main_r, over_far, wall)
    main_far = lax.ppermute(main_x, "inst", other_chip)

    inside, across = on_chip(over_kernel, [halo, halo], over_ko, over_r, over_far, wall)
    inside = lax.ppermute(inside, "space", [(i, i ^ 1) for i in range(spaces)])
    across = lax.ppermute(
        across, "space", [(i, ((i + 1) ^ 1) - 1) for i in range(1, spaces - 1)]
    )
    design_grad = pl.pallas_call(
        functools.partial(design_kernel, scale, rows),
        out_shape=jax.ShapeDtypeStruct((DV_DEV,), jnp.float32),
        in_specs=[vmem],
        out_specs=pl.BlockSpec(memory_space=pltpu.SMEM),
        compiler_params=pltpu.CompilerParams(vmem_limit_bytes=4 * 2**20),
    )(walls)
    [mesh_adjoint] = on_chip(
        functools.partial(last_kernel, scale, spaces), [(3, rows, block, depth)],
        main_ko, main_near, main_far, stiffness, inside, across,
    )
    return (mesh_adjoint, design_grad)


def solution(mesh):
    in_specs = (
        P("inst", None, "space", None, None),
        P("inst", None, None, "space", None, None),
        P("space", "inst", None),
        P(None, "space", "inst"),
        P("space", "inst"),
    )
    out_specs = (P(None, "space", "inst", None), P(("inst", "space")))
    return jax.shard_map(
        per_device, mesh=mesh, in_specs=in_specs, out_specs=out_specs, check_vma=False
    )
```

```python
import functools
import jax
import jax.numpy as jnp
from jax import lax
from jax.experimental import pallas as pl
from jax.experimental.pallas import tpu as pltpu
from jax.sharding import PartitionSpec as P

DIAG = 6.5
DV_DEV = 8
REACH = 3
PAD = REACH + 1
CHUNK = 4
REACHES = (3, 2, 2)
LOW_AT = (0, 3, 5)
OVER = 7
GROUP = 64
FACE_AT = (REACH, 24, 44)


def shifted_rows(tiles, top, bottom):
    down = [pltpu.roll(t, 1, 0) for t in tiles]
    up = [pltpu.roll(t, 7, 0) for t in tiles]
    zero = jnp.zeros_like(tiles[0])
    down = [jnp.where(top, p, n) for p, n in zip([zero] + down[:-1], down)]
    up = [jnp.where(bottom, n, p) for p, n in zip(up, up[1:] + [zero])]
    return down, up


def front_kernel(
    adj_hbm, flux_hbm,
    main_ko, main_kx, main_so, main_sx, over_ko, over_kx, over_s, wall,
    adj, flux, work, metric, plane, side, band, stack, along, adj_sems, flux_sems,
):
    kinds, variables, rows, width, depth = adj.shape
    chunks = rows // CHUNK
    tiles = width // 8
    inst, space = lax.axis_index("inst"), lax.axis_index("space")
    low_open = jnp.where(space > 0, 1.0, 0.0)
    high_open = jnp.where(space < lax.axis_size("space") - 1, 1.0, 0.0)

    def adj_copy(i):
        part = pl.ds(i * CHUNK, CHUNK)
        return pltpu.make_async_copy(
            adj_hbm.at[:, :, part], adj.at[:, :, part], adj_sems.at[i]
        )

    def flux_copy(i):
        part = pl.ds(i * CHUNK, CHUNK)
        return pltpu.make_async_copy(
            flux_hbm.at[:, :, :, part], flux.at[:, :, :, part], flux_sems.at[i]
        )

    for i in range(chunks):
        adj_copy(i).start()
        flux_copy(i).start()

    near = jnp.abs(
        lax.broadcasted_iota(jnp.int32, (depth, depth), 0)
        - lax.broadcasted_iota(jnp.int32, (depth, depth), 1)
    )
    lane = lax.broadcasted_iota(jnp.int32, (depth, depth), 1)
    ends = jnp.where((lane == 0) | (lane == depth - 1), 1.0, 2.0)
    once = jnp.where(near == 1, 1.0, 0.0).astype(jnp.bfloat16)
    twice = jnp.where(near == 0, ends, jnp.where(near == 2, 1.0, 0.0)).astype(jnp.bfloat16)
    for half in (slice(0, depth), slice(depth, 2 * depth)):
        band[half, :depth] = once
        band[half, depth:] = twice
    zero = jnp.zeros((width, depth), jnp.float32)
    for d in range(3):
        for x in (-2, -1, rows, rows + 1):
            metric[d, x + PAD] = zero
            side[d, x + PAD] = zero
            plane[d, x + PAD] = zero
    for x in (-2, -1, rows, rows + 1):
        work[0, x + PAD] = zero

    row = lax.broadcasted_iota(jnp.int32, (8, depth), 0)
    top, bottom = row == 0, row == 7
    column = lax.broadcasted_iota(jnp.int32, (8, depth), 1)
    first, last = column == 0, column == depth - 1

    def weigh(x):
        for h in range(width // 16):
            part = slice(16 * h, 16 * h + 16)
            sums = [jnp.zeros((16, depth), jnp.float32) for _ in range(3)]
            for k in range(kinds):
                for v in range(variables):
                    a = adj[k, v, x, part].astype(jnp.float32)
                    for d in range(3):
                        sums[d] = sums[d] + a * flux[k, v, d, x, part].astype(jnp.float32)
            for d in range(3):
                work[d, x + PAD, part] = sums[d]

    def tile(t):
        return slice(8 * t, 8 * t + 8)

    def planes(slabs):
        count = len(slabs) * width
        for s, (d, x) in enumerate(slabs):
            r = x + PAD
            here = [work[d, r, tile(t)] for t in range(tiles)]
            if d == 0:
                open_ = jnp.where(x < 0, low_open, jnp.where(x >= rows, high_open, 1.0))
                low = [work[0, r - 1, tile(t)] for t in range(tiles)]
                high = [work[0, r + 1, tile(t)] for t in range(tiles)]
                m = [(h + 0.5 * (p - n)) * open_ for h, p, n in zip(here, low, high)]
            elif d == 1:
                low, high = shifted_rows(here, top, bottom)
                m = [h + 0.5 * (p - n) for h, p, n in zip(here, low, high)]
            else:
                m = [
                    h + 0.5 * (
                        jnp.where(first, 0.0, pltpu.roll(h, 1, 1))
                        - jnp.where(last, 0.0, pltpu.roll(h, depth - 1, 1))
                    )
                    for h in here
                ]
            for t in range(tiles):
                metric[d, r, tile(t)] = m[t]
            for t in range(0, tiles, 2):
                both = jnp.concatenate(m[t : t + 2], axis=0)
                rounded = both.astype(jnp.bfloat16)
                part = slice(s * width + 8 * t, s * width + 8 * t + 16)
                stack[part, :depth] = rounded
                stack[part, depth:] = (both - rounded.astype(jnp.float32)).astype(jnp.bfloat16)
        along[:count] = jnp.dot(stack[:count], band[...], preferred_element_type=jnp.float32)
        for s, (d, x) in enumerate(slabs):
            r = x + PAD
            at = s * width
            m = [metric[d, r, tile(t)] for t in range(tiles)]
            along_1 = [along[at + 8 * t : at + 8 * t + 8, :depth] for t in range(tiles)]
            along_2 = [along[at + 8 * t : at + 8 * t + 8, depth:] for t in range(tiles)]
            low, high = shifted_rows(m, top, bottom)
            once = [(p + n) + q for p, n, q in zip(low, high, along_1)]
            low, high = shifted_rows([o + q for o, q in zip(once, along_1)], top, bottom)
            returns = 2.0 - jnp.where(
                x == 0, 1.0 - low_open, jnp.where(x == rows - 1, 1.0 - high_open, 0.0)
            )
            weight = DIAG * DIAG + returns
            for t in range(tiles):
                side[d, r, tile(t)] = DIAG * m[t] + (once[t] + once[t])
                twice = (low[t] + high[t]) + along_2[t]
                plane[d, r, tile(t)] = weight * m[t] + DIAG * once[t] + twice

    def settle(i, extra):
        planes(
            [(1, i * CHUNK + j) for j in range(CHUNK)]
            + [(2, i * CHUNK + j) for j in range(CHUNK)]
            + [(0, i * CHUNK + j - 1) for j in range(CHUNK + extra)]
        )

    def arrive(i):
        adj_copy(i).wait()
        flux_copy(i).wait()

    arrive(0)
    for j in range(CHUNK):
        weigh(j)

    def stage(i, _):
        arrive(i)
        settle(i - 1, 0)
        for j in range(CHUNK):
            weigh(i * CHUNK + j)
        return 0

    lax.fori_loop(1, chunks, stage, 0)
    settle(chunks - 1, 2)

    def put(refs, index, place, total, face):
        for j, ref, shift in zip((0, 2, 1, 3), refs, (0, 0, 2 * OVER, 0)):
            b = inst ^ j
            at = pl.multiple_of(8 * b, 8)
            value = total(pl.ds(at, 8))
            if ref is over_s:
                ref[index + shift] = value
            else:
                ref[index] = value
            face = jnp.where(column == GROUP * b + place, value[:, 0:1], face)
        return face

    main_refs = (main_ko, main_kx, main_so, main_sx)
    over_refs = (over_ko, over_kx, over_s, over_s)

    def reached(d, x, part):
        r = x + PAD
        first, last = (PAD - 1, PAD + rows) if d == 0 else (PAD, PAD + rows - 1)
        terms = (
            [plane[d, r, part]] * (first <= r <= last)
            + [side[d, s, part] for s in (r - 1, r + 1) if first <= s <= last]
            + [metric[d, s, part] for s in (r - 2, r + 2) if first <= s <= last]
        )
        return functools.reduce(jnp.add, terms)

    face = jnp.zeros((8, depth), jnp.float32)
    for d in range(3):
        for x in range(-REACHES[d], 0):
            face = put(
                over_refs, LOW_AT[d] + x + REACHES[d], FACE_AT[d] + x,
                functools.partial(reached, d, x), face,
            )
        for x in range(rows, rows + REACHES[d]):
            face = put(
                over_refs, OVER + LOW_AT[d] + x - rows, FACE_AT[d] + x,
                functools.partial(reached, d, x), face,
            )

    def inner(x, face):
        r = x + PAD
        for d in range(3):

            def total(part):
                value = plane[d, r, part] + (side[d, r - 1, part] + side[d, r + 1, part])
                return value + (metric[d, r - 2, part] + metric[d, r + 2, part])

            face = put(main_refs, (d, x), FACE_AT[d] + x, total, face)
        return face

    face = lax.fori_loop(0, rows, inner, face, unroll=2)
    wall[0] = face


def front(adjoint, flux_terms):
    kinds, variables, rows, width, depth = adjoint.shape
    f32 = jnp.float32
    block = width // 4
    main = jax.ShapeDtypeStruct((3, rows, block, depth), f32)
    vmem = pl.BlockSpec(memory_space=pltpu.VMEM)
    hbm = pl.BlockSpec(memory_space=pltpu.HBM)
    padded = (3, rows + 2 * PAD, width, depth)
    most = (3 * CHUNK + 2) * width
    over_rows = (2 * OVER, 2 * OVER, 4 * OVER, 1)
    return pl.pallas_call(
        front_kernel,
        out_shape=[main] * 4
        + [jax.ShapeDtypeStruct((count, block, depth), f32) for count in over_rows],
        in_specs=[hbm] * 2,
        out_specs=[vmem] * 8,
        scratch_shapes=[
            pltpu.VMEM(adjoint.shape, adjoint.dtype),
            pltpu.VMEM(flux_terms.shape, flux_terms.dtype),
            pltpu.VMEM(padded, f32),
            pltpu.VMEM(padded, f32),
            pltpu.VMEM(padded, f32),
            pltpu.VMEM(padded, f32),
            pltpu.VMEM((2 * depth, 2 * depth), jnp.bfloat16),
            pltpu.VMEM((most, 2 * depth), jnp.bfloat16),
            pltpu.VMEM((most, 2 * depth), f32),
            pltpu.SemaphoreType.DMA((rows // CHUNK,)),
            pltpu.SemaphoreType.DMA((rows // CHUNK,)),
        ],
        compiler_params=pltpu.CompilerParams(vmem_limit_bytes=51 * 2**20),
        cost_estimate=pl.CostEstimate(
            flops=60_000_000, bytes_accessed=13_000_000, transcendentals=0
        ),
    )(adjoint, flux_terms)


def coefs_kernel(stiffness, normals, ids, after, out):
    del after
    rows, block, depth = stiffness.shape
    column = lax.broadcasted_iota(jnp.int32, (block, depth), 1)
    own = GROUP * lax.axis_index("inst")
    coefs = jnp.zeros((block, depth), jnp.float32)
    for x in range(rows):
        inverse = 1.0 / stiffness[x, :, 0:1]
        for d in range(3):
            here = normals[d, :, x : x + 1] * inverse
            coefs = jnp.where(column == own + d * rows + x, here, coefs)
        here = ids[:, x : x + 1].astype(jnp.float32)
        coefs = jnp.where(column == own + 3 * rows + x, here, coefs)
    out[0] = coefs


def add_kernel(keep, near, *rest):
    out = rest[-1]
    for d in range(out.shape[0]):
        for x in range(out.shape[1]):
            out[d, x] = keep[d, x] + near[d, x]


def wall_near_kernel(face, face_near, coefs, coefs_near, out):
    out[0] = face[0] + face_near[0]
    out[1] = coefs[0] + coefs_near[0]


def over_near_kernel(over, over_near, after, out):
    del after
    for i in range(2 * OVER):
        out[i] = over[i] + over_near[i]


def over_low(keep, over_near, far, i):
    return keep[i] + over_near[2 * OVER + i] + far[i]


def over_high(keep, over_near, far, i):
    return keep[OVER + i] + over_near[3 * OVER + i] + far[OVER + i]


def wall_kernel(near, far, after, out):
    del after
    for i in range(2):
        value = near[i] + far[i]
        for s in range(out.shape[0]):
            out[s, i] = value


def over_kernel(keep, over_near, far, after, inside, outside):
    del after
    even = lax.axis_index("space") % 2 == 0
    for i in range(OVER):
        low, high = (f(keep, over_near, far, i) for f in (over_low, over_high))
        inside[i] = jnp.where(even, high, low)
        outside[i] = jnp.where(even, low, high)


def design_kernel(scale, rows, walls, out):
    faces = [walls[s, 0] for s in range(walls.shape[0])]
    coefs = [walls[s, 1] for s in range(walls.shape[0])]
    spaces = len(faces)
    block, depth = faces[0].shape
    column = lax.broadcasted_iota(jnp.int32, (block, depth), 1) % GROUP
    at_low = functools.reduce(
        jnp.logical_or,
        [(column >= at) & (column < at + n) for at, n in zip(FACE_AT, REACHES)],
    )
    at_high = functools.reduce(
        jnp.logical_or,
        [
            (column >= at + rows - n) & (column < at + rows)
            for at, n in zip(FACE_AT, REACHES)
        ],
    )
    mine = (lax.axis_index("inst") * spaces + lax.axis_index("space")) * DV_DEV
    sums = [jnp.zeros((block, depth), jnp.float32) for _ in range(DV_DEV)]
    for s in range(spaces):
        whole = faces[s]
        if s > 0:
            whole = whole + jnp.where(at_low, pltpu.roll(faces[s - 1], depth - rows, 1), 0.0)
        if s < spaces - 1:
            whole = whole + jnp.where(at_high, pltpu.roll(faces[s + 1], rows, 1), 0.0)
        surface = jnp.zeros((block, depth), jnp.float32)
        for d in range(3):
            turned = pltpu.roll(coefs[s], depth - d * rows, 1) if d else coefs[s]
            surface = surface + pltpu.roll(whole, depth - FACE_AT[d], 1) * turned
        ids = pltpu.roll(coefs[s], depth - 3 * rows, 1).astype(jnp.int32) - mine
        ids = jnp.where(column < rows, ids, -1)
        for j in range(DV_DEV):
            sums[j] = sums[j] + jnp.where(ids == j, surface, 0.0)
    for j in range(DV_DEV):
        out[j] = jnp.sum(sums[j]) * scale


def last_kernel(scale, spaces, keep, near, far, stiffness, inside, across, out):
    rows = keep.shape[1]
    space = lax.axis_index("space")
    even = space % 2 == 0
    inner = (space > 0) & (space < spaces - 1)
    for x in range(rows):
        inverse = scale / stiffness[x]
        for d in range(3):
            value = keep[d, x] + near[d, x] + far[d, x]
            for at, side in (
                (LOW_AT[d] + x, even if x < REACHES[d] else None),
                (LOW_AT[d] + x - rows + REACHES[d], ~even if x >= rows - REACHES[d] else None),
            ):
                if side is not None:
                    outer = jnp.where(inner, across[at], 0.0)
                    value = value + jnp.where(side, outer, inside[at])
            out[d, x] = value * inverse


def per_device(adjoint, flux_terms, stiffness, normals, design_map):
    insts, spaces = lax.axis_size("inst"), lax.axis_size("space")
    rows, block, depth = stiffness.shape
    scale = 1.0 / (DIAG**3 * adjoint.shape[0] * insts)

    vmem = pl.BlockSpec(memory_space=pltpu.VMEM)

    def on_chip(kernel, shapes, *operands, after=()):
        out = [jax.ShapeDtypeStruct(shape, jnp.float32) for shape in shapes]
        return pl.pallas_call(
            kernel,
            out_shape=out,
            in_specs=[vmem] * len(operands) + [pl.BlockSpec(memory_space=pl.ANY)] * len(after),
            out_specs=[vmem] * len(out),
            compiler_params=pltpu.CompilerParams(vmem_limit_bytes=4 * 2**20),
            cost_estimate=pl.CostEstimate(
                flops=500_000, bytes_accessed=1_500_000, transcendentals=0
            ),
        )(*operands, *after)

    main_ko, main_kx, main_so, main_sx, over_ko, over_kx, over_s, face = front(
        adjoint, flux_terms
    )

    other_core = [(i, i ^ 1) for i in range(insts)]
    other_chip = [(i, i ^ 2) for i in range(insts)]

    plane = (1, block, depth)
    face_r = lax.ppermute(face, "inst", other_core)
    [coefs] = on_chip(
        coefs_kernel, [plane], stiffness, normals.transpose(0, 2, 1), design_map.T,
        after=[face],
    )
    coefs_r = lax.ppermute(coefs, "inst", other_core)
    over_r = lax.ppermute(over_s, "inst", other_core)
    main_r = lax.ppermute(main_sx, "inst", other_core)
    main_near = lax.ppermute(main_so, "inst", other_core)
    halo, plane = (OVER, block, depth), (2, block, depth)
    [wall_near] = on_chip(wall_near_kernel, [plane], face, face_r, coefs, coefs_r)
    wall_far = lax.ppermute(wall_near, "inst", other_chip)
    [over_x] = on_chip(
        over_near_kernel, [over_kx.shape], over_kx, over_r, after=[wall_near]
    )
    over_far = lax.ppermute(over_x, "inst", other_chip)
    [wall] = on_chip(
        wall_kernel, [(spaces,) + plane], wall_near, wall_far, after=[over_x]
    )
    walls = lax.all_to_all(wall, "space", 0, 0, tiled=True)
    [main_x] = on_chip(add_kernel, [main_kx.shape], main_kx, main_r, after=[wall, over_far])
    main_far = lax.ppermute(main_x, "inst", other_chip)

    inside, across = on_chip(
        over_kernel, [halo, halo], over_ko, over_r, over_far, after=[main_x]
    )
    inside = lax.ppermute(inside, "space", [(i, i ^ 1) for i in range(spaces)])
    across = lax.ppermute(
        across, "space", [(i, (((i + 1) ^ 1) - 1) % spaces) for i in range(spaces)]
    )
    design_grad = pl.pallas_call(
        functools.partial(design_kernel, scale, rows),
        out_shape=jax.ShapeDtypeStruct((DV_DEV,), jnp.float32),
        in_specs=[vmem],
        out_specs=pl.BlockSpec(memory_space=pltpu.SMEM),
        compiler_params=pltpu.CompilerParams(vmem_limit_bytes=4 * 2**20),
    )(walls)
    [mesh_adjoint] = on_chip(
        functools.partial(last_kernel, scale, spaces), [(3, rows, block, depth)],
        main_ko, main_near, main_far, stiffness, inside, across,
    )
    return (mesh_adjoint, design_grad)


def solution(mesh):
    in_specs = (
        P("inst", None, "space", None, None),
        P("inst", None, None, "space", None, None),
        P("space", "inst", None),
        P(None, "space", "inst"),
        P("space", "inst"),
    )
    out_specs = (P(None, "space", "inst", None), P(("inst", "space")))
    return jax.shard_map(
        per_device, mesh=mesh, in_specs=in_specs, out_specs=out_specs, check_vma=False
    )
```

```python
import functools
import jax
import jax.numpy as jnp
from jax import lax
from jax.experimental import pallas as pl
from jax.experimental.pallas import tpu as pltpu
from jax.sharding import PartitionSpec as P

DIAG = 6.5
DV_DEV = 8
REACH = 3
PAD = REACH + 1
CHUNK = 2
REACHES = (3, 2, 2)
LOW_AT = (0, 3, 5)
OVER = 7
GROUP = 64
FACE_AT = (REACH, 24, 44)


def shifted_rows(tiles, top, bottom):
    down = [pltpu.roll(t, 1, 0) for t in tiles]
    up = [pltpu.roll(t, 7, 0) for t in tiles]
    zero = jnp.zeros_like(tiles[0])
    down = [jnp.where(top, p, n) for p, n in zip([zero] + down[:-1], down)]
    up = [jnp.where(bottom, n, p) for p, n in zip(up, up[1:] + [zero])]
    return down, up


def front_kernel(
    adj_hbm, flux_hbm,
    main_ko, main_kx, main_so, main_sx, over_ko, over_kx, over_s, wall,
    adj, flux, work, metric, plane, side, band, stack, along, adj_sems, flux_sems,
):
    kinds, variables, rows, width, depth = adj.shape
    chunks = rows // CHUNK
    tiles = width // 8
    inst, space = lax.axis_index("inst"), lax.axis_index("space")
    low_open = jnp.where(space > 0, 1.0, 0.0)
    high_open = jnp.where(space < lax.axis_size("space") - 1, 1.0, 0.0)

    def adj_copy(i):
        part = pl.ds(i * CHUNK, CHUNK)
        return pltpu.make_async_copy(
            adj_hbm.at[:, :, part], adj.at[:, :, part], adj_sems.at[i]
        )

    def flux_copy(i):
        part = pl.ds(i * CHUNK, CHUNK)
        return pltpu.make_async_copy(
            flux_hbm.at[:, :, :, part], flux.at[:, :, :, part], flux_sems.at[i]
        )

    for i in range(chunks):
        adj_copy(i).start()
        flux_copy(i).start()

    near = jnp.abs(
        lax.broadcasted_iota(jnp.int32, (depth, depth), 0)
        - lax.broadcasted_iota(jnp.int32, (depth, depth), 1)
    )
    lane = lax.broadcasted_iota(jnp.int32, (depth, depth), 1)
    ends = jnp.where((lane == 0) | (lane == depth - 1), 1.0, 2.0)
    once = jnp.where(near == 1, 1.0, 0.0).astype(jnp.bfloat16)
    twice = jnp.where(near == 0, ends, jnp.where(near == 2, 1.0, 0.0)).astype(jnp.bfloat16)
    for half in (slice(0, depth), slice(depth, 2 * depth)):
        band[half, :depth] = once
        band[half, depth:] = twice
    zero = jnp.zeros((width, depth), jnp.float32)
    for d in range(3):
        for x in (-2, -1, rows, rows + 1):
            metric[d, x + PAD] = zero
            side[d, x + PAD] = zero
            plane[d, x + PAD] = zero
    for x in (-2, -1, rows, rows + 1):
        work[0, x + PAD] = zero

    row = lax.broadcasted_iota(jnp.int32, (8, depth), 0)
    top, bottom = row == 0, row == 7
    column = lax.broadcasted_iota(jnp.int32, (8, depth), 1)
    first, last = column == 0, column == depth - 1

    def weigh(x):
        for h in range(width // 16):
            part = slice(16 * h, 16 * h + 16)
            sums = [jnp.zeros((16, depth), jnp.float32) for _ in range(3)]
            for k in range(kinds):
                for v in range(variables):
                    a = adj[k, v, x, part].astype(jnp.float32)
                    for d in range(3):
                        sums[d] = sums[d] + a * flux[k, v, d, x, part].astype(jnp.float32)
            for d in range(3):
                work[d, x + PAD, part] = sums[d]

    def tile(t):
        return slice(8 * t, 8 * t + 8)

    def planes(slabs):
        count = len(slabs) * width
        for s, (d, x) in enumerate(slabs):
            r = x + PAD
            here = [work[d, r, tile(t)] for t in range(tiles)]
            if d == 0:
                open_ = jnp.where(x < 0, low_open, jnp.where(x >= rows, high_open, 1.0))
                low = [work[0, r - 1, tile(t)] for t in range(tiles)]
                high = [work[0, r + 1, tile(t)] for t in range(tiles)]
                m = [(h + 0.5 * (p - n)) * open_ for h, p, n in zip(here, low, high)]
            elif d == 1:
                low, high = shifted_rows(here, top, bottom)
                m = [h + 0.5 * (p - n) for h, p, n in zip(here, low, high)]
            else:
                m = [
                    h + 0.5 * (
                        jnp.where(first, 0.0, pltpu.roll(h, 1, 1))
                        - jnp.where(last, 0.0, pltpu.roll(h, depth - 1, 1))
                    )
                    for h in here
                ]
            for t in range(tiles):
                metric[d, r, tile(t)] = m[t]
            for t in range(0, tiles, 2):
                both = jnp.concatenate(m[t : t + 2], axis=0)
                rounded = both.astype(jnp.bfloat16)
                part = slice(s * width + 8 * t, s * width + 8 * t + 16)
                stack[part, :depth] = rounded
                stack[part, depth:] = (both - rounded.astype(jnp.float32)).astype(jnp.bfloat16)
        along[:count] = jnp.dot(stack[:count], band[...], preferred_element_type=jnp.float32)
        for s, (d, x) in enumerate(slabs):
            r = x + PAD
            at = s * width
            m = [metric[d, r, tile(t)] for t in range(tiles)]
            along_1 = [along[at + 8 * t : at + 8 * t + 8, :depth] for t in range(tiles)]
            along_2 = [along[at + 8 * t : at + 8 * t + 8, depth:] for t in range(tiles)]
            low, high = shifted_rows(m, top, bottom)
            once = [(p + n) + q for p, n, q in zip(low, high, along_1)]
            low, high = shifted_rows([o + q for o, q in zip(once, along_1)], top, bottom)
            returns = 2.0 - jnp.where(
                x == 0, 1.0 - low_open, jnp.where(x == rows - 1, 1.0 - high_open, 0.0)
            )
            weight = DIAG * DIAG + returns
            for t in range(tiles):
                side[d, r, tile(t)] = DIAG * m[t] + (once[t] + once[t])
                twice = (low[t] + high[t]) + along_2[t]
                plane[d, r, tile(t)] = weight * m[t] + DIAG * once[t] + twice

    def settle(i, extra):
        planes(
            [(1, i * CHUNK + j) for j in range(CHUNK)]
            + [(2, i * CHUNK + j) for j in range(CHUNK)]
            + [(0, i * CHUNK + j - 1) for j in range(CHUNK + extra)]
        )

    def arrive(i):
        adj_copy(i).wait()
        flux_copy(i).wait()

    arrive(0)
    for j in range(CHUNK):
        weigh(j)

    def stage(i, _):
        arrive(i)
        settle(i - 1, 0)
        for j in range(CHUNK):
            weigh(i * CHUNK + j)
        return 0

    lax.fori_loop(1, chunks, stage, 0)
    settle(chunks - 1, 2)

    def put(refs, index, place, total, face):
        for j, ref, shift in zip((0, 2, 1, 3), refs, (0, 0, 2 * OVER, 0)):
            b = inst ^ j
            at = pl.multiple_of(8 * b, 8)
            value = total(pl.ds(at, 8))
            if ref is over_s:
                ref[index + shift] = value
            else:
                ref[index] = value
            face = jnp.where(column == GROUP * b + place, value[:, 0:1], face)
        return face

    main_refs = (main_ko, main_kx, main_so, main_sx)
    over_refs = (over_ko, over_kx, over_s, over_s)

    def reached(d, x, part):
        r = x + PAD
        first, last = (PAD - 1, PAD + rows) if d == 0 else (PAD, PAD + rows - 1)
        terms = (
            [plane[d, r, part]] * (first <= r <= last)
            + [side[d, s, part] for s in (r - 1, r + 1) if first <= s <= last]
            + [metric[d, s, part] for s in (r - 2, r + 2) if first <= s <= last]
        )
        return functools.reduce(jnp.add, terms)

    face = jnp.zeros((8, depth), jnp.float32)
    for d in range(3):
        for x in range(-REACHES[d], 0):
            face = put(
                over_refs, LOW_AT[d] + x + REACHES[d], FACE_AT[d] + x,
                functools.partial(reached, d, x), face,
            )
        for x in range(rows, rows + REACHES[d]):
            face = put(
                over_refs, OVER + LOW_AT[d] + x - rows, FACE_AT[d] + x,
                functools.partial(reached, d, x), face,
            )

    def inner(x, face):
        r = x + PAD
        for d in range(3):

            def total(part):
                value = plane[d, r, part] + (side[d, r - 1, part] + side[d, r + 1, part])
                return value + (metric[d, r - 2, part] + metric[d, r + 2, part])

            face = put(main_refs, (d, x), FACE_AT[d] + x, total, face)
        return face

    face = lax.fori_loop(0, rows, inner, face, unroll=2)
    wall[0] = face


def front(adjoint, flux_terms):
    kinds, variables, rows, width, depth = adjoint.shape
    f32 = jnp.float32
    block = width // 4
    main = jax.ShapeDtypeStruct((3, rows, block, depth), f32)
    vmem = pl.BlockSpec(memory_space=pltpu.VMEM)
    hbm = pl.BlockSpec(memory_space=pltpu.HBM)
    padded = (3, rows + 2 * PAD, width, depth)
    most = (3 * CHUNK + 2) * width
    over_rows = (2 * OVER, 2 * OVER, 4 * OVER, 1)
    return pl.pallas_call(
        front_kernel,
        out_shape=[main] * 4
        + [jax.ShapeDtypeStruct((count, block, depth), f32) for count in over_rows],
        in_specs=[hbm] * 2,
        out_specs=[vmem] * 8,
        scratch_shapes=[
            pltpu.VMEM(adjoint.shape, adjoint.dtype),
            pltpu.VMEM(flux_terms.shape, flux_terms.dtype),
            pltpu.VMEM(padded, f32),
            pltpu.VMEM(padded, f32),
            pltpu.VMEM(padded, f32),
            pltpu.VMEM(padded, f32),
            pltpu.VMEM((2 * depth, 2 * depth), jnp.bfloat16),
            pltpu.VMEM((most, 2 * depth), jnp.bfloat16),
            pltpu.VMEM((most, 2 * depth), f32),
            pltpu.SemaphoreType.DMA((rows // CHUNK,)),
            pltpu.SemaphoreType.DMA((rows // CHUNK,)),
        ],
        compiler_params=pltpu.CompilerParams(vmem_limit_bytes=51 * 2**20),
        cost_estimate=pl.CostEstimate(
            flops=60_000_000, bytes_accessed=13_000_000, transcendentals=0
        ),
    )(adjoint, flux_terms)


def coefs_kernel(stiffness, normals, ids, after, out):
    del after
    rows, block, depth = stiffness.shape
    column = lax.broadcasted_iota(jnp.int32, (block, depth), 1)
    own = GROUP * lax.axis_index("inst")
    coefs = jnp.zeros((block, depth), jnp.float32)
    for x in range(rows):
        inverse = 1.0 / stiffness[x, :, 0:1]
        for d in range(3):
            here = normals[d, :, x : x + 1] * inverse
            coefs = jnp.where(column == own + d * rows + x, here, coefs)
        here = ids[:, x : x + 1].astype(jnp.float32)
        coefs = jnp.where(column == own + 3 * rows + x, here, coefs)
    out[0] = coefs


def add_kernel(keep, near, *rest):
    out = rest[-1]
    for d in range(out.shape[0]):
        for x in range(out.shape[1]):
            out[d, x] = keep[d, x] + near[d, x]


def wall_near_kernel(face, face_near, coefs, coefs_near, out):
    out[0] = face[0] + face_near[0]
    out[1] = coefs[0] + coefs_near[0]


def over_near_kernel(over, over_near, after, out):
    del after
    for i in range(2 * OVER):
        out[i] = over[i] + over_near[i]


def over_low(keep, over_near, far, i):
    return keep[i] + over_near[2 * OVER + i] + far[i]


def over_high(keep, over_near, far, i):
    return keep[OVER + i] + over_near[3 * OVER + i] + far[OVER + i]


def wall_kernel(near, far, after, out):
    del after
    for i in range(2):
        value = near[i] + far[i]
        for s in range(out.shape[0]):
            out[s, i] = value


def over_kernel(keep, over_near, far, after, inside, outside):
    del after
    even = lax.axis_index("space") % 2 == 0
    for i in range(OVER):
        low, high = (f(keep, over_near, far, i) for f in (over_low, over_high))
        inside[i] = jnp.where(even, high, low)
        outside[i] = jnp.where(even, low, high)


def design_sums(scale, rows, walls, out):
    faces = [walls[s, 0] for s in range(walls.shape[0])]
    coefs = [walls[s, 1] for s in range(walls.shape[0])]
    spaces = len(faces)
    block, depth = faces[0].shape
    column = lax.broadcasted_iota(jnp.int32, (block, depth), 1) % GROUP
    at_low = functools.reduce(
        jnp.logical_or,
        [(column >= at) & (column < at + n) for at, n in zip(FACE_AT, REACHES)],
    )
    at_high = functools.reduce(
        jnp.logical_or,
        [
            (column >= at + rows - n) & (column < at + rows)
            for at, n in zip(FACE_AT, REACHES)
        ],
    )
    mine = (lax.axis_index("inst") * spaces + lax.axis_index("space")) * DV_DEV
    sums = [jnp.zeros((block, depth), jnp.float32) for _ in range(DV_DEV)]
    for s in range(spaces):
        whole = faces[s]
        if s > 0:
            whole = whole + jnp.where(at_low, pltpu.roll(faces[s - 1], depth - rows, 1), 0.0)
        if s < spaces - 1:
            whole = whole + jnp.where(at_high, pltpu.roll(faces[s + 1], rows, 1), 0.0)
        surface = jnp.zeros((block, depth), jnp.float32)
        for d in range(3):
            turned = pltpu.roll(coefs[s], depth - d * rows, 1) if d else coefs[s]
            surface = surface + pltpu.roll(whole, depth - FACE_AT[d], 1) * turned
        ids = pltpu.roll(coefs[s], depth - 3 * rows, 1).astype(jnp.int32) - mine
        ids = jnp.where(column < rows, ids, -1)
        for j in range(DV_DEV):
            sums[j] = sums[j] + jnp.where(ids == j, surface, 0.0)
    for j in range(DV_DEV):
        out[j] = jnp.sum(sums[j]) * scale


def last_kernel(
    scale, spaces, keep, near, far, stiffness, inside, across, walls_ref,
    out, design, walls, sem,
):
    rows = keep.shape[1]
    copy = pltpu.make_async_copy(walls_ref, walls, sem)
    copy.start()
    space = lax.axis_index("space")
    even = space % 2 == 0
    inner = (space > 0) & (space < spaces - 1)
    for x in range(rows):
        inverse = scale / stiffness[x]
        for d in range(3):
            value = keep[d, x] + near[d, x] + far[d, x]
            for at, side in (
                (LOW_AT[d] + x, even if x < REACHES[d] else None),
                (LOW_AT[d] + x - rows + REACHES[d], ~even if x >= rows - REACHES[d] else None),
            ):
                if side is not None:
                    outer = jnp.where(inner, across[at], 0.0)
                    value = value + jnp.where(side, outer, inside[at])
            out[d, x] = value * inverse
    copy.wait()
    design_sums(scale, rows, walls, design)


def per_device(adjoint, flux_terms, stiffness, normals, design_map):
    insts, spaces = lax.axis_size("inst"), lax.axis_size("space")
    rows, block, depth = stiffness.shape
    scale = 1.0 / (DIAG**3 * adjoint.shape[0] * insts)

    vmem = pl.BlockSpec(memory_space=pltpu.VMEM)

    def on_chip(kernel, shapes, *operands, after=()):
        out = [jax.ShapeDtypeStruct(shape, jnp.float32) for shape in shapes]
        return pl.pallas_call(
            kernel,
            out_shape=out,
            in_specs=[vmem] * len(operands) + [pl.BlockSpec(memory_space=pl.ANY)] * len(after),
            out_specs=[vmem] * len(out),
            compiler_params=pltpu.CompilerParams(vmem_limit_bytes=4 * 2**20),
            cost_estimate=pl.CostEstimate(
                flops=500_000, bytes_accessed=1_500_000, transcendentals=0
            ),
        )(*operands, *after)

    main_ko, main_kx, main_so, main_sx, over_ko, over_kx, over_s, face = front(
        adjoint, flux_terms
    )

    other_core = [(i, i ^ 1) for i in range(insts)]
    other_chip = [(i, i ^ 2) for i in range(insts)]

    plane = (1, block, depth)
    face_r = lax.ppermute(face, "inst", other_core)
    [coefs] = on_chip(
        coefs_kernel, [plane], stiffness, normals.transpose(0, 2, 1), design_map.T,
        after=[face],
    )
    coefs_r = lax.ppermute(coefs, "inst", other_core)
    over_r = lax.ppermute(over_s, "inst", other_core)
    main_r = lax.ppermute(main_sx, "inst", other_core)
    main_near = lax.ppermute(main_so, "inst", other_core)
    halo, plane = (OVER, block, depth), (2, block, depth)
    [wall_near] = on_chip(wall_near_kernel, [plane], face, face_r, coefs, coefs_r)
    wall_far = lax.ppermute(wall_near, "inst", other_chip)
    [over_x] = on_chip(
        over_near_kernel, [over_kx.shape], over_kx, over_r, after=[wall_near]
    )
    over_far = lax.ppermute(over_x, "inst", other_chip)
    [wall] = on_chip(
        wall_kernel, [(spaces,) + plane], wall_near, wall_far, after=[over_x]
    )
    walls = lax.all_to_all(wall, "space", 0, 0, tiled=True)
    [main_x] = on_chip(add_kernel, [main_kx.shape], main_kx, main_r, after=[wall, over_far])
    main_far = lax.ppermute(main_x, "inst", other_chip)

    inside, across = on_chip(
        over_kernel, [halo, halo], over_ko, over_r, over_far, after=[main_x]
    )
    inside = lax.ppermute(inside, "space", [(i, i ^ 1) for i in range(spaces)])
    across = lax.ppermute(
        across, "space", [(i, (((i + 1) ^ 1) - 1) % spaces) for i in range(spaces)]
    )
    mesh_adjoint, design_grad = pl.pallas_call(
        functools.partial(last_kernel, scale, spaces),
        out_shape=[
            jax.ShapeDtypeStruct((3, rows, block, depth), jnp.float32),
            jax.ShapeDtypeStruct((DV_DEV,), jnp.float32),
        ],
        in_specs=[vmem] * 6 + [pl.BlockSpec(memory_space=pl.ANY)],
        out_specs=[vmem, pl.BlockSpec(memory_space=pltpu.SMEM)],
        scratch_shapes=[
            pltpu.VMEM(walls.shape, jnp.float32),
            pltpu.SemaphoreType.DMA(()),
        ],
        compiler_params=pltpu.CompilerParams(vmem_limit_bytes=6 * 2**20),
    )(main_ko, main_near, main_far, stiffness, inside, across, walls)
    return (mesh_adjoint, design_grad)


def solution(mesh):
    in_specs = (
        P("inst", None, "space", None, None),
        P("inst", None, None, "space", None, None),
        P("space", "inst", None),
        P(None, "space", "inst"),
        P("space", "inst"),
    )
    out_specs = (P(None, "space", "inst", None), P(("inst", "space")))
    return jax.shard_map(
        per_device, mesh=mesh, in_specs=in_specs, out_specs=out_specs, check_vma=False
    )
```

```python
import functools
import jax
import jax.numpy as jnp
from jax import lax
from jax.experimental import pallas as pl
from jax.experimental.pallas import tpu as pltpu
from jax.sharding import PartitionSpec as P

DIAG = 6.5
DV_DEV = 8
REACH = 3
PAD = REACH + 1
CHUNK = 2
REACHES = (3, 2, 2)
LOW_AT = (0, 3, 5)
OVER = 7
FACE = 2 * OVER
GROUP = 64
FACE_AT = (REACH, 24, 44)


def shifted_rows(tiles, top, bottom):
    down = [pltpu.roll(t, 1, 0) for t in tiles]
    up = [pltpu.roll(t, 7, 0) for t in tiles]
    zero = jnp.zeros_like(tiles[0])
    down = [jnp.where(top, p, n) for p, n in zip([zero] + down[:-1], down)]
    up = [jnp.where(bottom, n, p) for p, n in zip(up, up[1:] + [zero])]
    return down, up


def front_kernel(
    adj_hbm, flux_hbm,
    main_ko, main_kx, main_so, main_sx, over_ko, over_kx, over_s, wall,
    adj, flux, work, metric, plane, side, band, stack, along, adj_sems, flux_sems,
):
    kinds, variables, rows, width, depth = adj.shape
    chunks = rows // CHUNK
    tiles = width // 8
    inst, space = lax.axis_index("inst"), lax.axis_index("space")
    low_open = jnp.where(space > 0, 1.0, 0.0)
    high_open = jnp.where(space < lax.axis_size("space") - 1, 1.0, 0.0)

    def adj_copy(i):
        part = pl.ds(i * CHUNK, CHUNK)
        return pltpu.make_async_copy(
            adj_hbm.at[:, :, part], adj.at[:, :, part], adj_sems.at[i]
        )

    def flux_copy(i):
        part = pl.ds(i * CHUNK, CHUNK)
        return pltpu.make_async_copy(
            flux_hbm.at[:, :, :, part], flux.at[:, :, :, part], flux_sems.at[i]
        )

    for i in range(chunks):
        adj_copy(i).start()
        flux_copy(i).start()

    near = jnp.abs(
        lax.broadcasted_iota(jnp.int32, (depth, depth), 0)
        - lax.broadcasted_iota(jnp.int32, (depth, depth), 1)
    )
    lane = lax.broadcasted_iota(jnp.int32, (depth, depth), 1)
    ends = jnp.where((lane == 0) | (lane == depth - 1), 1.0, 2.0)
    once = jnp.where(near == 1, 1.0, 0.0).astype(jnp.bfloat16)
    twice = jnp.where(near == 0, ends, jnp.where(near == 2, 1.0, 0.0)).astype(jnp.bfloat16)
    for half in (slice(0, depth), slice(depth, 2 * depth)):
        band[half, :depth] = once
        band[half, depth:] = twice
    zero = jnp.zeros((width, depth), jnp.float32)
    for d in range(3):
        for x in (-2, -1, rows, rows + 1):
            metric[d, x + PAD] = zero
            side[d, x + PAD] = zero
            plane[d, x + PAD] = zero
    for x in (-2, -1, rows, rows + 1):
        work[0, x + PAD] = zero

    row = lax.broadcasted_iota(jnp.int32, (8, depth), 0)
    top, bottom = row == 0, row == 7
    column = lax.broadcasted_iota(jnp.int32, (8, depth), 1)
    first, last = column == 0, column == depth - 1

    def weigh(x):
        for h in range(width // 16):
            part = slice(16 * h, 16 * h + 16)
            sums = [jnp.zeros((16, depth), jnp.float32) for _ in range(3)]
            for k in range(kinds):
                for v in range(variables):
                    a = adj[k, v, x, part].astype(jnp.float32)
                    for d in range(3):
                        sums[d] = sums[d] + a * flux[k, v, d, x, part].astype(jnp.float32)
            for d in range(3):
                work[d, x + PAD, part] = sums[d]

    def tile(t):
        return slice(8 * t, 8 * t + 8)

    def planes(slabs):
        count = len(slabs) * width
        for s, (d, x) in enumerate(slabs):
            r = x + PAD
            here = [work[d, r, tile(t)] for t in range(tiles)]
            if d == 0:
                open_ = jnp.where(x < 0, low_open, jnp.where(x >= rows, high_open, 1.0))
                low = [work[0, r - 1, tile(t)] for t in range(tiles)]
                high = [work[0, r + 1, tile(t)] for t in range(tiles)]
                m = [(h + 0.5 * (p - n)) * open_ for h, p, n in zip(here, low, high)]
            elif d == 1:
                low, high = shifted_rows(here, top, bottom)
                m = [h + 0.5 * (p - n) for h, p, n in zip(here, low, high)]
            else:
                m = [
                    h + 0.5 * (
                        jnp.where(first, 0.0, pltpu.roll(h, 1, 1))
                        - jnp.where(last, 0.0, pltpu.roll(h, depth - 1, 1))
                    )
                    for h in here
                ]
            for t in range(tiles):
                metric[d, r, tile(t)] = m[t]
            for t in range(0, tiles, 2):
                both = jnp.concatenate(m[t : t + 2], axis=0)
                rounded = both.astype(jnp.bfloat16)
                part = slice(s * width + 8 * t, s * width + 8 * t + 16)
                stack[part, :depth] = rounded
                stack[part, depth:] = (both - rounded.astype(jnp.float32)).astype(jnp.bfloat16)
        along[:count] = jnp.dot(stack[:count], band[...], preferred_element_type=jnp.float32)
        for s, (d, x) in enumerate(slabs):
            r = x + PAD
            at = s * width
            m = [metric[d, r, tile(t)] for t in range(tiles)]
            along_1 = [along[at + 8 * t : at + 8 * t + 8, :depth] for t in range(tiles)]
            along_2 = [along[at + 8 * t : at + 8 * t + 8, depth:] for t in range(tiles)]
            low, high = shifted_rows(m, top, bottom)
            once = [(p + n) + q for p, n, q in zip(low, high, along_1)]
            low, high = shifted_rows([o + q for o, q in zip(once, along_1)], top, bottom)
            returns = 2.0 - jnp.where(
                x == 0, 1.0 - low_open, jnp.where(x == rows - 1, 1.0 - high_open, 0.0)
            )
            weight = DIAG * DIAG + returns
            for t in range(tiles):
                side[d, r, tile(t)] = DIAG * m[t] + (once[t] + once[t])
                twice = (low[t] + high[t]) + along_2[t]
                plane[d, r, tile(t)] = weight * m[t] + DIAG * once[t] + twice

    def settle(i, extra):
        planes(
            [(1, i * CHUNK + j) for j in range(CHUNK)]
            + [(2, i * CHUNK + j) for j in range(CHUNK)]
            + [(0, i * CHUNK + j - 1) for j in range(CHUNK + extra)]
        )

    def arrive(i):
        adj_copy(i).wait()
        flux_copy(i).wait()

    arrive(0)
    for j in range(CHUNK):
        weigh(j)

    def stage(i, _):
        arrive(i)
        settle(i - 1, 0)
        for j in range(CHUNK):
            weigh(i * CHUNK + j)
        return 0

    lax.fori_loop(1, chunks, stage, 0)
    settle(chunks - 1, 2)

    def put(refs, index, place, total, face):
        for j, ref, shift in zip((0, 2, 1, 3), refs, (0, 0, 2 * OVER, 0)):
            b = inst ^ j
            at = pl.multiple_of(8 * b, 8)
            value = total(pl.ds(at, 8))
            if ref is over_s:
                ref[index + shift] = value
            else:
                ref[index] = value
            face = jnp.where(column == GROUP * b + place, value[:, 0:1], face)
        return face

    main_refs = (main_ko, main_kx, main_so, main_sx)
    over_refs = (over_ko, over_kx, over_s, over_s)

    def reached(d, x, part):
        r = x + PAD
        first, last = (PAD - 1, PAD + rows) if d == 0 else (PAD, PAD + rows - 1)
        terms = (
            [plane[d, r, part]] * (first <= r <= last)
            + [side[d, s, part] for s in (r - 1, r + 1) if first <= s <= last]
            + [metric[d, s, part] for s in (r - 2, r + 2) if first <= s <= last]
        )
        return functools.reduce(jnp.add, terms)

    face = jnp.zeros((8, depth), jnp.float32)
    for d in range(3):
        for x in range(-REACHES[d], 0):
            face = put(
                over_refs, LOW_AT[d] + x + REACHES[d], FACE_AT[d] + x,
                functools.partial(reached, d, x), face,
            )
        for x in range(rows, rows + REACHES[d]):
            face = put(
                over_refs, OVER + LOW_AT[d] + x - rows, FACE_AT[d] + x,
                functools.partial(reached, d, x), face,
            )

    def inner(x, face):
        r = x + PAD
        for d in range(3):

            def total(part):
                value = plane[d, r, part] + (side[d, r - 1, part] + side[d, r + 1, part])
                return value + (metric[d, r - 2, part] + metric[d, r + 2, part])

            face = put(main_refs, (d, x), FACE_AT[d] + x, total, face)
        return face

    face = lax.fori_loop(0, rows, inner, face, unroll=2)
    wall[0] = face


def front(adjoint, flux_terms):
    kinds, variables, rows, width, depth = adjoint.shape
    f32 = jnp.float32
    block = width // 4
    main = jax.ShapeDtypeStruct((3, rows, block, depth), f32)
    vmem = pl.BlockSpec(memory_space=pltpu.VMEM)
    hbm = pl.BlockSpec(memory_space=pltpu.HBM)
    padded = (3, rows + 2 * PAD, width, depth)
    most = (3 * CHUNK + 2) * width
    over_rows = (2 * OVER, 2 * OVER, 4 * OVER, 1)
    return pl.pallas_call(
        front_kernel,
        out_shape=[main] * 4
        + [jax.ShapeDtypeStruct((count, block, depth), f32) for count in over_rows],
        in_specs=[hbm] * 2,
        out_specs=[vmem] * 8,
        scratch_shapes=[
            pltpu.VMEM(adjoint.shape, adjoint.dtype),
            pltpu.VMEM(flux_terms.shape, flux_terms.dtype),
            pltpu.VMEM(padded, f32),
            pltpu.VMEM(padded, f32),
            pltpu.VMEM(padded, f32),
            pltpu.VMEM(padded, f32),
            pltpu.VMEM((2 * depth, 2 * depth), jnp.bfloat16),
            pltpu.VMEM((most, 2 * depth), jnp.bfloat16),
            pltpu.VMEM((most, 2 * depth), f32),
            pltpu.SemaphoreType.DMA((rows // CHUNK,)),
            pltpu.SemaphoreType.DMA((rows // CHUNK,)),
        ],
        compiler_params=pltpu.CompilerParams(vmem_limit_bytes=51 * 2**20),
        cost_estimate=pl.CostEstimate(
            flops=60_000_000, bytes_accessed=13_000_000, transcendentals=0
        ),
    )(adjoint, flux_terms)


def coefs_kernel(stiffness, normals, ids, after, out):
    del after
    rows, block, depth = stiffness.shape
    column = lax.broadcasted_iota(jnp.int32, (block, depth), 1)
    own = GROUP * lax.axis_index("inst")
    coefs = jnp.zeros((block, depth), jnp.float32)
    for x in range(rows):
        inverse = 1.0 / stiffness[x, :, 0:1]
        for d in range(3):
            here = normals[d, :, x : x + 1] * inverse
            coefs = jnp.where(column == own + d * rows + x, here, coefs)
        here = ids[:, x : x + 1].astype(jnp.float32)
        coefs = jnp.where(column == own + 3 * rows + x, here, coefs)
    out[0] = coefs


def add_kernel(keep, near, after, *out):
    del after
    for d in range(3):
        for x in range(keep.shape[1]):
            out[d][x] = keep[d, x] + near[d, x]


def near_kernel(over, over_near, face, face_near, coefs, coefs_near, out):
    for i in range(2 * OVER):
        out[i] = over[i] + over_near[i]
    out[FACE] = face[0] + face_near[0]
    out[FACE + 1] = coefs[0] + coefs_near[0]


def over_low(keep, over_near, far, i):
    return keep[i] + over_near[2 * OVER + i] + far[i]


def over_high(keep, over_near, far, i):
    return keep[OVER + i] + over_near[3 * OVER + i] + far[OVER + i]


def wall_kernel(near, far, *rest):
    out = rest[-1]
    for i in range(2):
        value = near[FACE + i] + far[FACE + i]
        for s in range(out.shape[0]):
            out[s, i] = value


def over_kernel(keep, over_near, far, after, inside, outside):
    del after
    even = lax.axis_index("space") % 2 == 0
    for i in range(OVER):
        low, high = (f(keep, over_near, far, i) for f in (over_low, over_high))
        inside[i] = jnp.where(even, high, low)
        outside[i] = jnp.where(even, low, high)


def design_sums(scale, rows, walls, out):
    faces = [walls[s, 0] for s in range(walls.shape[0])]
    coefs = [walls[s, 1] for s in range(walls.shape[0])]
    spaces = len(faces)
    block, depth = faces[0].shape
    column = lax.broadcasted_iota(jnp.int32, (block, depth), 1) % GROUP
    at_low = functools.reduce(
        jnp.logical_or,
        [(column >= at) & (column < at + n) for at, n in zip(FACE_AT, REACHES)],
    )
    at_high = functools.reduce(
        jnp.logical_or,
        [
            (column >= at + rows - n) & (column < at + rows)
            for at, n in zip(FACE_AT, REACHES)
        ],
    )
    mine = (lax.axis_index("inst") * spaces + lax.axis_index("space")) * DV_DEV
    sums = [jnp.zeros((block, depth), jnp.float32) for _ in range(DV_DEV)]
    for s in range(spaces):
        whole = faces[s]
        if s > 0:
            whole = whole + jnp.where(at_low, pltpu.roll(faces[s - 1], depth - rows, 1), 0.0)
        if s < spaces - 1:
            whole = whole + jnp.where(at_high, pltpu.roll(faces[s + 1], rows, 1), 0.0)
        surface = jnp.zeros((block, depth), jnp.float32)
        for d in range(3):
            turned = pltpu.roll(coefs[s], depth - d * rows, 1) if d else coefs[s]
            surface = surface + pltpu.roll(whole, depth - FACE_AT[d], 1) * turned
        ids = pltpu.roll(coefs[s], depth - 3 * rows, 1).astype(jnp.int32) - mine
        ids = jnp.where(column < rows, ids, -1)
        for j in range(DV_DEV):
            sums[j] = sums[j] + jnp.where(ids == j, surface, 0.0)
    for j in range(DV_DEV):
        out[j] = jnp.sum(sums[j]) * scale


def last_kernel(
    scale, spaces, keep, near, far_0, far_1, far_2, stiffness, inside, across, walls_ref,
    out, design, walls, sem,
):
    rows = keep.shape[1]
    far = (far_0, far_1, far_2)
    copy = pltpu.make_async_copy(walls_ref, walls, sem)
    copy.start()
    space = lax.axis_index("space")
    even = space % 2 == 0
    inner = (space > 0) & (space < spaces - 1)
    for x in range(rows):
        inverse = scale / stiffness[x]
        for d in range(3):
            value = keep[d, x] + near[d, x] + far[d][x]
            for at, side in (
                (LOW_AT[d] + x, even if x < REACHES[d] else None),
                (LOW_AT[d] + x - rows + REACHES[d], ~even if x >= rows - REACHES[d] else None),
            ):
                if side is not None:
                    outer = jnp.where(inner, across[at], 0.0)
                    value = value + jnp.where(side, outer, inside[at])
            out[d, x] = value * inverse
    copy.wait()
    design_sums(scale, rows, walls, design)


def per_device(adjoint, flux_terms, stiffness, normals, design_map):
    insts, spaces = lax.axis_size("inst"), lax.axis_size("space")
    rows, block, depth = stiffness.shape
    scale = 1.0 / (DIAG**3 * adjoint.shape[0] * insts)

    vmem = pl.BlockSpec(memory_space=pltpu.VMEM)

    def on_chip(kernel, shapes, *operands, after=()):
        out = [jax.ShapeDtypeStruct(shape, jnp.float32) for shape in shapes]
        return pl.pallas_call(
            kernel,
            out_shape=out,
            in_specs=[vmem] * len(operands) + [pl.BlockSpec(memory_space=pl.ANY)] * len(after),
            out_specs=[vmem] * len(out),
            compiler_params=pltpu.CompilerParams(vmem_limit_bytes=4 * 2**20),
            cost_estimate=pl.CostEstimate(
                flops=500_000, bytes_accessed=1_500_000, transcendentals=0
            ),
        )(*operands, *after)

    main_ko, main_kx, main_so, main_sx, over_ko, over_kx, over_s, face = front(
        adjoint, flux_terms
    )

    other_core = [(i, i ^ 1) for i in range(insts)]
    other_chip = [(i, i ^ 2) for i in range(insts)]

    plane = (1, block, depth)
    face_r = lax.ppermute(face, "inst", other_core)
    [coefs] = on_chip(
        coefs_kernel, [plane], stiffness, normals.transpose(0, 2, 1), design_map.T,
        after=[face],
    )
    coefs_r = lax.ppermute(coefs, "inst", other_core)
    over_r = lax.ppermute(over_s, "inst", other_core)
    main_r = lax.ppermute(main_sx, "inst", other_core)
    main_near = lax.ppermute(main_so, "inst", other_core)
    halo = (OVER, block, depth)
    [near] = on_chip(
        near_kernel, [(FACE + 2, block, depth)], over_kx, over_r, face, face_r, coefs, coefs_r
    )
    far = lax.ppermute(near, "inst", other_chip)
    main_x = on_chip(add_kernel, [main_kx.shape[1:]] * 3, main_kx, main_r, after=[near])
    main_far = [lax.ppermute(part, "inst", other_chip) for part in main_x]
    [wall] = on_chip(wall_kernel, [(spaces, 2, block, depth)], near, far, after=main_x)
    walls = lax.all_to_all(wall, "space", 0, 0, tiled=True)

    inside, across = on_chip(
        over_kernel, [halo, halo], over_ko, over_r, far, after=[wall]
    )
    inside = lax.ppermute(inside, "space", [(i, i ^ 1) for i in range(spaces)])
    across = lax.ppermute(
        across, "space", [(i, (((i + 1) ^ 1) - 1) % spaces) for i in range(spaces)]
    )
    mesh_adjoint, design_grad = pl.pallas_call(
        functools.partial(last_kernel, scale, spaces),
        out_shape=[
            jax.ShapeDtypeStruct((3, rows, block, depth), jnp.float32),
            jax.ShapeDtypeStruct((DV_DEV,), jnp.float32),
        ],
        in_specs=[vmem] * 8 + [pl.BlockSpec(memory_space=pl.ANY)],
        out_specs=[vmem, pl.BlockSpec(memory_space=pltpu.SMEM)],
        scratch_shapes=[
            pltpu.VMEM(walls.shape, jnp.float32),
            pltpu.SemaphoreType.DMA(()),
        ],
        compiler_params=pltpu.CompilerParams(vmem_limit_bytes=6 * 2**20),
    )(main_ko, main_near, *main_far, stiffness, inside, across, walls)
    return (mesh_adjoint, design_grad)


def solution(mesh):
    in_specs = (
        P("inst", None, "space", None, None),
        P("inst", None, None, "space", None, None),
        P("space", "inst", None),
        P(None, "space", "inst"),
        P("space", "inst"),
    )
    out_specs = (P(None, "space", "inst", None), P(("inst", "space")))
    return jax.shard_map(
        per_device, mesh=mesh, in_specs=in_specs, out_specs=out_specs, check_vma=False
    )
```

```python
import functools
import jax
import jax.numpy as jnp
from jax import lax
from jax.experimental import pallas as pl
from jax.experimental.pallas import tpu as pltpu
from jax.sharding import PartitionSpec as P

DIAG = 6.5
DV_DEV = 8
REACH = 3
PAD = REACH + 1
CHUNK = 2
REACHES = (3, 2, 2)
LOW_AT = (0, 3, 5)
OVER = 7
GROUP = 64
FACE_AT = (REACH, 24, 44)


def shifted_rows(tiles, top, bottom):
    down = [pltpu.roll(t, 1, 0) for t in tiles]
    up = [pltpu.roll(t, 7, 0) for t in tiles]
    zero = jnp.zeros_like(tiles[0])
    down = [jnp.where(top, p, n) for p, n in zip([zero] + down[:-1], down)]
    up = [jnp.where(bottom, n, p) for p, n in zip(up, up[1:] + [zero])]
    return down, up


def front_kernel(
    adj_hbm, flux_hbm,
    main_ko, main_kx, main_so, main_sx, over_ko, over_kx, over_s, wall,
    adj, flux, work, metric, plane, side, band, stack, along, adj_sems, flux_sems,
):
    kinds, variables, rows, width, depth = adj.shape
    chunks = rows // CHUNK
    tiles = width // 8
    inst, space = lax.axis_index("inst"), lax.axis_index("space")
    low_open = jnp.where(space > 0, 1.0, 0.0)
    high_open = jnp.where(space < lax.axis_size("space") - 1, 1.0, 0.0)

    def adj_copy(i):
        part = pl.ds(i * CHUNK, CHUNK)
        return pltpu.make_async_copy(
            adj_hbm.at[:, :, part], adj.at[:, :, part], adj_sems.at[i]
        )

    def flux_copy(i):
        part = pl.ds(i * CHUNK, CHUNK)
        return pltpu.make_async_copy(
            flux_hbm.at[:, :, :, part], flux.at[:, :, :, part], flux_sems.at[i]
        )

    for i in range(chunks):
        adj_copy(i).start()
        flux_copy(i).start()

    near = jnp.abs(
        lax.broadcasted_iota(jnp.int32, (depth, depth), 0)
        - lax.broadcasted_iota(jnp.int32, (depth, depth), 1)
    )
    lane = lax.broadcasted_iota(jnp.int32, (depth, depth), 1)
    ends = jnp.where((lane == 0) | (lane == depth - 1), 1.0, 2.0)
    once = jnp.where(near == 1, 1.0, 0.0).astype(jnp.bfloat16)
    twice = jnp.where(near == 0, ends, jnp.where(near == 2, 1.0, 0.0)).astype(jnp.bfloat16)
    for half in (slice(0, depth), slice(depth, 2 * depth)):
        band[half, :depth] = once
        band[half, depth:] = twice
    zero = jnp.zeros((width, depth), jnp.float32)
    for d in range(3):
        for x in (-2, -1, rows, rows + 1):
            metric[d, x + PAD] = zero
            side[d, x + PAD] = zero
            plane[d, x + PAD] = zero
    for x in (-2, -1, rows, rows + 1):
        work[0, x + PAD] = zero

    row = lax.broadcasted_iota(jnp.int32, (8, depth), 0)
    top, bottom = row == 0, row == 7
    column = lax.broadcasted_iota(jnp.int32, (8, depth), 1)
    first, last = column == 0, column == depth - 1

    def weigh(x):
        for h in range(width // 16):
            part = slice(16 * h, 16 * h + 16)
            sums = [jnp.zeros((16, depth), jnp.float32) for _ in range(3)]
            for k in range(kinds):
                for v in range(variables):
                    a = adj[k, v, x, part].astype(jnp.float32)
                    for d in range(3):
                        sums[d] = sums[d] + a * flux[k, v, d, x, part].astype(jnp.float32)
            for d in range(3):
                work[d, x + PAD, part] = sums[d]

    def tile(t):
        return slice(8 * t, 8 * t + 8)

    def planes(slabs):
        count = len(slabs) * width
        for s, (d, x) in enumerate(slabs):
            r = x + PAD
            here = [work[d, r, tile(t)] for t in range(tiles)]
            if d == 0:
                open_ = jnp.where(x < 0, low_open, jnp.where(x >= rows, high_open, 1.0))
                low = [work[0, r - 1, tile(t)] for t in range(tiles)]
                high = [work[0, r + 1, tile(t)] for t in range(tiles)]
                m = [(h + 0.5 * (p - n)) * open_ for h, p, n in zip(here, low, high)]
            elif d == 1:
                low, high = shifted_rows(here, top, bottom)
                m = [h + 0.5 * (p - n) for h, p, n in zip(here, low, high)]
            else:
                m = [
                    h + 0.5 * (
                        jnp.where(first, 0.0, pltpu.roll(h, 1, 1))
                        - jnp.where(last, 0.0, pltpu.roll(h, depth - 1, 1))
                    )
                    for h in here
                ]
            for t in range(tiles):
                metric[d, r, tile(t)] = m[t]
            for t in range(0, tiles, 2):
                both = jnp.concatenate(m[t : t + 2], axis=0)
                rounded = both.astype(jnp.bfloat16)
                part = slice(s * width + 8 * t, s * width + 8 * t + 16)
                stack[part, :depth] = rounded
                stack[part, depth:] = (both - rounded.astype(jnp.float32)).astype(jnp.bfloat16)
        along[:count] = jnp.dot(stack[:count], band[...], preferred_element_type=jnp.float32)
        for s, (d, x) in enumerate(slabs):
            r = x + PAD
            at = s * width
            m = [metric[d, r, tile(t)] for t in range(tiles)]
            along_1 = [along[at + 8 * t : at + 8 * t + 8, :depth] for t in range(tiles)]
            along_2 = [along[at + 8 * t : at + 8 * t + 8, depth:] for t in range(tiles)]
            low, high = shifted_rows(m, top, bottom)
            once = [(p + n) + q for p, n, q in zip(low, high, along_1)]
            low, high = shifted_rows([o + q for o, q in zip(once, along_1)], top, bottom)
            returns = 2.0 - jnp.where(
                x == 0, 1.0 - low_open, jnp.where(x == rows - 1, 1.0 - high_open, 0.0)
            )
            weight = DIAG * DIAG + returns
            for t in range(tiles):
                side[d, r, tile(t)] = DIAG * m[t] + (once[t] + once[t])
                twice = (low[t] + high[t]) + along_2[t]
                plane[d, r, tile(t)] = weight * m[t] + DIAG * once[t] + twice

    def settle(i, extra):
        planes(
            [(1, i * CHUNK + j) for j in range(CHUNK)]
            + [(2, i * CHUNK + j) for j in range(CHUNK)]
            + [(0, i * CHUNK + j - 1) for j in range(CHUNK + extra)]
        )

    def arrive(i):
        adj_copy(i).wait()
        flux_copy(i).wait()

    arrive(0)
    for j in range(CHUNK):
        weigh(j)

    def stage(i, _):
        arrive(i)
        settle(i - 1, 0)
        for j in range(CHUNK):
            weigh(i * CHUNK + j)
        return 0

    lax.fori_loop(1, chunks, stage, 0)
    settle(chunks - 1, 2)

    def put(refs, index, place, total, face):
        for j, ref, shift in zip((0, 2, 1, 3), refs, (0, 0, 2 * OVER, 0)):
            b = inst ^ j
            at = pl.multiple_of(8 * b, 8)
            value = total(pl.ds(at, 8))
            if ref is over_s:
                ref[index + shift] = value
            else:
                ref[index] = value
            face = jnp.where(column == GROUP * b + place, value[:, 0:1], face)
        return face

    main_refs = (main_ko, main_kx, main_so, main_sx)
    over_refs = (over_ko, over_kx, over_s, over_s)

    def reached(d, x, part):
        r = x + PAD
        first, last = (PAD - 1, PAD + rows) if d == 0 else (PAD, PAD + rows - 1)
        terms = (
            [plane[d, r, part]] * (first <= r <= last)
            + [side[d, s, part] for s in (r - 1, r + 1) if first <= s <= last]
            + [metric[d, s, part] for s in (r - 2, r + 2) if first <= s <= last]
        )
        return functools.reduce(jnp.add, terms)

    face = jnp.zeros((8, depth), jnp.float32)
    for d in range(3):
        for x in range(-REACHES[d], 0):
            face = put(
                over_refs, LOW_AT[d] + x + REACHES[d], FACE_AT[d] + x,
                functools.partial(reached, d, x), face,
            )
        for x in range(rows, rows + REACHES[d]):
            face = put(
                over_refs, OVER + LOW_AT[d] + x - rows, FACE_AT[d] + x,
                functools.partial(reached, d, x), face,
            )

    def inner(x, face):
        r = x + PAD
        for d in range(3):

            def total(part):
                value = plane[d, r, part] + (side[d, r - 1, part] + side[d, r + 1, part])
                return value + (metric[d, r - 2, part] + metric[d, r + 2, part])

            face = put(main_refs, (d, x), FACE_AT[d] + x, total, face)
        return face

    face = lax.fori_loop(0, rows, inner, face, unroll=2)
    wall[0] = face


def front(adjoint, flux_terms):
    kinds, variables, rows, width, depth = adjoint.shape
    f32 = jnp.float32
    block = width // 4
    main = jax.ShapeDtypeStruct((3, rows, block, depth), f32)
    vmem = pl.BlockSpec(memory_space=pltpu.VMEM)
    hbm = pl.BlockSpec(memory_space=pltpu.HBM)
    padded = (3, rows + 2 * PAD, width, depth)
    most = (3 * CHUNK + 2) * width
    over_rows = (2 * OVER, 2 * OVER, 4 * OVER, 1)
    return pl.pallas_call(
        front_kernel,
        out_shape=[main] * 4
        + [jax.ShapeDtypeStruct((count, block, depth), f32) for count in over_rows],
        in_specs=[hbm] * 2,
        out_specs=[vmem] * 8,
        scratch_shapes=[
            pltpu.VMEM(adjoint.shape, adjoint.dtype),
            pltpu.VMEM(flux_terms.shape, flux_terms.dtype),
            pltpu.VMEM(padded, f32),
            pltpu.VMEM(padded, f32),
            pltpu.VMEM(padded, f32),
            pltpu.VMEM(padded, f32),
            pltpu.VMEM((2 * depth, 2 * depth), jnp.bfloat16),
            pltpu.VMEM((most, 2 * depth), jnp.bfloat16),
            pltpu.VMEM((most, 2 * depth), f32),
            pltpu.SemaphoreType.DMA((rows // CHUNK,)),
            pltpu.SemaphoreType.DMA((rows // CHUNK,)),
        ],
        compiler_params=pltpu.CompilerParams(vmem_limit_bytes=51 * 2**20),
        cost_estimate=pl.CostEstimate(
            flops=60_000_000, bytes_accessed=13_000_000, transcendentals=0
        ),
    )(adjoint, flux_terms)


def coefs_kernel(stiffness, normals, ids, after, out):
    del after
    rows, block, depth = stiffness.shape
    column = lax.broadcasted_iota(jnp.int32, (block, depth), 1)
    own = GROUP * lax.axis_index("inst")
    coefs = jnp.zeros((block, depth), jnp.float32)
    for x in range(rows):
        inverse = 1.0 / stiffness[x, :, 0:1]
        for d in range(3):
            here = normals[d, :, x : x + 1] * inverse
            coefs = jnp.where(column == own + d * rows + x, here, coefs)
        here = ids[:, x : x + 1].astype(jnp.float32)
        coefs = jnp.where(column == own + 3 * rows + x, here, coefs)
    out[0] = coefs


def add_kernel(keep, near, *rest):
    out = rest[-1]
    for d in range(out.shape[0]):
        for x in range(out.shape[1]):
            out[d, x] = keep[d, x] + near[d, x]


def wall_near_kernel(face, face_near, coefs, coefs_near, out):
    out[0] = face[0] + face_near[0]
    out[1] = coefs[0] + coefs_near[0]


def over_near_kernel(over, over_near, after, out):
    del after
    for i in range(2 * OVER):
        out[i] = over[i] + over_near[i]


def over_low(keep, over_near, far, i):
    return keep[i] + over_near[2 * OVER + i] + far[i]


def over_high(keep, over_near, far, i):
    return keep[OVER + i] + over_near[3 * OVER + i] + far[OVER + i]


def wall_kernel(near, far, after, out):
    del after
    for i in range(2):
        value = near[i] + far[i]
        for s in range(out.shape[0]):
            out[s, i] = value


def over_kernel(keep, over_near, far, after, outside, inside):
    del after
    even = lax.axis_index("space") % 2 == 0
    for i in range(OVER):
        low, high = (f(keep, over_near, far, i) for f in (over_low, over_high))
        inside[i] = jnp.where(even, high, low)
        outside[i] = jnp.where(even, low, high)


def design_sums(scale, rows, walls, out):
    faces = [walls[s, 0] for s in range(walls.shape[0])]
    coefs = [walls[s, 1] for s in range(walls.shape[0])]
    spaces = len(faces)
    block, depth = faces[0].shape
    column = lax.broadcasted_iota(jnp.int32, (block, depth), 1) % GROUP
    at_low = functools.reduce(
        jnp.logical_or,
        [(column >= at) & (column < at + n) for at, n in zip(FACE_AT, REACHES)],
    )
    at_high = functools.reduce(
        jnp.logical_or,
        [
            (column >= at + rows - n) & (column < at + rows)
            for at, n in zip(FACE_AT, REACHES)
        ],
    )
    mine = (lax.axis_index("inst") * spaces + lax.axis_index("space")) * DV_DEV
    sums = [jnp.zeros((block, depth), jnp.float32) for _ in range(DV_DEV)]
    for s in range(spaces):
        whole = faces[s]
        if s > 0:
            whole = whole + jnp.where(at_low, pltpu.roll(faces[s - 1], depth - rows, 1), 0.0)
        if s < spaces - 1:
            whole = whole + jnp.where(at_high, pltpu.roll(faces[s + 1], rows, 1), 0.0)
        surface = jnp.zeros((block, depth), jnp.float32)
        for d in range(3):
            turned = pltpu.roll(coefs[s], depth - d * rows, 1) if d else coefs[s]
            surface = surface + pltpu.roll(whole, depth - FACE_AT[d], 1) * turned
        ids = pltpu.roll(coefs[s], depth - 3 * rows, 1).astype(jnp.int32) - mine
        ids = jnp.where(column < rows, ids, -1)
        for j in range(DV_DEV):
            sums[j] = sums[j] + jnp.where(ids == j, surface, 0.0)
    for j in range(DV_DEV):
        out[j] = jnp.sum(sums[j]) * scale


def last_kernel(
    scale, spaces, keep, near, far, stiffness, across, inside, walls_ref,
    out, design, walls, sem,
):
    rows = keep.shape[1]
    copy = pltpu.make_async_copy(walls_ref, walls, sem)
    copy.start()
    space = lax.axis_index("space")
    even = space % 2 == 0
    inner = (space > 0) & (space < spaces - 1)
    for x in range(rows):
        inverse = scale / stiffness[x]
        for d in range(3):
            value = keep[d, x] + near[d, x] + far[d, x]
            for at, side in (
                (LOW_AT[d] + x, even if x < REACHES[d] else None),
                (LOW_AT[d] + x - rows + REACHES[d], ~even if x >= rows - REACHES[d] else None),
            ):
                if side is not None:
                    outer = jnp.where(inner, across[at], 0.0)
                    value = value + jnp.where(side, outer, inside[at])
            out[d, x] = value * inverse
    copy.wait()
    design_sums(scale, rows, walls, design)


def per_device(adjoint, flux_terms, stiffness, normals, design_map):
    insts, spaces = lax.axis_size("inst"), lax.axis_size("space")
    rows, block, depth = stiffness.shape
    scale = 1.0 / (DIAG**3 * adjoint.shape[0] * insts)

    vmem = pl.BlockSpec(memory_space=pltpu.VMEM)

    def on_chip(kernel, shapes, *operands, after=()):
        out = [jax.ShapeDtypeStruct(shape, jnp.float32) for shape in shapes]
        return pl.pallas_call(
            kernel,
            out_shape=out,
            in_specs=[vmem] * len(operands) + [pl.BlockSpec(memory_space=pl.ANY)] * len(after),
            out_specs=[vmem] * len(out),
            compiler_params=pltpu.CompilerParams(vmem_limit_bytes=4 * 2**20),
            cost_estimate=pl.CostEstimate(
                flops=500_000, bytes_accessed=1_500_000, transcendentals=0
            ),
        )(*operands, *after)

    main_ko, main_kx, main_so, main_sx, over_ko, over_kx, over_s, face = front(
        adjoint, flux_terms
    )

    other_core = [(i, i ^ 1) for i in range(insts)]
    other_chip = [(i, i ^ 2) for i in range(insts)]

    plane = (1, block, depth)
    face_r = lax.ppermute(face, "inst", other_core)
    [coefs] = on_chip(
        coefs_kernel, [plane], stiffness, normals.transpose(0, 2, 1), design_map.T,
        after=[face],
    )
    coefs_r = lax.ppermute(coefs, "inst", other_core)
    over_r = lax.ppermute(over_s, "inst", other_core)
    main_r = lax.ppermute(main_sx, "inst", other_core)
    main_near = lax.ppermute(main_so, "inst", other_core)
    halo, plane = (OVER, block, depth), (2, block, depth)
    [wall_near] = on_chip(wall_near_kernel, [plane], face, face_r, coefs, coefs_r)
    wall_far = lax.ppermute(wall_near, "inst", other_chip)
    [over_x] = on_chip(
        over_near_kernel, [over_kx.shape], over_kx, over_r, after=[wall_near]
    )
    over_far = lax.ppermute(over_x, "inst", other_chip)
    [wall] = on_chip(
        wall_kernel, [(spaces,) + plane], wall_near, wall_far, after=[over_x]
    )
    wall = pltpu.with_memory_space_constraint(wall, pltpu.VMEM)
    walls = lax.all_to_all(wall, "space", 0, 0, tiled=True)
    [main_x] = on_chip(add_kernel, [main_kx.shape], main_kx, main_r, after=[wall, over_far])
    main_far = lax.ppermute(main_x, "inst", other_chip)

    across, inside = on_chip(
        over_kernel, [halo, halo], over_ko, over_r, over_far, after=[main_x]
    )
    across = lax.ppermute(
        across, "space", [(i, (((i + 1) ^ 1) - 1) % spaces) for i in range(spaces)]
    )
    inside = lax.ppermute(inside, "space", [(i, i ^ 1) for i in range(spaces)])
    mesh_adjoint, design_grad = pl.pallas_call(
        functools.partial(last_kernel, scale, spaces),
        out_shape=[
            jax.ShapeDtypeStruct((3, rows, block, depth), jnp.float32),
            jax.ShapeDtypeStruct((DV_DEV,), jnp.float32),
        ],
        in_specs=[vmem] * 6 + [pl.BlockSpec(memory_space=pl.ANY)],
        out_specs=[vmem, pl.BlockSpec(memory_space=pltpu.SMEM)],
        scratch_shapes=[
            pltpu.VMEM(walls.shape, jnp.float32),
            pltpu.SemaphoreType.DMA(()),
        ],
        compiler_params=pltpu.CompilerParams(vmem_limit_bytes=6 * 2**20),
    )(main_ko, main_near, main_far, stiffness, across, inside, walls)
    return (mesh_adjoint, design_grad)


def solution(mesh):
    in_specs = (
        P("inst", None, "space", None, None),
        P("inst", None, None, "space", None, None),
        P("space", "inst", None),
        P(None, "space", "inst"),
        P("space", "inst"),
    )
    out_specs = (P(None, "space", "inst", None), P(("inst", "space")))
    return jax.shard_map(
        per_device, mesh=mesh, in_specs=in_specs, out_specs=out_specs, check_vma=False
    )
```

```python
import functools
import jax
import jax.numpy as jnp
from jax import lax
from jax.experimental import pallas as pl
from jax.experimental.pallas import tpu as pltpu
from jax.sharding import PartitionSpec as P

DIAG = 6.5
DV_DEV = 8
REACH = 3
PAD = REACH + 1
CHUNK = 2
REACHES = (3, 2, 2)
LOW_AT = (0, 3, 5)
OVER = 7
GROUP = 64
FACE_AT = (REACH, 24, 44)


def shifted_rows(tiles, top, bottom):
    down = [pltpu.roll(t, 1, 0) for t in tiles]
    up = [pltpu.roll(t, 7, 0) for t in tiles]
    zero = jnp.zeros_like(tiles[0])
    down = [jnp.where(top, p, n) for p, n in zip([zero] + down[:-1], down)]
    up = [jnp.where(bottom, n, p) for p, n in zip(up, up[1:] + [zero])]
    return down, up


def front_kernel(
    adj_hbm, flux_hbm,
    main_ko, main_kx, main_so, main_sx, over_ko, over_kx, over_s, wall,
    adj, flux, work, metric, plane, side, band, stack, along, adj_sems, flux_sems,
):
    kinds, variables, rows, width, depth = adj.shape
    chunks = rows // CHUNK
    tiles = width // 8
    inst, space = lax.axis_index("inst"), lax.axis_index("space")
    low_open = jnp.where(space > 0, 1.0, 0.0)
    high_open = jnp.where(space < lax.axis_size("space") - 1, 1.0, 0.0)

    def adj_copy(i):
        part = pl.ds(i * CHUNK, CHUNK)
        return pltpu.make_async_copy(
            adj_hbm.at[:, :, part], adj.at[:, :, part], adj_sems.at[i]
        )

    def flux_copy(i):
        part = pl.ds(i * CHUNK, CHUNK)
        return pltpu.make_async_copy(
            flux_hbm.at[:, :, :, part], flux.at[:, :, :, part], flux_sems.at[i]
        )

    for i in range(chunks):
        adj_copy(i).start()
        flux_copy(i).start()

    near = jnp.abs(
        lax.broadcasted_iota(jnp.int32, (depth, depth), 0)
        - lax.broadcasted_iota(jnp.int32, (depth, depth), 1)
    )
    lane = lax.broadcasted_iota(jnp.int32, (depth, depth), 1)
    ends = jnp.where((lane == 0) | (lane == depth - 1), 1.0, 2.0)
    once = jnp.where(near == 1, 1.0, 0.0).astype(jnp.bfloat16)
    twice = jnp.where(near == 0, ends, jnp.where(near == 2, 1.0, 0.0)).astype(jnp.bfloat16)
    for half in (slice(0, depth), slice(depth, 2 * depth)):
        band[half, :depth] = once
        band[half, depth:] = twice
    zero = jnp.zeros((width, depth), jnp.float32)
    for d in range(3):
        for x in (-2, -1, rows, rows + 1):
            metric[d, x + PAD] = zero
            side[d, x + PAD] = zero
            plane[d, x + PAD] = zero
    for x in (-2, -1, rows, rows + 1):
        work[0, x + PAD] = zero

    row = lax.broadcasted_iota(jnp.int32, (8, depth), 0)
    top, bottom = row == 0, row == 7
    column = lax.broadcasted_iota(jnp.int32, (8, depth), 1)
    first, last = column == 0, column == depth - 1

    def weigh(x):
        for h in range(width // 16):
            part = slice(16 * h, 16 * h + 16)
            sums = [jnp.zeros((16, depth), jnp.float32) for _ in range(3)]
            for k in range(kinds):
                for v in range(variables):
                    a = adj[k, v, x, part].astype(jnp.float32)
                    for d in range(3):
                        sums[d] = sums[d] + a * flux[k, v, d, x, part].astype(jnp.float32)
            for d in range(3):
                work[d, x + PAD, part] = sums[d]

    def tile(t):
        return slice(8 * t, 8 * t + 8)

    def planes(slabs):
        count = len(slabs) * width
        for s, (d, x) in enumerate(slabs):
            r = x + PAD
            here = [work[d, r, tile(t)] for t in range(tiles)]
            if d == 0:
                open_ = jnp.where(x < 0, low_open, jnp.where(x >= rows, high_open, 1.0))
                low = [work[0, r - 1, tile(t)] for t in range(tiles)]
                high = [work[0, r + 1, tile(t)] for t in range(tiles)]
                m = [(h + 0.5 * (p - n)) * open_ for h, p, n in zip(here, low, high)]
            elif d == 1:
                low, high = shifted_rows(here, top, bottom)
                m = [h + 0.5 * (p - n) for h, p, n in zip(here, low, high)]
            else:
                m = [
                    h + 0.5 * (
                        jnp.where(first, 0.0, pltpu.roll(h, 1, 1))
                        - jnp.where(last, 0.0, pltpu.roll(h, depth - 1, 1))
                    )
                    for h in here
                ]
            for t in range(tiles):
                metric[d, r, tile(t)] = m[t]
            for t in range(0, tiles, 2):
                both = jnp.concatenate(m[t : t + 2], axis=0)
                rounded = both.astype(jnp.bfloat16)
                part = slice(s * width + 8 * t, s * width + 8 * t + 16)
                stack[part, :depth] = rounded
                stack[part, depth:] = (both - rounded.astype(jnp.float32)).astype(jnp.bfloat16)
        along[:count] = jnp.dot(stack[:count], band[...], preferred_element_type=jnp.float32)
        for s, (d, x) in enumerate(slabs):
            r = x + PAD
            at = s * width
            m = [metric[d, r, tile(t)] for t in range(tiles)]
            along_1 = [along[at + 8 * t : at + 8 * t + 8, :depth] for t in range(tiles)]
            along_2 = [along[at + 8 * t : at + 8 * t + 8, depth:] for t in range(tiles)]
            low, high = shifted_rows(m, top, bottom)
            once = [(p + n) + q for p, n, q in zip(low, high, along_1)]
            low, high = shifted_rows([o + q for o, q in zip(once, along_1)], top, bottom)
            returns = 2.0 - jnp.where(
                x == 0, 1.0 - low_open, jnp.where(x == rows - 1, 1.0 - high_open, 0.0)
            )
            weight = DIAG * DIAG + returns
            for t in range(tiles):
                side[d, r, tile(t)] = DIAG * m[t] + (once[t] + once[t])
                twice = (low[t] + high[t]) + along_2[t]
                plane[d, r, tile(t)] = weight * m[t] + DIAG * once[t] + twice

    def settle(i, extra):
        planes(
            [(1, i * CHUNK + j) for j in range(CHUNK)]
            + [(2, i * CHUNK + j) for j in range(CHUNK)]
            + [(0, i * CHUNK + j - 1) for j in range(CHUNK + extra)]
        )

    def arrive(i):
        adj_copy(i).wait()
        flux_copy(i).wait()

    arrive(0)
    for j in range(CHUNK):
        weigh(j)

    def stage(i, _):
        arrive(i)
        settle(i - 1, 0)
        for j in range(CHUNK):
            weigh(i * CHUNK + j)
        return 0

    lax.fori_loop(1, chunks, stage, 0)
    settle(chunks - 1, 2)

    def put(refs, index, place, total, face):
        for j, ref, shift in zip((0, 2, 1, 3), refs, (0, 0, 2 * OVER, 0)):
            b = inst ^ j
            at = pl.multiple_of(8 * b, 8)
            value = total(pl.ds(at, 8))
            if ref is over_s:
                ref[index + shift] = value
            else:
                ref[index] = value
            face = jnp.where(column == GROUP * b + place, value[:, 0:1], face)
        return face

    main_refs = (main_ko, main_kx, main_so, main_sx)
    over_refs = (over_ko, over_kx, over_s, over_s)

    def reached(d, x, part):
        r = x + PAD
        first, last = (PAD - 1, PAD + rows) if d == 0 else (PAD, PAD + rows - 1)
        terms = (
            [plane[d, r, part]] * (first <= r <= last)
            + [side[d, s, part] for s in (r - 1, r + 1) if first <= s <= last]
            + [metric[d, s, part] for s in (r - 2, r + 2) if first <= s <= last]
        )
        return functools.reduce(jnp.add, terms)

    face = jnp.zeros((8, depth), jnp.float32)
    for d in range(3):
        for x in range(-REACHES[d], 0):
            face = put(
                over_refs, LOW_AT[d] + x + REACHES[d], FACE_AT[d] + x,
                functools.partial(reached, d, x), face,
            )
        for x in range(rows, rows + REACHES[d]):
            face = put(
                over_refs, OVER + LOW_AT[d] + x - rows, FACE_AT[d] + x,
                functools.partial(reached, d, x), face,
            )

    def inner(x, face):
        r = x + PAD
        for d in range(3):

            def total(part):
                value = plane[d, r, part] + (side[d, r - 1, part] + side[d, r + 1, part])
                return value + (metric[d, r - 2, part] + metric[d, r + 2, part])

            face = put(main_refs, (d, x), FACE_AT[d] + x, total, face)
        return face

    face = lax.fori_loop(0, rows, inner, face, unroll=2)
    wall[0] = face


def front(adjoint, flux_terms):
    kinds, variables, rows, width, depth = adjoint.shape
    f32 = jnp.float32
    block = width // 4
    main = jax.ShapeDtypeStruct((3, rows, block, depth), f32)
    vmem = pl.BlockSpec(memory_space=pltpu.VMEM)
    hbm = pl.BlockSpec(memory_space=pltpu.HBM)
    padded = (3, rows + 2 * PAD, width, depth)
    most = (3 * CHUNK + 2) * width
    over_rows = (2 * OVER, 2 * OVER, 4 * OVER, 1)
    return pl.pallas_call(
        front_kernel,
        out_shape=[main] * 4
        + [jax.ShapeDtypeStruct((count, block, depth), f32) for count in over_rows],
        in_specs=[hbm] * 2,
        out_specs=[vmem] * 8,
        scratch_shapes=[
            pltpu.VMEM(adjoint.shape, adjoint.dtype),
            pltpu.VMEM(flux_terms.shape, flux_terms.dtype),
            pltpu.VMEM(padded, f32),
            pltpu.VMEM(padded, f32),
            pltpu.VMEM(padded, f32),
            pltpu.VMEM(padded, f32),
            pltpu.VMEM((2 * depth, 2 * depth), jnp.bfloat16),
            pltpu.VMEM((most, 2 * depth), jnp.bfloat16),
            pltpu.VMEM((most, 2 * depth), f32),
            pltpu.SemaphoreType.DMA((rows // CHUNK,)),
            pltpu.SemaphoreType.DMA((rows // CHUNK,)),
        ],
        compiler_params=pltpu.CompilerParams(vmem_limit_bytes=51 * 2**20),
        cost_estimate=pl.CostEstimate(
            flops=60_000_000, bytes_accessed=13_000_000, transcendentals=0
        ),
    )(adjoint, flux_terms)


def coefs_kernel(stiffness, normals, ids, after, out):
    del after
    rows, block, depth = stiffness.shape
    column = lax.broadcasted_iota(jnp.int32, (block, depth), 1)
    own = GROUP * lax.axis_index("inst")
    coefs = jnp.zeros((block, depth), jnp.float32)
    for x in range(rows):
        inverse = 1.0 / stiffness[x, :, 0:1]
        for d in range(3):
            here = normals[d, :, x : x + 1] * inverse
            coefs = jnp.where(column == own + d * rows + x, here, coefs)
        here = ids[:, x : x + 1].astype(jnp.float32)
        coefs = jnp.where(column == own + 3 * rows + x, here, coefs)
    out[0] = coefs


def add_kernel(keep, near, *rest):
    out = rest[-1]
    for d in range(out.shape[0]):
        for x in range(out.shape[1]):
            out[d, x] = keep[d, x] + near[d, x]


def wall_near_kernel(face, face_near, coefs, coefs_near, out):
    out[0] = face[0] + face_near[0]
    out[1] = coefs[0] + coefs_near[0]


def over_near_kernel(over, over_near, after, out):
    del after
    for i in range(2 * OVER):
        out[i] = over[i] + over_near[i]


def over_low(keep, over_near, far, i):
    return keep[i] + over_near[2 * OVER + i] + far[i]


def over_high(keep, over_near, far, i):
    return keep[OVER + i] + over_near[3 * OVER + i] + far[OVER + i]


def pass_kernel(value, after, out):
    del after
    for i in range(out.shape[0]):
        out[i] = value[i]


def wall_kernel(near, far, after, out):
    del after
    for i in range(2):
        out[i] = near[i] + far[i]


def in_order(bit, own, other):
    upper = (lax.axis_index("space") >> bit) % 2 == 1
    planes = []
    for g in range(own.shape[0] // 2):
        at = (2 * g, 2 * g + 1)
        planes += [jnp.where(upper, other[i], own[i]) for i in at]
        planes += [jnp.where(upper, own[i], other[i]) for i in at]
    return planes


def gather_kernel(bit, own, other, out):
    for i, value in enumerate(in_order(bit, own, other)):
        out[i] = value


def over_kernel(keep, over_near, far, after, outside, inside):
    del after
    even = lax.axis_index("space") % 2 == 0
    for i in range(OVER):
        low, high = (f(keep, over_near, far, i) for f in (over_low, over_high))
        inside[i] = jnp.where(even, high, low)
        outside[i] = jnp.where(even, low, high)


def design_sums(scale, rows, own, other, out):
    planes = in_order(0, own, other)
    faces, coefs = planes[::2], planes[1::2]
    spaces = len(faces)
    block, depth = faces[0].shape
    column = lax.broadcasted_iota(jnp.int32, (block, depth), 1) % GROUP
    at_low = functools.reduce(
        jnp.logical_or,
        [(column >= at) & (column < at + n) for at, n in zip(FACE_AT, REACHES)],
    )
    at_high = functools.reduce(
        jnp.logical_or,
        [
            (column >= at + rows - n) & (column < at + rows)
            for at, n in zip(FACE_AT, REACHES)
        ],
    )
    mine = (lax.axis_index("inst") * spaces + lax.axis_index("space")) * DV_DEV
    sums = [jnp.zeros((block, depth), jnp.float32) for _ in range(DV_DEV)]
    for s in range(spaces):
        whole = faces[s]
        if s > 0:
            whole = whole + jnp.where(at_low, pltpu.roll(faces[s - 1], depth - rows, 1), 0.0)
        if s < spaces - 1:
            whole = whole + jnp.where(at_high, pltpu.roll(faces[s + 1], rows, 1), 0.0)
        surface = jnp.zeros((block, depth), jnp.float32)
        for d in range(3):
            turned = pltpu.roll(coefs[s], depth - d * rows, 1) if d else coefs[s]
            surface = surface + pltpu.roll(whole, depth - FACE_AT[d], 1) * turned
        ids = pltpu.roll(coefs[s], depth - 3 * rows, 1).astype(jnp.int32) - mine
        ids = jnp.where(column < rows, ids, -1)
        for j in range(DV_DEV):
            sums[j] = sums[j] + jnp.where(ids == j, surface, 0.0)
    for j in range(DV_DEV):
        out[j] = jnp.sum(sums[j]) * scale


def last_kernel(
    scale, spaces, keep, near, far, stiffness, across, inside, wall, other_wall,
    out, design,
):
    rows = keep.shape[1]
    space = lax.axis_index("space")
    even = space % 2 == 0
    inner = (space > 0) & (space < spaces - 1)
    for x in range(rows):
        inverse = scale / stiffness[x]
        for d in range(3):
            value = keep[d, x] + near[d, x] + far[d, x]
            for at, side in (
                (LOW_AT[d] + x, even if x < REACHES[d] else None),
                (LOW_AT[d] + x - rows + REACHES[d], ~even if x >= rows - REACHES[d] else None),
            ):
                if side is not None:
                    outer = jnp.where(inner, across[at], 0.0)
                    value = value + jnp.where(side, outer, inside[at])
            out[d, x] = value * inverse
    design_sums(scale, rows, wall, other_wall, design)


def per_device(adjoint, flux_terms, stiffness, normals, design_map):
    insts, spaces = lax.axis_size("inst"), lax.axis_size("space")
    rows, block, depth = stiffness.shape
    scale = 1.0 / (DIAG**3 * adjoint.shape[0] * insts)

    vmem = pl.BlockSpec(memory_space=pltpu.VMEM)

    def on_chip(kernel, shapes, *operands, after=()):
        out = [jax.ShapeDtypeStruct(shape, jnp.float32) for shape in shapes]
        return pl.pallas_call(
            kernel,
            out_shape=out,
            in_specs=[vmem] * len(operands) + [pl.BlockSpec(memory_space=pl.ANY)] * len(after),
            out_specs=[vmem] * len(out),
            compiler_params=pltpu.CompilerParams(vmem_limit_bytes=4 * 2**20),
            cost_estimate=pl.CostEstimate(
                flops=500_000, bytes_accessed=1_500_000, transcendentals=0
            ),
        )(*operands, *after)

    main_ko, main_kx, main_so, main_sx, over_ko, over_kx, over_s, face = front(
        adjoint, flux_terms
    )

    other_core = [(i, i ^ 1) for i in range(insts)]
    other_chip = [(i, i ^ 2) for i in range(insts)]

    plane = (1, block, depth)
    face_r = lax.ppermute(face, "inst", other_core)
    [coefs] = on_chip(
        coefs_kernel, [plane], stiffness, normals.transpose(0, 2, 1), design_map.T,
        after=[face],
    )
    coefs_r = lax.ppermute(coefs, "inst", other_core)
    over_r = lax.ppermute(over_s, "inst", other_core)
    main_r = lax.ppermute(main_sx, "inst", other_core)
    main_near = lax.ppermute(main_so, "inst", other_core)
    halo, plane = (OVER, block, depth), (2, block, depth)
    [wall_near] = on_chip(wall_near_kernel, [plane], face, face_r, coefs, coefs_r)
    wall_far = lax.ppermute(wall_near, "inst", other_chip)
    [over_x] = on_chip(
        over_near_kernel, [over_kx.shape], over_kx, over_r, after=[wall_near]
    )
    over_far = lax.ppermute(over_x, "inst", other_chip)
    [wall] = on_chip(wall_kernel, [plane], wall_near, wall_far, after=[over_x])
    [main_x] = on_chip(add_kernel, [main_kx.shape], main_kx, main_r, after=[wall, over_far])
    main_far = lax.ppermute(main_x, "inst", other_chip)

    across, inside = on_chip(
        over_kernel, [halo, halo], over_ko, over_r, over_far, after=[main_x]
    )
    across = lax.ppermute(
        across, "space", [(i, (((i + 1) ^ 1) - 1) % spaces) for i in range(spaces)]
    )
    for bit in reversed(range(spaces.bit_length() - 1)):
        swap = [(i, i ^ (1 << bit)) for i in range(spaces)]
        other_wall = lax.ppermute(wall, "space", swap)
        if bit > 0:
            gathered = (2 * wall.shape[0], block, depth)
            [wall] = on_chip(
                functools.partial(gather_kernel, bit), [gathered], wall, other_wall
            )
    [inside] = on_chip(pass_kernel, [halo], inside, after=[wall])
    inside = lax.ppermute(inside, "space", swap)
    mesh_adjoint, design_grad = pl.pallas_call(
        functools.partial(last_kernel, scale, spaces),
        out_shape=[
            jax.ShapeDtypeStruct((3, rows, block, depth), jnp.float32),
            jax.ShapeDtypeStruct((DV_DEV,), jnp.float32),
        ],
        in_specs=[vmem] * 8,
        out_specs=[vmem, pl.BlockSpec(memory_space=pltpu.SMEM)],
        compiler_params=pltpu.CompilerParams(vmem_limit_bytes=6 * 2**20),
    )(main_ko, main_near, main_far, stiffness, across, inside, wall, other_wall)
    return (mesh_adjoint, design_grad)


def solution(mesh):
    in_specs = (
        P("inst", None, "space", None, None),
        P("inst", None, None, "space", None, None),
        P("space", "inst", None),
        P(None, "space", "inst"),
        P("space", "inst"),
    )
    out_specs = (P(None, "space", "inst", None), P(("inst", "space")))
    return jax.shard_map(
        per_device, mesh=mesh, in_specs=in_specs, out_specs=out_specs, check_vma=False
    )
```

```python
import functools
import jax
import jax.numpy as jnp
from jax import lax
from jax.experimental import pallas as pl
from jax.experimental.pallas import tpu as pltpu
from jax.sharding import PartitionSpec as P

DIAG = 6.5
DV_DEV = 8
REACH = 3
PAD = REACH + 1
CHUNK = 2
REACHES = (3, 2, 2)
LOW_AT = (0, 3, 5)
OVER = 7
GROUP = 64
FACE_AT = (REACH, 24, 44)


def shifted_rows(tiles, top, bottom):
    down = [pltpu.roll(t, 1, 0) for t in tiles]
    up = [pltpu.roll(t, 7, 0) for t in tiles]
    zero = jnp.zeros_like(tiles[0])
    down = [jnp.where(top, p, n) for p, n in zip([zero] + down[:-1], down)]
    up = [jnp.where(bottom, n, p) for p, n in zip(up, up[1:] + [zero])]
    return down, up


def shifted_lanes(tile, first, last):
    halves = tile[:, :128], tile[:, 128:]
    up = [pltpu.roll(h, 1, 1) for h in halves]
    down = [pltpu.roll(h, 127, 1) for h in halves]
    zero = jnp.zeros_like(up[0])
    up = [jnp.where(first, zero, up[0]), jnp.where(first, up[0], up[1])]
    down = [jnp.where(last, down[1], down[0]), jnp.where(last, zero, down[1])]
    return jnp.concatenate(up, axis=1), jnp.concatenate(down, axis=1)


def front_kernel(
    adj_hbm, flux_hbm,
    main_ko, main_kx, main_so, main_sx, over_ko, over_kx, over_s, wall,
    adj, flux, work, metric, plane, side, adj_sems, flux_sems,
):
    kinds, variables, rows, width, depth = adj.shape
    chunks = rows // CHUNK
    tiles = width // 8
    inst, space = lax.axis_index("inst"), lax.axis_index("space")
    low_open = jnp.where(space > 0, 1.0, 0.0)
    high_open = jnp.where(space < lax.axis_size("space") - 1, 1.0, 0.0)

    def adj_copy(i):
        part = pl.ds(i * CHUNK, CHUNK)
        return pltpu.make_async_copy(
            adj_hbm.at[:, :, part], adj.at[:, :, part], adj_sems.at[i]
        )

    def flux_copy(i):
        part = pl.ds(i * CHUNK, CHUNK)
        return pltpu.make_async_copy(
            flux_hbm.at[:, :, :, part], flux.at[:, :, :, part], flux_sems.at[i]
        )

    for i in range(chunks):
        adj_copy(i).start()
        flux_copy(i).start()

    zero = jnp.zeros((width, depth), jnp.float32)
    for d in range(3):
        for x in (-2, -1, rows, rows + 1):
            metric[d, x + PAD] = zero
            side[d, x + PAD] = zero
            plane[d, x + PAD] = zero
    for x in (-2, -1, rows, rows + 1):
        work[0, x + PAD] = zero

    row = lax.broadcasted_iota(jnp.int32, (8, depth), 0)
    top, bottom = row == 0, row == 7
    column = lax.broadcasted_iota(jnp.int32, (8, depth), 1)
    lane = lax.broadcasted_iota(jnp.int32, (8, 128), 1)
    first, last = lane == 0, lane == 127

    def weigh(x):
        for h in range(width // 16):
            part = slice(16 * h, 16 * h + 16)
            sums = [jnp.zeros((16, depth), jnp.float32) for _ in range(3)]
            for k in range(kinds):
                for v in range(variables):
                    a = adj[k, v, x, part].astype(jnp.float32)
                    for d in range(3):
                        sums[d] = sums[d] + a * flux[k, v, d, x, part].astype(jnp.float32)
            for d in range(3):
                work[d, x + PAD, part] = sums[d]

    def tile(t):
        return slice(8 * t, 8 * t + 8)

    def around(parts):
        low, high = shifted_rows(parts, top, bottom)
        sums = []
        for p, n, part in zip(low, high, parts):
            left, right = shifted_lanes(part, first, last)
            sums.append((p + n) + (left + right))
        return sums

    def planes(slabs):
        for d, x in slabs:
            r = x + PAD
            here = [work[d, r, tile(t)] for t in range(tiles)]
            if d == 0:
                open_ = jnp.where(x < 0, low_open, jnp.where(x >= rows, high_open, 1.0))
                low = [work[0, r - 1, tile(t)] for t in range(tiles)]
                high = [work[0, r + 1, tile(t)] for t in range(tiles)]
                m = [(h + 0.5 * (p - n)) * open_ for h, p, n in zip(here, low, high)]
            elif d == 1:
                low, high = shifted_rows(here, top, bottom)
                m = [h + 0.5 * (p - n) for h, p, n in zip(here, low, high)]
            else:
                m = []
                for h in here:
                    left, right = shifted_lanes(h, first, last)
                    m.append(h + 0.5 * (left - right))
            once = around(m)
            twice = around(once)
            returns = 2.0 - jnp.where(
                x == 0, 1.0 - low_open, jnp.where(x == rows - 1, 1.0 - high_open, 0.0)
            )
            weight = DIAG * DIAG + returns
            for t in range(tiles):
                metric[d, r, tile(t)] = m[t]
                side[d, r, tile(t)] = DIAG * m[t] + (once[t] + once[t])
                plane[d, r, tile(t)] = weight * m[t] + DIAG * once[t] + twice[t]

    def settle(i, extra):
        planes(
            [(1, i * CHUNK + j) for j in range(CHUNK)]
            + [(2, i * CHUNK + j) for j in range(CHUNK)]
            + [(0, i * CHUNK + j - 1) for j in range(CHUNK + extra)]
        )

    def arrive(i):
        adj_copy(i).wait()
        flux_copy(i).wait()

    arrive(0)
    for j in range(CHUNK):
        weigh(j)

    def stage(i, _):
        arrive(i)
        settle(i - 1, 0)
        for j in range(CHUNK):
            weigh(i * CHUNK + j)
        return 0

    lax.fori_loop(1, chunks, stage, 0)
    settle(chunks - 1, 2)

    def put(refs, index, place, total, face):
        for j, ref, shift in zip((0, 2, 1, 3), refs, (0, 0, 2 * OVER, 0)):
            b = inst ^ j
            at = pl.multiple_of(8 * b, 8)
            value = total(pl.ds(at, 8))
            if ref is over_s:
                ref[index + shift] = value
            else:
                ref[index] = value
            face = jnp.where(column == GROUP * b + place, value[:, 0:1], face)
        return face

    main_refs = (main_ko, main_kx, main_so, main_sx)
    over_refs = (over_ko, over_kx, over_s, over_s)

    def reached(d, x, part):
        r = x + PAD
        first, last = (PAD - 1, PAD + rows) if d == 0 else (PAD, PAD + rows - 1)
        terms = (
            [plane[d, r, part]] * (first <= r <= last)
            + [side[d, s, part] for s in (r - 1, r + 1) if first <= s <= last]
            + [metric[d, s, part] for s in (r - 2, r + 2) if first <= s <= last]
        )
        return functools.reduce(jnp.add, terms)

    face = jnp.zeros((8, depth), jnp.float32)
    for d in range(3):
        for x in range(-REACHES[d], 0):
            face = put(
                over_refs, LOW_AT[d] + x + REACHES[d], FACE_AT[d] + x,
                functools.partial(reached, d, x), face,
            )
        for x in range(rows, rows + REACHES[d]):
            face = put(
                over_refs, OVER + LOW_AT[d] + x - rows, FACE_AT[d] + x,
                functools.partial(reached, d, x), face,
            )

    def inner(x, face):
        r = x + PAD
        for d in range(3):

            def total(part):
                value = plane[d, r, part] + (side[d, r - 1, part] + side[d, r + 1, part])
                return value + (metric[d, r - 2, part] + metric[d, r + 2, part])

            face = put(main_refs, (d, x), FACE_AT[d] + x, total, face)
        return face

    face = lax.fori_loop(0, rows, inner, face, unroll=2)
    wall[0] = face


def front(adjoint, flux_terms):
    kinds, variables, rows, width, depth = adjoint.shape
    f32 = jnp.float32
    block = width // 4
    main = jax.ShapeDtypeStruct((3, rows, block, depth), f32)
    vmem = pl.BlockSpec(memory_space=pltpu.VMEM)
    hbm = pl.BlockSpec(memory_space=pltpu.HBM)
    padded = (3, rows + 2 * PAD, width, depth)
    over_rows = (2 * OVER, 2 * OVER, 4 * OVER, 1)
    return pl.pallas_call(
        front_kernel,
        out_shape=[main] * 4
        + [jax.ShapeDtypeStruct((count, block, depth), f32) for count in over_rows],
        in_specs=[hbm] * 2,
        out_specs=[vmem] * 8,
        scratch_shapes=[
            pltpu.VMEM(adjoint.shape, adjoint.dtype),
            pltpu.VMEM(flux_terms.shape, flux_terms.dtype),
            pltpu.VMEM(padded, f32),
            pltpu.VMEM(padded, f32),
            pltpu.VMEM(padded, f32),
            pltpu.VMEM(padded, f32),
            pltpu.SemaphoreType.DMA((rows // CHUNK,)),
            pltpu.SemaphoreType.DMA((rows // CHUNK,)),
        ],
        compiler_params=pltpu.CompilerParams(vmem_limit_bytes=51 * 2**20),
        cost_estimate=pl.CostEstimate(
            flops=60_000_000, bytes_accessed=13_000_000, transcendentals=0
        ),
    )(adjoint, flux_terms)


def coefs_kernel(stiffness, normals, ids, after, out):
    del after
    rows, block, depth = stiffness.shape
    column = lax.broadcasted_iota(jnp.int32, (block, depth), 1)
    own = GROUP * lax.axis_index("inst")
    coefs = jnp.zeros((block, depth), jnp.float32)
    for x in range(rows):
        inverse = 1.0 / stiffness[x, :, 0:1]
        for d in range(3):
            here = normals[d, :, x : x + 1] * inverse
            coefs = jnp.where(column == own + d * rows + x, here, coefs)
        here = ids[:, x : x + 1].astype(jnp.float32)
        coefs = jnp.where(column == own + 3 * rows + x, here, coefs)
    out[0] = coefs


def add_kernel(keep, near, *rest):
    out = rest[-1]
    for d in range(out.shape[0]):
        for x in range(out.shape[1]):
            out[d, x] = keep[d, x] + near[d, x]


def wall_near_kernel(face, face_near, coefs, coefs_near, out):
    out[0] = face[0] + face_near[0]
    out[1] = coefs[0] + coefs_near[0]


def over_near_kernel(over, over_near, after, out):
    del after
    for i in range(2 * OVER):
        out[i] = over[i] + over_near[i]


def over_low(keep, over_near, far, i):
    return keep[i] + over_near[2 * OVER + i] + far[i]


def over_high(keep, over_near, far, i):
    return keep[OVER + i] + over_near[3 * OVER + i] + far[OVER + i]


def wall_kernel(near, far, after, out):
    del after
    for i in range(2):
        value = near[i] + far[i]
        for s in range(out.shape[0]):
            out[s, i] = value


def over_kernel(keep, over_near, far, after, outside, inside):
    del after
    even = lax.axis_index("space") % 2 == 0
    for i in range(OVER):
        low, high = (f(keep, over_near, far, i) for f in (over_low, over_high))
        inside[i] = jnp.where(even, high, low)
        outside[i] = jnp.where(even, low, high)


def design_sums(scale, rows, walls, out):
    faces = [walls[s, 0] for s in range(walls.shape[0])]
    coefs = [walls[s, 1] for s in range(walls.shape[0])]
    spaces = len(faces)
    block, depth = faces[0].shape
    column = lax.broadcasted_iota(jnp.int32, (block, depth), 1) % GROUP
    at_low = functools.reduce(
        jnp.logical_or,
        [(column >= at) & (column < at + n) for at, n in zip(FACE_AT, REACHES)],
    )
    at_high = functools.reduce(
        jnp.logical_or,
        [
            (column >= at + rows - n) & (column < at + rows)
            for at, n in zip(FACE_AT, REACHES)
        ],
    )
    mine = (lax.axis_index("inst") * spaces + lax.axis_index("space")) * DV_DEV
    sums = [jnp.zeros((block, depth), jnp.float32) for _ in range(DV_DEV)]
    for s in range(spaces):
        whole = faces[s]
        if s > 0:
            whole = whole + jnp.where(at_low, pltpu.roll(faces[s - 1], depth - rows, 1), 0.0)
        if s < spaces - 1:
            whole = whole + jnp.where(at_high, pltpu.roll(faces[s + 1], rows, 1), 0.0)
        surface = jnp.zeros((block, depth), jnp.float32)
        for d in range(3):
            turned = pltpu.roll(coefs[s], depth - d * rows, 1) if d else coefs[s]
            surface = surface + pltpu.roll(whole, depth - FACE_AT[d], 1) * turned
        ids = pltpu.roll(coefs[s], depth - 3 * rows, 1).astype(jnp.int32) - mine
        ids = jnp.where(column < rows, ids, -1)
        for j in range(DV_DEV):
            sums[j] = sums[j] + jnp.where(ids == j, surface, 0.0)
    for j in range(DV_DEV):
        out[j] = jnp.sum(sums[j]) * scale


def last_kernel(
    scale, spaces, keep, near, far, stiffness, across, inside, walls_ref,
    out, design, walls, sem,
):
    rows = keep.shape[1]
    copy = pltpu.make_async_copy(walls_ref, walls, sem)
    copy.start()
    space = lax.axis_index("space")
    even = space % 2 == 0
    inner = (space > 0) & (space < spaces - 1)
    for x in range(rows):
        inverse = scale / stiffness[x]
        for d in range(3):
            value = keep[d, x] + near[d, x] + far[d, x]
            for at, side in (
                (LOW_AT[d] + x, even if x < REACHES[d] else None),
                (LOW_AT[d] + x - rows + REACHES[d], ~even if x >= rows - REACHES[d] else None),
            ):
                if side is not None:
                    outer = jnp.where(inner, across[at], 0.0)
                    value = value + jnp.where(side, outer, inside[at])
            out[d, x] = value * inverse
    copy.wait()
    design_sums(scale, rows, walls, design)


def per_device(adjoint, flux_terms, stiffness, normals, design_map):
    insts, spaces = lax.axis_size("inst"), lax.axis_size("space")
    rows, block, depth = stiffness.shape
    scale = 1.0 / (DIAG**3 * adjoint.shape[0] * insts)

    vmem = pl.BlockSpec(memory_space=pltpu.VMEM)

    def on_chip(kernel, shapes, *operands, after=()):
        out = [jax.ShapeDtypeStruct(shape, jnp.float32) for shape in shapes]
        return pl.pallas_call(
            kernel,
            out_shape=out,
            in_specs=[vmem] * len(operands) + [pl.BlockSpec(memory_space=pl.ANY)] * len(after),
            out_specs=[vmem] * len(out),
            compiler_params=pltpu.CompilerParams(vmem_limit_bytes=4 * 2**20),
            cost_estimate=pl.CostEstimate(
                flops=500_000, bytes_accessed=1_500_000, transcendentals=0
            ),
        )(*operands, *after)

    main_ko, main_kx, main_so, main_sx, over_ko, over_kx, over_s, face = front(
        adjoint, flux_terms
    )

    other_core = [(i, i ^ 1) for i in range(insts)]
    other_chip = [(i, i ^ 2) for i in range(insts)]

    plane = (1, block, depth)
    face_r = lax.ppermute(face, "inst", other_core)
    [coefs] = on_chip(
        coefs_kernel, [plane], stiffness, normals.transpose(0, 2, 1), design_map.T,
        after=[face],
    )
    coefs_r = lax.ppermute(coefs, "inst", other_core)
    over_r = lax.ppermute(over_s, "inst", other_core)
    main_r = lax.ppermute(main_sx, "inst", other_core)
    main_near = lax.ppermute(main_so, "inst", other_core)
    halo, plane = (OVER, block, depth), (2, block, depth)
    [wall_near] = on_chip(wall_near_kernel, [plane], face, face_r, coefs, coefs_r)
    wall_far = lax.ppermute(wall_near, "inst", other_chip)
    [over_x] = on_chip(
        over_near_kernel, [over_kx.shape], over_kx, over_r, after=[wall_near]
    )
    over_far = lax.ppermute(over_x, "inst", other_chip)
    [wall] = on_chip(
        wall_kernel, [(spaces,) + plane], wall_near, wall_far, after=[over_x]
    )
    wall = pltpu.with_memory_space_constraint(wall, pltpu.VMEM)
    walls = lax.all_to_all(wall, "space", 0, 0, tiled=True)
    [main_x] = on_chip(add_kernel, [main_kx.shape], main_kx, main_r, after=[wall, over_far])
    main_far = lax.ppermute(main_x, "inst", other_chip)

    across, inside = on_chip(
        over_kernel, [halo, halo], over_ko, over_r, over_far, after=[main_x]
    )
    across = lax.ppermute(
        across, "space", [(i, (((i + 1) ^ 1) - 1) % spaces) for i in range(spaces)]
    )
    inside = lax.ppermute(inside, "space", [(i, i ^ 1) for i in range(spaces)])
    mesh_adjoint, design_grad = pl.pallas_call(
        functools.partial(last_kernel, scale, spaces),
        out_shape=[
            jax.ShapeDtypeStruct((3, rows, block, depth), jnp.float32),
            jax.ShapeDtypeStruct((DV_DEV,), jnp.float32),
        ],
        in_specs=[vmem] * 6 + [pl.BlockSpec(memory_space=pl.ANY)],
        out_specs=[vmem, pl.BlockSpec(memory_space=pltpu.SMEM)],
        scratch_shapes=[
            pltpu.VMEM(walls.shape, jnp.float32),
            pltpu.SemaphoreType.DMA(()),
        ],
        compiler_params=pltpu.CompilerParams(vmem_limit_bytes=6 * 2**20),
    )(main_ko, main_near, main_far, stiffness, across, inside, walls)
    return (mesh_adjoint, design_grad)


def solution(mesh):
    in_specs = (
        P("inst", None, "space", None, None),
        P("inst", None, None, "space", None, None),
        P("space", "inst", None),
        P(None, "space", "inst"),
        P("space", "inst"),
    )
    out_specs = (P(None, "space", "inst", None), P(("inst", "space")))
    return jax.shard_map(
        per_device, mesh=mesh, in_specs=in_specs, out_specs=out_specs, check_vma=False
    )
```

```python
import functools
import jax
import jax.numpy as jnp
from jax import lax
from jax.experimental import pallas as pl
from jax.experimental.pallas import tpu as pltpu
from jax.sharding import PartitionSpec as P

DIAG = 6.5
DV_DEV = 8
REACH = 3
PAD = REACH + 1
CHUNK = 2
REACHES = (3, 2, 2)
LOW_AT = (0, 3, 5)
OVER = 7
GROUP = 64
FACE_AT = (REACH, 24, 44)


def shifted_rows(tiles, top, bottom):
    down = [pltpu.roll(t, 1, 0) for t in tiles]
    up = [pltpu.roll(t, 7, 0) for t in tiles]
    zero = jnp.zeros_like(tiles[0])
    down = [jnp.where(top, p, n) for p, n in zip([zero] + down[:-1], down)]
    up = [jnp.where(bottom, n, p) for p, n in zip(up, up[1:] + [zero])]
    return down, up


def front_kernel(
    adj_hbm, flux_hbm,
    main_ko, main_kx, main_so, main_sx, over_ko, over_kx, over_s, wall,
    adj, flux, work, metric, plane, side, band, pairs, stack, along, beside, adj_sems, flux_sems,
):
    kinds, variables, rows, width, depth = adj.shape
    chunks = rows // CHUNK
    tiles = width // 8
    inst, space = lax.axis_index("inst"), lax.axis_index("space")
    low_open = jnp.where(space > 0, 1.0, 0.0)
    high_open = jnp.where(space < lax.axis_size("space") - 1, 1.0, 0.0)

    def adj_copy(i):
        part = pl.ds(i * CHUNK, CHUNK)
        return pltpu.make_async_copy(
            adj_hbm.at[:, :, part], adj.at[:, :, part], adj_sems.at[i]
        )

    def flux_copy(i):
        part = pl.ds(i * CHUNK, CHUNK)
        return pltpu.make_async_copy(
            flux_hbm.at[:, :, :, part], flux.at[:, :, :, part], flux_sems.at[i]
        )

    for i in range(chunks):
        adj_copy(i).start()
        flux_copy(i).start()

    near = jnp.abs(
        lax.broadcasted_iota(jnp.int32, (depth, depth), 0)
        - lax.broadcasted_iota(jnp.int32, (depth, depth), 1)
    )
    lane = lax.broadcasted_iota(jnp.int32, (depth, depth), 1)
    ends = jnp.where((lane == 0) | (lane == depth - 1), 1.0, 2.0)
    once = jnp.where(near == 1, 1.0, 0.0).astype(jnp.bfloat16)
    twice = jnp.where(near == 0, ends, jnp.where(near == 2, 1.0, 0.0)).astype(jnp.bfloat16)
    for half in (slice(0, depth), slice(depth, 2 * depth)):
        band[half, :depth] = once
        band[half, depth:] = twice
    most = pairs.shape[0]
    one = lax.broadcasted_iota(jnp.int32, (most, most), 0)
    two = lax.broadcasted_iota(jnp.int32, (most, most), 1)
    adjacent = (jnp.abs(one - two) == 1) & (one // width == two // width)
    pairs[...] = jnp.where(adjacent, 1.0, 0.0).astype(jnp.bfloat16)
    stack[...] = jnp.zeros(stack.shape, jnp.bfloat16)
    zero = jnp.zeros((width, depth), jnp.float32)
    for d in range(3):
        for x in (-2, -1, rows, rows + 1):
            metric[d, x + PAD] = zero
            side[d, x + PAD] = zero
            plane[d, x + PAD] = zero
    for x in (-2, -1, rows, rows + 1):
        work[0, x + PAD] = zero

    row = lax.broadcasted_iota(jnp.int32, (8, depth), 0)
    top, bottom = row == 0, row == 7
    column = lax.broadcasted_iota(jnp.int32, (8, depth), 1)
    first, last = column == 0, column == depth - 1

    def weigh(x):
        for h in range(width // 16):
            part = slice(16 * h, 16 * h + 16)
            sums = [jnp.zeros((16, depth), jnp.float32) for _ in range(3)]
            for k in range(kinds):
                for v in range(variables):
                    a = adj[k, v, x, part].astype(jnp.float32)
                    for d in range(3):
                        sums[d] = sums[d] + a * flux[k, v, d, x, part].astype(jnp.float32)
            for d in range(3):
                work[d, x + PAD, part] = sums[d]

    def tile(t):
        return slice(8 * t, 8 * t + 8)

    def planes(slabs):
        count = len(slabs) * width
        for s, (d, x) in enumerate(slabs):
            r = x + PAD
            here = [work[d, r, tile(t)] for t in range(tiles)]
            if d == 0:
                open_ = jnp.where(x < 0, low_open, jnp.where(x >= rows, high_open, 1.0))
                low = [work[0, r - 1, tile(t)] for t in range(tiles)]
                high = [work[0, r + 1, tile(t)] for t in range(tiles)]
                m = [(h + 0.5 * (p - n)) * open_ for h, p, n in zip(here, low, high)]
            elif d == 1:
                low, high = shifted_rows(here, top, bottom)
                m = [h + 0.5 * (p - n) for h, p, n in zip(here, low, high)]
            else:
                m = [
                    h + 0.5 * (
                        jnp.where(first, 0.0, pltpu.roll(h, 1, 1))
                        - jnp.where(last, 0.0, pltpu.roll(h, depth - 1, 1))
                    )
                    for h in here
                ]
            for t in range(tiles):
                metric[d, r, tile(t)] = m[t]
            for t in range(0, tiles, 2):
                both = jnp.concatenate(m[t : t + 2], axis=0)
                rounded = both.astype(jnp.bfloat16)
                part = slice(s * width + 8 * t, s * width + 8 * t + 16)
                stack[part, :depth] = rounded
                stack[part, depth:] = (both - rounded.astype(jnp.float32)).astype(jnp.bfloat16)
        along[:count] = jnp.dot(stack[:count], band[...], preferred_element_type=jnp.float32)
        beside[...] = jnp.dot(pairs[...], stack[...], preferred_element_type=jnp.float32)
        for s, (d, x) in enumerate(slabs):
            r = x + PAD
            at = s * width
            m = [metric[d, r, tile(t)] for t in range(tiles)]
            along_1 = [along[at + 8 * t : at + 8 * t + 8, :depth] for t in range(tiles)]
            along_2 = [along[at + 8 * t : at + 8 * t + 8, depth:] for t in range(tiles)]
            parts = [beside[at + 8 * t : at + 8 * t + 8] for t in range(tiles)]
            once = [(p[:, :depth] + p[:, depth:]) + q for p, q in zip(parts, along_1)]
            low, high = shifted_rows([o + q for o, q in zip(once, along_1)], top, bottom)
            returns = 2.0 - jnp.where(
                x == 0, 1.0 - low_open, jnp.where(x == rows - 1, 1.0 - high_open, 0.0)
            )
            weight = DIAG * DIAG + returns
            for t in range(tiles):
                side[d, r, tile(t)] = DIAG * m[t] + (once[t] + once[t])
                twice = (low[t] + high[t]) + along_2[t]
                plane[d, r, tile(t)] = weight * m[t] + DIAG * once[t] + twice

    def settle(i, extra):
        planes(
            [(1, i * CHUNK + j) for j in range(CHUNK)]
            + [(2, i * CHUNK + j) for j in range(CHUNK)]
            + [(0, i * CHUNK + j - 1) for j in range(CHUNK + extra)]
        )

    def arrive(i):
        adj_copy(i).wait()
        flux_copy(i).wait()

    arrive(0)
    for j in range(CHUNK):
        weigh(j)

    def stage(i, _):
        arrive(i)
        settle(i - 1, 0)
        for j in range(CHUNK):
            weigh(i * CHUNK + j)
        return 0

    lax.fori_loop(1, chunks, stage, 0)
    settle(chunks - 1, 2)

    def put(refs, index, place, total, face):
        for j, ref, shift in zip((0, 2, 1, 3), refs, (0, 0, 2 * OVER, 0)):
            b = inst ^ j
            at = pl.multiple_of(8 * b, 8)
            value = total(pl.ds(at, 8))
            if ref is over_s:
                ref[index + shift] = value
            else:
                ref[index] = value
            face = jnp.where(column == GROUP * b + place, value[:, 0:1], face)
        return face

    main_refs = (main_ko, main_kx, main_so, main_sx)
    over_refs = (over_ko, over_kx, over_s, over_s)

    def reached(d, x, part):
        r = x + PAD
        first, last = (PAD - 1, PAD + rows) if d == 0 else (PAD, PAD + rows - 1)
        terms = (
            [plane[d, r, part]] * (first <= r <= last)
            + [side[d, s, part] for s in (r - 1, r + 1) if first <= s <= last]
            + [metric[d, s, part] for s in (r - 2, r + 2) if first <= s <= last]
        )
        return functools.reduce(jnp.add, terms)

    face = jnp.zeros((8, depth), jnp.float32)
    for d in range(3):
        for x in range(-REACHES[d], 0):
            face = put(
                over_refs, LOW_AT[d] + x + REACHES[d], FACE_AT[d] + x,
                functools.partial(reached, d, x), face,
            )
        for x in range(rows, rows + REACHES[d]):
            face = put(
                over_refs, OVER + LOW_AT[d] + x - rows, FACE_AT[d] + x,
                functools.partial(reached, d, x), face,
            )

    def inner(x, face):
        r = x + PAD
        for d in range(3):

            def total(part):
                value = plane[d, r, part] + (side[d, r - 1, part] + side[d, r + 1, part])
                return value + (metric[d, r - 2, part] + metric[d, r + 2, part])

            face = put(main_refs, (d, x), FACE_AT[d] + x, total, face)
        return face

    face = lax.fori_loop(0, rows, inner, face, unroll=2)
    wall[0] = face


def front(adjoint, flux_terms):
    kinds, variables, rows, width, depth = adjoint.shape
    f32 = jnp.float32
    block = width // 4
    main = jax.ShapeDtypeStruct((3, rows, block, depth), f32)
    vmem = pl.BlockSpec(memory_space=pltpu.VMEM)
    hbm = pl.BlockSpec(memory_space=pltpu.HBM)
    padded = (3, rows + 2 * PAD, width, depth)
    most = (3 * CHUNK + 2) * width
    over_rows = (2 * OVER, 2 * OVER, 4 * OVER, 1)
    return pl.pallas_call(
        front_kernel,
        out_shape=[main] * 4
        + [jax.ShapeDtypeStruct((count, block, depth), f32) for count in over_rows],
        in_specs=[hbm] * 2,
        out_specs=[vmem] * 8,
        scratch_shapes=[
            pltpu.VMEM(adjoint.shape, adjoint.dtype),
            pltpu.VMEM(flux_terms.shape, flux_terms.dtype),
            pltpu.VMEM(padded, f32),
            pltpu.VMEM(padded, f32),
            pltpu.VMEM(padded, f32),
            pltpu.VMEM(padded, f32),
            pltpu.VMEM((2 * depth, 2 * depth), jnp.bfloat16),
            pltpu.VMEM((most, most), jnp.bfloat16),
            pltpu.VMEM((most, 2 * depth), jnp.bfloat16),
            pltpu.VMEM((most, 2 * depth), f32),
            pltpu.VMEM((most, 2 * depth), f32),
            pltpu.SemaphoreType.DMA((rows // CHUNK,)),
            pltpu.SemaphoreType.DMA((rows // CHUNK,)),
        ],
        compiler_params=pltpu.CompilerParams(vmem_limit_bytes=51 * 2**20),
        cost_estimate=pl.CostEstimate(
            flops=60_000_000, bytes_accessed=13_000_000, transcendentals=0
        ),
    )(adjoint, flux_terms)


def coefs_kernel(stiffness, normals, ids, after, out):
    del after
    rows, block, depth = stiffness.shape
    column = lax.broadcasted_iota(jnp.int32, (block, depth), 1)
    own = GROUP * lax.axis_index("inst")
    coefs = jnp.zeros((block, depth), jnp.float32)
    for x in range(rows):
        inverse = 1.0 / stiffness[x, :, 0:1]
        for d in range(3):
            here = normals[d, :, x : x + 1] * inverse
            coefs = jnp.where(column == own + d * rows + x, here, coefs)
        here = ids[:, x : x + 1].astype(jnp.float32)
        coefs = jnp.where(column == own + 3 * rows + x, here, coefs)
    out[0] = coefs


def add_kernel(keep, near, *rest):
    out = rest[-1]
    for d in range(out.shape[0]):
        for x in range(out.shape[1]):
            out[d, x] = keep[d, x] + near[d, x]


def wall_near_kernel(face, face_near, coefs, coefs_near, out):
    out[0] = face[0] + face_near[0]
    out[1] = coefs[0] + coefs_near[0]


def over_near_kernel(over, over_near, after, out):
    del after
    for i in range(2 * OVER):
        out[i] = over[i] + over_near[i]


def over_low(keep, over_near, far, i):
    return keep[i] + over_near[2 * OVER + i] + far[i]


def over_high(keep, over_near, far, i):
    return keep[OVER + i] + over_near[3 * OVER + i] + far[OVER + i]


def wall_kernel(near, far, after, out):
    del after
    for i in range(2):
        value = near[i] + far[i]
        for s in range(out.shape[0]):
            out[s, i] = value


def over_kernel(keep, over_near, far, after, outside, inside):
    del after
    even = lax.axis_index("space") % 2 == 0
    for i in range(OVER):
        low, high = (f(keep, over_near, far, i) for f in (over_low, over_high))
        inside[i] = jnp.where(even, high, low)
        outside[i] = jnp.where(even, low, high)


def design_sums(scale, rows, walls, out):
    faces = [walls[s, 0] for s in range(walls.shape[0])]
    coefs = [walls[s, 1] for s in range(walls.shape[0])]
    spaces = len(faces)
    block, depth = faces[0].shape
    column = lax.broadcasted_iota(jnp.int32, (block, depth), 1) % GROUP
    at_low = functools.reduce(
        jnp.logical_or,
        [(column >= at) & (column < at + n) for at, n in zip(FACE_AT, REACHES)],
    )
    at_high = functools.reduce(
        jnp.logical_or,
        [
            (column >= at + rows - n) & (column < at + rows)
            for at, n in zip(FACE_AT, REACHES)
        ],
    )
    mine = (lax.axis_index("inst") * spaces + lax.axis_index("space")) * DV_DEV
    sums = [jnp.zeros((block, depth), jnp.float32) for _ in range(DV_DEV)]
    for s in range(spaces):
        whole = faces[s]
        if s > 0:
            whole = whole + jnp.where(at_low, pltpu.roll(faces[s - 1], depth - rows, 1), 0.0)
        if s < spaces - 1:
            whole = whole + jnp.where(at_high, pltpu.roll(faces[s + 1], rows, 1), 0.0)
        surface = jnp.zeros((block, depth), jnp.float32)
        for d in range(3):
            turned = pltpu.roll(coefs[s], depth - d * rows, 1) if d else coefs[s]
            surface = surface + pltpu.roll(whole, depth - FACE_AT[d], 1) * turned
        ids = pltpu.roll(coefs[s], depth - 3 * rows, 1).astype(jnp.int32) - mine
        ids = jnp.where(column < rows, ids, -1)
        for j in range(DV_DEV):
            sums[j] = sums[j] + jnp.where(ids == j, surface, 0.0)
    for j in range(DV_DEV):
        out[j] = jnp.sum(sums[j]) * scale


def last_kernel(
    scale, spaces, keep, near, far, stiffness, across, inside, walls_ref,
    out, design, walls, sem,
):
    rows = keep.shape[1]
    copy = pltpu.make_async_copy(walls_ref, walls, sem)
    copy.start()
    space = lax.axis_index("space")
    even = space % 2 == 0
    inner = (space > 0) & (space < spaces - 1)
    for x in range(rows):
        inverse = scale / stiffness[x]
        for d in range(3):
            value = keep[d, x] + near[d, x] + far[d, x]
            for at, side in (
                (LOW_AT[d] + x, even if x < REACHES[d] else None),
                (LOW_AT[d] + x - rows + REACHES[d], ~even if x >= rows - REACHES[d] else None),
            ):
                if side is not None:
                    outer = jnp.where(inner, across[at], 0.0)
                    value = value + jnp.where(side, outer, inside[at])
            out[d, x] = value * inverse
    copy.wait()
    design_sums(scale, rows, walls, design)


def per_device(adjoint, flux_terms, stiffness, normals, design_map):
    insts, spaces = lax.axis_size("inst"), lax.axis_size("space")
    rows, block, depth = stiffness.shape
    scale = 1.0 / (DIAG**3 * adjoint.shape[0] * insts)

    vmem = pl.BlockSpec(memory_space=pltpu.VMEM)

    def on_chip(kernel, shapes, *operands, after=()):
        out = [jax.ShapeDtypeStruct(shape, jnp.float32) for shape in shapes]
        return pl.pallas_call(
            kernel,
            out_shape=out,
            in_specs=[vmem] * len(operands) + [pl.BlockSpec(memory_space=pl.ANY)] * len(after),
            out_specs=[vmem] * len(out),
            compiler_params=pltpu.CompilerParams(vmem_limit_bytes=4 * 2**20),
            cost_estimate=pl.CostEstimate(
                flops=500_000, bytes_accessed=1_500_000, transcendentals=0
            ),
        )(*operands, *after)

    main_ko, main_kx, main_so, main_sx, over_ko, over_kx, over_s, face = front(
        adjoint, flux_terms
    )

    other_core = [(i, i ^ 1) for i in range(insts)]
    other_chip = [(i, i ^ 2) for i in range(insts)]

    plane = (1, block, depth)
    face_r = lax.ppermute(face, "inst", other_core)
    [coefs] = on_chip(
        coefs_kernel, [plane], stiffness, normals.transpose(0, 2, 1), design_map.T,
        after=[face],
    )
    coefs_r = lax.ppermute(coefs, "inst", other_core)
    over_r = lax.ppermute(over_s, "inst", other_core)
    main_r = lax.ppermute(main_sx, "inst", other_core)
    main_near = lax.ppermute(main_so, "inst", other_core)
    halo, plane = (OVER, block, depth), (2, block, depth)
    [wall_near] = on_chip(wall_near_kernel, [plane], face, face_r, coefs, coefs_r)
    wall_far = lax.ppermute(wall_near, "inst", other_chip)
    [over_x] = on_chip(
        over_near_kernel, [over_kx.shape], over_kx, over_r, after=[wall_near]
    )
    over_far = lax.ppermute(over_x, "inst", other_chip)
    [wall] = on_chip(
        wall_kernel, [(spaces,) + plane], wall_near, wall_far, after=[over_x]
    )
    wall = pltpu.with_memory_space_constraint(wall, pltpu.VMEM)
    walls = lax.all_to_all(wall, "space", 0, 0, tiled=True)
    [main_x] = on_chip(add_kernel, [main_kx.shape], main_kx, main_r, after=[wall, over_far])
    main_far = lax.ppermute(main_x, "inst", other_chip)

    across, inside = on_chip(
        over_kernel, [halo, halo], over_ko, over_r, over_far, after=[main_x]
    )
    across = lax.ppermute(
        across, "space", [(i, (((i + 1) ^ 1) - 1) % spaces) for i in range(spaces)]
    )
    inside = lax.ppermute(inside, "space", [(i, i ^ 1) for i in range(spaces)])
    mesh_adjoint, design_grad = pl.pallas_call(
        functools.partial(last_kernel, scale, spaces),
        out_shape=[
            jax.ShapeDtypeStruct((3, rows, block, depth), jnp.float32),
            jax.ShapeDtypeStruct((DV_DEV,), jnp.float32),
        ],
        in_specs=[vmem] * 6 + [pl.BlockSpec(memory_space=pl.ANY)],
        out_specs=[vmem, pl.BlockSpec(memory_space=pltpu.SMEM)],
        scratch_shapes=[
            pltpu.VMEM(walls.shape, jnp.float32),
            pltpu.SemaphoreType.DMA(()),
        ],
        compiler_params=pltpu.CompilerParams(vmem_limit_bytes=6 * 2**20),
    )(main_ko, main_near, main_far, stiffness, across, inside, walls)
    return (mesh_adjoint, design_grad)


def solution(mesh):
    in_specs = (
        P("inst", None, "space", None, None),
        P("inst", None, None, "space", None, None),
        P("space", "inst", None),
        P(None, "space", "inst"),
        P("space", "inst"),
    )
    out_specs = (P(None, "space", "inst", None), P(("inst", "space")))
    return jax.shard_map(
        per_device, mesh=mesh, in_specs=in_specs, out_specs=out_specs, check_vma=False
    )
```
